32 devices in a mesh: seq: 8 (over y, x, core), head: 4 (over z).
Axes of the slice: x: 2, y: 2, z: 4, core: 2. Of those that a mesh axis runs over, the one named last changes fastest.
Arguments:
- tokens: bfloat16 [8192, 2048], P('seq'), may hold values from -20 to 20
- cotangent: bfloat16 [8192, 2048], P('seq'), may hold values from -6 to 6
- seq_lengths: int32 [2], replicated, may hold values from 128 to 8064, as said below
- attn_master: float32 [4, 2048, 2048], P(None, 'seq', 'head'), may hold values from -0.5 to 0.5
- ffn_master: float32 [3, 2048, 8192], P(None, 'seq', 'head'), may hold values from -0.088388348 to 0.088388348
- gain_master: float32 [2, 2048], P(None, 'seq'), may hold values from 0.3 to 2.5
- attn_first: float32 [4, 2048, 2048], P(None, 'seq', 'head'), may hold values from -0.0017089844 to 0.0017089844
- attn_second: float32 [4, 2048, 2048], P(None, 'seq', 'head'), may hold values from 7.450126e-09 to 5.9601007e-08
- ffn_first: float32 [3, 2048, 8192], P(None, 'seq', 'head'), may hold values from -0.0017089844 to 0.0017089844
- ffn_second: float32 [3, 2048, 8192], P(None, 'seq', 'head'), may hold values from 7.450126e-10 to 5.960101e-09
- gain_first: float32 [2, 2048], P(None, 'seq'), may hold values from -0.0048828125 to 0.0048828125
- gain_second: float32 [2, 2048], P(None, 'seq'), may hold values from 6.705113e-08 to 5.3640906e-07
Outputs:
- layer_output: float32 [8192, 2048], P('seq')
- input_grad: float32 [8192, 2048], P('seq')
- attn_mass: float32 [16, 8192], P('head', 'seq')
- grad_norm: float32 [], replicated
- attn_grad: float32 [4, 2048, 2048], P(None, 'seq', 'head')
- attn_first_new: float32 [4, 2048, 2048], P(None, 'seq', 'head')
- attn_second_new: float32 [4, 2048, 2048], P(None, 'seq', 'head')
- attn_new: float32 [4, 2048, 2048], P(None, 'seq', 'head')
- attn_low: bfloat16 [4, 2048, 2048], P(None, 'seq', 'head')
- ffn_grad: float32 [3, 2048, 8192], P(None, 'seq', 'head')
- ffn_first_new: float32 [3, 2048, 8192], P(None, 'seq', 'head')
- ffn_second_new: float32 [3, 2048, 8192], P(None, 'seq', 'head')
- ffn_new: float32 [3, 2048, 8192], P(None, 'seq', 'head')
- ffn_low: bfloat16 [3, 2048, 8192], P(None, 'seq', 'head')
- gain_grad: float32 [2, 2048], P(None, 'seq')
- gain_first_new: float32 [2, 2048], P(None, 'seq')
- gain_second_new: float32 [2, 2048], P(None, 'seq')
- gain_new: float32 [2, 2048], P(None, 'seq')
- gain_low: bfloat16 [2, 2048], P(None, 'seq')
The draws below stay inside these ranges and needn't reach their ends.
Inputs may be any that keep to these rules, and one draw needn't show every extreme that they name: `seq_lengths`: two sequences that together hold all 8192 tokens: one has 128 to 1023 tokens and the other the rest; which of the two comes first varies.
All inputs are finite; a program needn't handle non-finite values.
Results may differ from the reference program's by a relative error of at most 0.024.
Values may be sent and summed in bfloat16 or wider, within the bound.
No kernel may reach another device: no remote copies, remote signals or barrier semaphores. Data moves between devices by JAX's collectives and lax.ppermute only.
A program may use at most 320 MiB of HBM per device.

```python
import math
import jax
import jax.numpy as jnp
from jax import lax

D = 2048
HEADS = 16
HD = 128
FF = 8192
TOK_DEV = 1024
SEQ_MIN = 128
STEP = 10
TOKENS = 8192
SEQ_MAX = 8192
NBLK = 1


def draw_tokens(key, part):
    key = jax.random.fold_in(key, 17)
    entry_key, row_key, column_key = jax.random.split(key, 3)
    entries = jax.random.truncated_normal(entry_key, -4.0, 4.0, (TOKENS, D), jnp.float32)
    row_scale = jnp.exp(jax.random.uniform(row_key, (TOKENS,), jnp.float32, -1.2039728, 1.0986123))
    column_scale = jnp.exp(jax.random.uniform(column_key, (D,), jnp.float32, -0.5108256, 0.4700036))
    return (entries * row_scale[:, None] * column_scale[None, :]).astype(jnp.bfloat16)


def draw_seq_lengths(key, part):
    key = jax.random.fold_in(key, 19)
    side_key, cut_key = jax.random.split(key, 2)
    short_len = jax.random.randint(cut_key, (), SEQ_MIN, TOK_DEV)
    short_first = jax.random.randint(side_key, (), 0, 2)
    first_len = jnp.where(short_first == 1, short_len, TOKENS - short_len)
    return jnp.stack([first_len, TOKENS - first_len]).astype(jnp.int32)


def scaled_entries(key, shape, scales):
    entries = jax.random.truncated_normal(key, -4.0, 4.0, shape, jnp.float32)
    return entries * jnp.sqrt(scales)[:, None, None]


def draw_attn_master(key, part):
    key = jax.random.fold_in(key, 11)
    scales = jnp.array([2.0, 1.0, 1.0, 32.0], jnp.float32) / D
    return scaled_entries(key, (4, D, D), scales)


def draw_ffn_master(key, part):
    key = jax.random.fold_in(key, 23)
    scales = jnp.array([1.0 / D, 1.0 / D, 4.0 / FF], jnp.float32)
    return scaled_entries(key, (3, D, FF), scales)


def draw_gain_master(key, part):
    key = jax.random.fold_in(key, 13)
    ramp = jnp.arange(D, dtype=jnp.float32) / (D - 1)
    low_end = 0.6
    high_end = 1.8
    rough = jax.random.uniform(key, (2, D), jnp.float32, 0.8, 1.2)
    return (low_end + (high_end - low_end) * ramp)[None, :] * rough


def level_of(stream_key, shape, cuts, least, high):
    def one(axis_at, blocks):
        steps = jax.random.uniform(jax.random.fold_in(jax.random.fold_in(stream_key, 6), axis_at), (blocks,), jnp.float32, least / len(cuts), high / len(cuts))
        return jnp.repeat(jnp.exp(steps), shape[axis_at] // blocks).reshape((-1,) + (1,) * (len(shape) - axis_at - 1))

    gain = one(*cuts[0])
    for cut in cuts[1:]:
        gain = gain * one(*cut)
    return gain


def noise(own_key, extent, width, limit, shards=(), held_as=jnp.bfloat16):
    gain = level_of(own_key, extent, shards, -0.22, 0.18) if shards else 1.0
    values = jax.random.normal(own_key, extent, jnp.float32) * width * gain
    return jnp.minimum(jnp.maximum(values, -limit), limit).astype(held_as)


def setup_inputs(seed: int = 0) -> dict:
    arg_keys = jax.random.split(jax.random.key(seed), 13)
    return {
        "tokens": draw_tokens(jax.random.fold_in(arg_keys[12], 71), 0),
        "cotangent": noise(arg_keys[1], (TOKENS, D), 1.0, 6.0, ((0, 8),)),
        "seq_lengths": draw_seq_lengths(jax.random.fold_in(arg_keys[12], 71), 0),
        "attn_master": draw_attn_master(jax.random.fold_in(arg_keys[12], 71), 0),
        "ffn_master": draw_ffn_master(jax.random.fold_in(arg_keys[12], 71), 0),
        "gain_master": draw_gain_master(jax.random.fold_in(arg_keys[12], 71), 0),
        "attn_first": noise(arg_keys[6], (4, D, D), ((4 * D * D + 3 * D * FF + 2 * D) ** -0.5), 0.0017089844, ((1, 8), (2, 4)), jnp.float32),
        "attn_second": jnp.clip(jnp.exp(math.log(5.960100679658353e-08) - 2.0794415 * jax.random.uniform(arg_keys[7], (4, D, D), jnp.float32) ** level_of(arg_keys[7], (4, D, D), ((1, 8), (2, 4)), -0.2, 0.2)), 7.450125849572942e-09, 5.960100679658353e-08),
        "ffn_first": noise(arg_keys[8], (3, D, FF), ((4 * D * D + 3 * D * FF + 2 * D) ** -0.5), 0.0017089844, ((1, 8), (2, 4)), jnp.float32),
        "ffn_second": jnp.clip(jnp.exp(math.log(5.960100857294037e-09) - 2.0794415 * jax.random.uniform(arg_keys[9], (3, D, FF), jnp.float32) ** level_of(arg_keys[9], (3, D, FF), ((1, 8), (2, 4)), -0.2, 0.2)), 7.450126071617547e-10, 5.960100857294037e-09),
        "gain_first": noise(arg_keys[10], (2, D), (3 * (4 * D * D + 3 * D * FF + 2 * D) ** -0.5), 0.0048828125, ((1, 8),), jnp.float32),
        "gain_second": jnp.clip(jnp.exp(math.log(5.364090611692518e-07) - 2.0794415 * jax.random.uniform(arg_keys[11], (2, D), jnp.float32) ** level_of(arg_keys[11], (2, D), ((1, 8),), -0.2, 0.2)), 6.705113264615647e-08, 5.364090611692518e-07),
    }


EPS = 1e-05
CLIP = 1.0
BETA1 = 0.5
BETA2 = 0.5
RATE = 0.03
GAIN_RATE = 0.3
DECAY = 0.1
ADAM_EPS = 1e-08

@jax.custom_vjp
def low(v):
    return lax.optimization_barrier(v.astype(jnp.bfloat16)).astype(jnp.float32)

@jax.custom_vjp
def low_back(v):
    return v

def low_keep(v):
    return (low(v), None)

def low_pass(kept, grad):
    return (grad,)

def back_keep(v):
    return (v, None)

def back_low(kept, grad):
    return (low(grad),)
low.defvjp(low_keep, low_pass)
low_back.defvjp(back_keep, back_low)

def exact_dot(left, right):
    return jnp.dot(left, right, precision=lax.Precision.HIGHEST, preferred_element_type=jnp.float32)

def rms_norm(values_in, gain_row):
    factor = lax.rsqrt(lax.optimization_barrier(jnp.mean(values_in * values_in, axis=-1, keepdims=True)) + EPS)
    return values_in * factor * gain_row

def sequence_info(seq_lengths, row_count):
    lengths = seq_lengths.astype(jnp.int32)
    seq_ends = jnp.cumsum(lengths, dtype=jnp.int32)
    seq_starts = seq_ends - lengths
    places = jnp.arange(row_count, dtype=jnp.int32)[:, None]
    seq_first = lax.optimization_barrier(jnp.sum(jnp.where(seq_ends[None, :] <= places, lengths[None, :], 0), axis=1, dtype=jnp.int32))
    inside = (seq_starts[None, :] <= places) & (places < seq_ends[None, :])
    seq_len = lax.optimization_barrier(jnp.sum(jnp.where(inside, lengths[None, :], 0), axis=1, dtype=jnp.int32))
    return (seq_first, seq_len)

def sequence_heads(queries, key_rows, value_rows, seq_first, seq_bias):
    factor = 1.0 / math.sqrt(HD)

    def split_heads(matrix):
        return matrix.reshape(NBLK, SEQ_MAX, HEADS, HD).transpose(0, 2, 1, 3).reshape(NBLK * HEADS, SEQ_MAX, HD)

    def per_block(vector):
        return jnp.repeat(vector.reshape(NBLK, SEQ_MAX), HEADS, axis=0)

    def one_head(packed):
        query_block, key_block, value_block, first_block, bias_block, token_place = packed
        score = low_back(exact_dot(query_block, key_block.T) * factor)
        allowed = (token_place[None, :] >= first_block[:, None]) & (token_place[None, :] <= token_place[:, None])
        weight = jnp.where(allowed, jax.nn.sigmoid(score + bias_block[:, None]), 0.0)
        return (exact_dot(low(weight), value_block), lax.optimization_barrier(jnp.sum(weight, axis=1)))
    places = per_block(jnp.arange(TOKENS, dtype=jnp.int32))
    mixed, mass = lax.map(jax.checkpoint(one_head), (split_heads(queries), split_heads(key_rows), split_heads(value_rows), per_block(seq_first), per_block(seq_bias), places))
    mixed = mixed.reshape(NBLK, HEADS, SEQ_MAX, HD).transpose(0, 2, 1, 3).reshape(TOKENS, D)
    mass = mass.reshape(NBLK, HEADS, SEQ_MAX).transpose(1, 0, 2).reshape(HEADS, TOKENS)
    return (mixed, mass)

def block_forward(residual, attn_weight, ffn_weight, gain_weight, seq_first, seq_bias):
    attn_weight = low(attn_weight)
    ffn_weight = low(ffn_weight)
    gain_weight = low(gain_weight)
    normed_one = low(rms_norm(residual, gain_weight[0]))
    projected = [low_back(low(exact_dot(normed_one, attn_weight[member]))) for member in range(3)]
    mixed, attn_mass = sequence_heads(projected[0], projected[1], projected[2], seq_first, seq_bias)
    heads_out = low_back(low(mixed))
    attn_branch = low_back(exact_dot(heads_out, attn_weight[3].T))
    resid_one = residual + attn_branch
    normed_two = low(rms_norm(resid_one, gain_weight[1]))
    gate_value = low_back(exact_dot(normed_two, ffn_weight[0]))
    up_value = low_back(exact_dot(normed_two, ffn_weight[1]))
    hidden = low(jax.nn.silu(gate_value) * up_value)
    ffn_branch = low_back(exact_dot(hidden, ffn_weight[2].T))
    return (resid_one + ffn_branch, attn_mass)

def adam_update(gradient, first_moment, second, master, step_rate):
    first_new = BETA1 * first_moment + (1.0 - BETA1) * gradient
    second_new = BETA2 * second + (1.0 - BETA2) * gradient * gradient
    first_hat = first_new / (1.0 - BETA1 ** STEP)
    second_hat = second_new / (1.0 - BETA2 ** STEP)
    master_new = master - step_rate * (first_hat / (jnp.sqrt(second_hat) + ADAM_EPS) + DECAY * master)
    return (first_new, second_new, master_new, master_new.astype(jnp.bfloat16))

def reference(tokens, cotangent, seq_lengths, attn_master, ffn_master, gain_master, attn_first, attn_second, ffn_first, ffn_second, gain_first, gain_second):
    seq_first, seq_len = sequence_info(seq_lengths, TOKENS)
    seq_bias = -jnp.log(seq_len.astype(jnp.float32))

    def forward(residual, attn_weight, ffn_weight, gain_weight):
        return block_forward(residual, attn_weight, ffn_weight, gain_weight, seq_first, seq_bias)
    layer_output, pullback, attn_mass = jax.vjp(forward, tokens.astype(jnp.float32), attn_master, ffn_master, gain_master, has_aux=True)
    input_grad, attn_raw, ffn_raw, gain_raw = pullback(cotangent.astype(jnp.float32))
    square_sum = jnp.sum(attn_raw * attn_raw) + jnp.sum(ffn_raw * ffn_raw) + jnp.sum(gain_raw * gain_raw)
    grad_norm = jnp.sqrt(square_sum)
    clip_factor = jnp.minimum(1.0, CLIP / (grad_norm + 1e-06))
    attn_grad = attn_raw * clip_factor
    ffn_grad = ffn_raw * clip_factor
    gain_grad = gain_raw * clip_factor
    attn_state = adam_update(attn_grad, attn_first, attn_second, attn_master, RATE)
    ffn_state = adam_update(ffn_grad, ffn_first, ffn_second, ffn_master, RATE)
    gain_state = adam_update(gain_grad, gain_first, gain_second, gain_master, GAIN_RATE)
    return (layer_output, input_grad, attn_mass, grad_norm, attn_grad, attn_state[0], attn_state[1], attn_state[2], attn_state[3], ffn_grad, ffn_state[0], ffn_state[1], ffn_state[2], ffn_state[3], gain_grad, gain_state[0], gain_state[1], gain_state[2], gain_state[3])
```

```python
import functools
import math

import jax
import jax.numpy as jnp
from jax import lax
from jax.experimental import pallas as pl
from jax.experimental.pallas import tpu as pltpu
from jax.sharding import PartitionSpec as P

HD = 128
STEP = 10


EPS = 1e-05
CLIP = 1.0
BETA1 = 0.5
BETA2 = 0.5
RATE = 0.03
GAIN_RATE = 0.3
DECAY = 0.1
ADAM_EPS = 1e-08

LOW = jnp.bfloat16
WIDE = jnp.float32
QUERY_FACTOR = -math.log2(math.e) / math.sqrt(HD)
FAR = 30000.0

NN = (((1,), (0,)), ((), ()))
NT = (((1,), (1,)), ((), ()))
TN = (((0,), (0,)), ((), ()))


def dot(left, right, dims=NN):
    return lax.dot_general(left, right, dims, preferred_element_type=WIDE)


def fill_key_columns(key_buf, total_rows, cut):
    rows = 1024

    def step(at, _):
        place = at * rows + lax.broadcasted_iota(jnp.int32, (rows, HD), 0)
        lane = lax.broadcasted_iota(jnp.int32, (rows, HD), 1)
        extra = jnp.where(lane < 3, 1.0, jnp.where((lane == 3) & (place < cut), FAR, 0.0))
        key_buf[pl.ds(pl.multiple_of(at * rows, rows), rows), HD:] = extra.astype(LOW)
        return 0

    lax.fori_loop(0, total_rows // rows, step, 0)


def query_columns(block, start, cut, floats):
    place = start + lax.broadcasted_iota(jnp.int32, (block, HD), 0)
    lane = lax.broadcasted_iota(jnp.int32, (block, HD), 1)
    second = place >= cut

    def part(at):
        return jnp.where(second, floats[3 + at], floats[at])

    extra = jnp.where(
        lane == 0,
        part(0),
        jnp.where(
            lane == 1,
            part(1),
            jnp.where(lane == 2, part(2), jnp.where((lane == 3) & second, 1.0, 0.0)),
        ),
    )
    return extra.astype(LOW)


def key_copies(count, parts, block, part, key_values, key_buf, value_buf, sem):
    for other in range(parts):
        for at in range(count):
            row = pl.multiple_of((at * parts + (part ^ other)) * block, block)
            yield pltpu.make_async_copy(
                key_values[other].at[at, :, 0:HD], key_buf.at[pl.ds(row, block), 0:HD], sem.at[0]
            )
            yield pltpu.make_async_copy(
                key_values[other].at[at, :, HD:], value_buf.at[pl.ds(row, block), 0:HD], sem.at[0]
            )


def forward_kernel(count, parts, block, tile, ints, floats, q_ref, *rest):
    key_values = rest[:parts]
    out_ref, mass_ref, key_buf, value_buf, query_buf, total, sem = rest[parts:]
    total_rows = count * parts * block
    step = pl.program_id(0)
    cut, part = ints[0], ints[1]

    @pl.when(step == 0)
    def _():
        for copy in key_copies(count, parts, block, part, key_values, key_buf, value_buf, sem):
            copy.start()
        fill_key_columns(key_buf, total_rows, cut)
        value_buf[:, HD:] = jnp.ones((total_rows, HD), LOW)
        for copy in key_copies(count, parts, block, part, key_values, key_buf, value_buf, sem):
            copy.wait()

    start = (step * parts + part) * block
    query_buf[:, :HD] = q_ref[...]
    query_buf[:, HD:] = query_columns(block, start, cut, floats)
    total[...] = jnp.zeros_like(total)
    first = jnp.where(start >= cut, cut // tile, 0)
    last = (start + block - 1) // tile

    def walk(at, masked):
        keys = pl.ds(pl.multiple_of(at * tile, tile), tile)
        exponent = dot(query_buf[...], key_buf[keys, :], NT)
        weight = pl.reciprocal(1.0 + jnp.exp2(exponent), approx=True)
        if masked:
            query_place = start + lax.broadcasted_iota(jnp.int32, (block, tile), 0)
            key_place = at * tile + lax.broadcasted_iota(jnp.int32, (block, tile), 1)
            weight = jnp.where(key_place <= query_place, weight, 0.0)
        total[...] += dot(weight.astype(LOW), value_buf[keys, :])

    def body(at, carry):
        walk(at, False)
        return carry

    lax.fori_loop(first, last, body, 0)
    walk(last, True)
    out_ref[...] = total[:, :HD].astype(LOW)
    mass_ref[...] = jnp.transpose(total[:, HD:])[0:1, :]


def attention_forward(ints, floats, queries, key_values):
    count, block, _ = queries.shape
    parts = len(key_values)
    total_rows = count * parts * block
    tile = 1024
    pairs = total_rows * total_rows // (2 * parts)
    return pl.pallas_call(
        functools.partial(forward_kernel, count, parts, block, tile),
        out_shape=[
            jax.ShapeDtypeStruct((count, block, HD), LOW),
            jax.ShapeDtypeStruct((count, 1, block), WIDE),
        ],
        grid_spec=pltpu.PrefetchScalarGridSpec(
            num_scalar_prefetch=2,
            grid=(count,),
            in_specs=[pl.BlockSpec((None, block, HD), lambda i, *_: (i, 0, 0))]
            + [pl.BlockSpec(memory_space=pl.ANY)] * parts,
            out_specs=[
                pl.BlockSpec((None, block, HD), lambda i, *_: (i, 0, 0)),
                pl.BlockSpec((None, 1, block), lambda i, *_: (i, 0, 0)),
            ],
            scratch_shapes=[
                pltpu.VMEM((total_rows, 2 * HD), LOW),
                pltpu.VMEM((total_rows, 2 * HD), LOW),
                pltpu.VMEM((block, 2 * HD), LOW),
                pltpu.VMEM((block, 2 * HD), WIDE),
                pltpu.SemaphoreType.DMA((1,)),
            ],
        ),
        compiler_params=pltpu.CompilerParams(vmem_limit_bytes=48 * 2**20),
        cost_estimate=pl.CostEstimate(
            flops=pairs * 8 * HD, bytes_accessed=total_rows * HD * 8, transcendentals=2 * pairs
        ),
        name="attention_forward",
    )(ints, floats, queries, *key_values)


def backward_kernel(count, parts, block, tile, ints, floats, q_ref, grad_ref, *rest):
    key_values = rest[:parts]
    (q_grad_ref, kv_grad_ref, key_buf, value_buf, turned, query_buf, q_total, k_total, v_total, sem) = (
        rest[parts:]
    )
    total_rows = count * parts * block
    step = pl.program_id(0)
    cut, part = ints[0], ints[1]

    @pl.when(step == 0)
    def _():
        for copy in key_copies(count, parts, block, part, key_values, key_buf, value_buf, sem):
            copy.start()
        fill_key_columns(key_buf, total_rows, cut)
        k_total[...] = jnp.zeros_like(k_total)
        v_total[...] = jnp.zeros_like(v_total)
        for copy in key_copies(count, parts, block, part, key_values, key_buf, value_buf, sem):
            copy.wait()

        def turn(at, carry):
            keys = pl.ds(pl.multiple_of(at * tile, tile), tile)
            turned[:, keys] = jnp.transpose(key_buf[keys, :HD])
            return carry

        lax.fori_loop(0, total_rows // tile, turn, 0)

    start = (step * parts + part) * block
    query_buf[:, :HD] = q_ref[...]
    query_buf[:, HD:] = query_columns(block, start, cut, floats)
    q_total[...] = jnp.zeros_like(q_total)
    first = jnp.where(start >= cut, cut // tile, 0)
    last = (start + block - 1) // tile

    def walk(at, masked):
        keys = pl.ds(pl.multiple_of(at * tile, tile), tile)
        exponent = dot(key_buf[keys, :], query_buf[...], NT)
        weight = pl.reciprocal(1.0 + jnp.exp2(exponent), approx=True)
        if masked:
            key_place = at * tile + lax.broadcasted_iota(jnp.int32, (tile, block), 0)
            query_place = start + lax.broadcasted_iota(jnp.int32, (tile, block), 1)
            weight = jnp.where(key_place <= query_place, weight, 0.0)
        weight_grad = dot(value_buf[keys, :], grad_ref[...], NT)
        score_grad = (weight_grad * (weight * (1.0 - weight))).astype(LOW)
        v_total[keys, :] += dot(weight.astype(LOW), grad_ref[...])
        k_total[keys, :] += dot(score_grad, query_buf[:, :HD])
        q_total[...] += dot(turned[:, keys], score_grad)

    def body(at, carry):
        walk(at, False)
        return carry

    lax.fori_loop(first, last, body, 0)
    walk(last, True)
    q_grad_ref[...] = (jnp.transpose(q_total[...]) * (1.0 / math.sqrt(HD))).astype(LOW)

    @pl.when(step == count - 1)
    def _():
        for owner in range(parts):
            for at in range(count):
                rows = pl.ds((at * parts + owner) * block, block)
                kv_grad_ref[owner, at, :, :HD] = (k_total[rows, :] * (-math.log(2.0))).astype(LOW)
                kv_grad_ref[owner, at, :, HD:] = v_total[rows, :].astype(LOW)


def attention_backward(ints, floats, queries, grads, key_values):
    count, block, _ = queries.shape
    parts = len(key_values)
    total_rows = count * parts * block
    tile = 1024
    pairs = total_rows * total_rows // (2 * parts)
    return pl.pallas_call(
        functools.partial(backward_kernel, count, parts, block, tile),
        out_shape=[
            jax.ShapeDtypeStruct((count, block, HD), LOW),
            jax.ShapeDtypeStruct((parts, count, block, 2 * HD), LOW),
        ],
        grid_spec=pltpu.PrefetchScalarGridSpec(
            num_scalar_prefetch=2,
            grid=(count,),
            in_specs=[pl.BlockSpec((None, block, HD), lambda i, *_: (i, 0, 0))] * 2
            + [pl.BlockSpec(memory_space=pl.ANY)] * parts,
            out_specs=[
                pl.BlockSpec((None, block, HD), lambda i, *_: (i, 0, 0)),
                pl.BlockSpec((parts, count, block, 2 * HD), lambda i, *_: (0, 0, 0, 0)),
            ],
            scratch_shapes=[
                pltpu.VMEM((total_rows, 2 * HD), LOW),
                pltpu.VMEM((total_rows, HD), LOW),
                pltpu.VMEM((HD, total_rows), LOW),
                pltpu.VMEM((block, 2 * HD), LOW),
                pltpu.VMEM((HD, block), WIDE),
                pltpu.VMEM((total_rows, HD), WIDE),
                pltpu.VMEM((total_rows, HD), WIDE),
                pltpu.SemaphoreType.DMA((1,)),
            ],
        ),
        compiler_params=pltpu.CompilerParams(vmem_limit_bytes=60 * 2**20),
        cost_estimate=pl.CostEstimate(
            flops=pairs * 20 * HD, bytes_accessed=total_rows * HD * 16, transcendentals=2 * pairs
        ),
        name="attention_backward",
    )(ints, floats, queries, grads, *key_values)


def attention_scalars(seq_lengths, total_rows, part):
    cut = seq_lengths[0]
    length = jnp.log2(jnp.stack([cut, total_rows - cut]).astype(WIDE))
    high = lax.reduce_precision(length, 8, 7)
    middle = lax.reduce_precision(length - high, 8, 7)
    low = length - high - middle
    return (
        jnp.stack([cut, part]).astype(jnp.int32),
        jnp.stack([high, middle, low], axis=1).reshape(6),
    )


def line_sum(pieces):
    at = lax.axis_index("head")
    count = lax.axis_size("head")
    if count != 4:
        return lax.psum_scatter(
            jnp.stack(pieces), "head", scatter_dimension=0, tiled=False
        ).astype(WIDE)
    low_side = at < 2

    def from_end(step):
        return jnp.where(low_side, pieces[step], pieces[3 - step])

    inward = [(0, 1), (3, 2)]
    far = lax.ppermute(from_end(3), "head", inward)
    middle = lax.ppermute(from_end(2), "head", inward)
    near = lax.ppermute(from_end(1), "head", inward)
    outer = lax.ppermute(from_end(0), "head", [(1, 0), (2, 3)])
    far_sum = (far.astype(WIDE) + from_end(3).astype(WIDE)).astype(LOW)
    middle_sum = (middle.astype(WIDE) + from_end(2).astype(WIDE)).astype(LOW)
    far_in = lax.ppermute(far_sum, "head", [(1, 3), (2, 0)])
    middle_in = lax.ppermute(middle_sum, "head", [(1, 2), (2, 1)])
    at_end = (at == 0) | (at == 3)
    return jnp.where(
        at_end,
        from_end(0).astype(WIDE) + outer.astype(WIDE) + far_in.astype(WIDE),
        from_end(1).astype(WIDE) + near.astype(WIDE) + middle_in.astype(WIDE),
    )


def line_gather(piece):
    count = lax.axis_size("head")
    if count != 4:
        return lax.all_gather(piece, "head", axis=0, tiled=True)
    at = lax.axis_index("head")
    rows = piece.shape[0]
    left_one = lax.ppermute(piece, "head", [(0, 1), (1, 2), (2, 3)])
    right_one = lax.ppermute(piece, "head", [(3, 2), (2, 1), (1, 0)])
    left_two = lax.ppermute(piece, "head", [(0, 2), (1, 3)])
    right_two = lax.ppermute(piece, "head", [(3, 1), (2, 0)])
    left_three = lax.ppermute(left_two, "head", [(2, 3)])
    right_three = lax.ppermute(right_two, "head", [(1, 0)])
    full = jnp.zeros((count * rows,) + piece.shape[1:], piece.dtype)
    for step, part in (
        (-3, left_three),
        (-2, left_two),
        (-1, left_one),
        (3, right_three),
        (2, right_two),
        (1, right_one),
        (0, piece),
    ):
        full = lax.dynamic_update_slice_in_dim(
            full, part, jnp.clip(at + step, 0, count - 1) * rows, 0
        )
    return full


def group_exchange(blocks, parts):
    count = lax.axis_size("seq")
    return [blocks[0]] + [
        lax.ppermute(blocks[k], "seq", [(j, j ^ k) for j in range(count)]) for k in range(1, parts)
    ]


def adam_update(gradient, first_moment, second, master, step_rate):
    first_new = BETA1 * first_moment + (1.0 - BETA1) * gradient
    second_new = BETA2 * second + (1.0 - BETA2) * gradient * gradient
    first_hat = first_new / (1.0 - BETA1**STEP)
    second_hat = second_new / (1.0 - BETA2**STEP)
    master_new = master - step_rate * (
        first_hat / (jnp.sqrt(second_hat) + ADAM_EPS) + DECAY * master
    )
    return (first_new, second_new, master_new, master_new.astype(LOW))


def per_device(
    tokens,
    cotangent,
    seq_lengths,
    attn_master,
    ffn_master,
    gain_master,
    attn_first,
    attn_second,
    ffn_first,
    ffn_second,
    gain_first,
    gain_second,
):
    seq_count = lax.axis_size("seq")
    head_count = lax.axis_size("head")
    seq_index = lax.axis_index("seq")
    head_index = lax.axis_index("head")
    local_rows, width = tokens.shape
    total_rows = local_rows * seq_count
    head_width = attn_master.shape[2]
    hidden_width = ffn_master.shape[2]
    shard_rows = attn_master.shape[1]
    local_heads = head_width // HD
    parts = seq_count // local_heads
    block = local_rows // parts
    part = seq_index % parts
    slice_rows = local_rows // head_count
    slice_start = head_index * slice_rows

    def own_slice(array):
        return lax.dynamic_slice_in_dim(array, slice_start, slice_rows, 0)

    qkv_shard = (
        attn_master[:3]
        .astype(LOW)
        .reshape(3, shard_rows, local_heads, HD)
        .transpose(1, 2, 0, 3)
        .reshape(shard_rows, 3 * head_width)
    )
    rest_shard = jnp.concatenate(
        [ffn_master[0], ffn_master[1], ffn_master[2], attn_master[3]], axis=1
    ).astype(LOW)
    gain_values = lax.all_gather(gain_master.astype(LOW), "seq", axis=1, tiled=True).astype(WIDE)
    qkv_weight = lax.all_gather(qkv_shard, "seq", axis=0, tiled=True)
    rest_weight = lax.all_gather(rest_shard, "seq", axis=0, tiled=True)
    gate_weight = rest_weight[:, :hidden_width]
    up_weight = rest_weight[:, hidden_width : 2 * hidden_width]
    down_weight = rest_weight[:, 2 * hidden_width : 3 * hidden_width]
    out_weight = rest_weight[:, 3 * hidden_width :]

    ints, floats = attention_scalars(seq_lengths, total_rows, part)

    residual = tokens.astype(WIDE)
    scale_one = lax.rsqrt(jnp.mean(residual * residual, axis=-1, keepdims=True) + EPS)
    normed_one = (residual * scale_one * gain_values[0]).astype(LOW)
    column = jnp.arange(3 * head_width, dtype=jnp.int32) % (3 * HD)
    column_factor = jnp.where(column < HD, QUERY_FACTOR, 1.0).astype(WIDE)
    projected = (dot(normed_one, qkv_weight) * column_factor).astype(LOW)

    def to_heads(array):
        columns = array.shape[1] // local_heads
        sent = (
            array.reshape(parts, block, local_heads, columns)
            .transpose(2, 0, 1, 3)
            .reshape(seq_count, block, columns)
        )
        return lax.all_to_all(sent, "seq", split_axis=0, concat_axis=0, tiled=True)

    def from_heads(array):
        columns = array.shape[2]
        got = lax.all_to_all(array, "seq", split_axis=0, concat_axis=0, tiled=True)
        return (
            got.reshape(local_heads, parts, block, columns)
            .transpose(1, 2, 0, 3)
            .reshape(local_rows, local_heads * columns)
        )

    qkv = to_heads(projected)
    head_queries = qkv[:, :, :HD]
    own_key_values = qkv[:, :, HD:]
    key_values = group_exchange([own_key_values] * parts, parts)
    mixed, mass = attention_forward(ints, floats, head_queries, key_values)
    heads_out = from_heads(mixed)
    mass_got = lax.all_to_all(mass, "seq", split_axis=0, concat_axis=0, tiled=True)
    attn_mass = mass_got.reshape(local_heads, local_rows)

    attn_part = dot(heads_out, out_weight, NT).astype(LOW)
    attn_sum = line_sum(jnp.split(attn_part, head_count, axis=0))
    resid_one = own_slice(tokens).astype(WIDE) + attn_sum
    scale_two = lax.rsqrt(jnp.mean(resid_one * resid_one, axis=-1, keepdims=True) + EPS)
    unit_two = resid_one * scale_two
    normed_two = line_gather((unit_two * gain_values[1]).astype(LOW))

    gate_value = dot(normed_two, gate_weight)
    up_value = dot(normed_two, up_weight)
    hidden_grad = dot(cotangent, down_weight)
    gate_sigmoid = jax.nn.sigmoid(gate_value)
    gate_silu = gate_value * gate_sigmoid
    hidden = (gate_silu * up_value).astype(LOW)
    gate_grad = (
        hidden_grad * up_value * (gate_sigmoid + gate_silu * (1.0 - gate_sigmoid))
    ).astype(LOW)
    up_grad = (hidden_grad * gate_silu).astype(LOW)
    two_grad_part = (dot(gate_grad, gate_weight, NT) + dot(up_grad, up_weight, NT)).astype(LOW)
    normed_two_grad = line_sum(jnp.split(two_grad_part, head_count, axis=0))

    ffn_part = dot(hidden, down_weight, NT).astype(LOW)
    ffn_sum = line_sum(jnp.split(ffn_part, head_count, axis=0))
    layer_output = line_gather((resid_one + ffn_sum).astype(LOW)).astype(WIDE)
    ffn_raw = jnp.concatenate(
        [
            dot(normed_two, gate_grad, TN).astype(LOW),
            dot(normed_two, up_grad, TN).astype(LOW),
            dot(cotangent, hidden, TN).astype(LOW),
        ],
        axis=1,
    )
    ffn_shard = lax.psum_scatter(ffn_raw, "seq", scatter_dimension=0, tiled=True).astype(WIDE)

    unit_grad_two = normed_two_grad * gain_values[1]
    resid_grad = own_slice(cotangent).astype(WIDE) + scale_two * (
        unit_grad_two - unit_two * jnp.mean(unit_grad_two * unit_two, axis=-1, keepdims=True)
    )
    branch_low = line_gather(resid_grad.astype(LOW))
    heads_grad = dot(branch_low, out_weight).astype(LOW)
    out_raw = dot(branch_low, heads_out, TN).astype(LOW)

    head_grads = to_heads(heads_grad)
    q_grad, kv_grad = attention_backward(ints, floats, head_queries, head_grads, key_values)
    kv_terms = group_exchange(
        [lax.dynamic_index_in_dim(kv_grad, part ^ k, 0, False) for k in range(parts)], parts
    )
    kv_sum = functools.reduce(lambda a, b: a + b, [t.astype(WIDE) for t in kv_terms]).astype(LOW)
    qkv_grad = from_heads(jnp.concatenate([q_grad, kv_sum], axis=2))

    one_grad_part = dot(qkv_grad, qkv_weight, NT).astype(LOW)
    normed_one_grad = line_sum(jnp.split(one_grad_part, head_count, axis=0))
    attn_raw = jnp.concatenate([dot(normed_one, qkv_grad, TN).astype(LOW), out_raw], axis=1)
    attn_shard = lax.psum_scatter(attn_raw, "seq", scatter_dimension=0, tiled=True).astype(WIDE)

    unit_one = own_slice(tokens).astype(WIDE) * own_slice(scale_one)
    unit_grad_one = normed_one_grad * gain_values[0]
    input_slice = resid_grad + own_slice(scale_one) * (
        unit_grad_one - unit_one * jnp.mean(unit_grad_one * unit_one, axis=-1, keepdims=True)
    )
    input_grad = line_gather(input_slice.astype(LOW)).astype(WIDE)

    own_gain = gain_master.astype(LOW).astype(WIDE)
    gain_terms = jnp.stack(
        [
            jnp.sum(qkv_shard.astype(WIDE) * attn_shard[:, : 3 * head_width], axis=1),
            jnp.sum(
                rest_shard[:, : 2 * hidden_width].astype(WIDE) * ffn_shard[:, : 2 * hidden_width],
                axis=1,
            ),
        ]
    ) / own_gain
    squares = jnp.sum(attn_shard * attn_shard) + jnp.sum(ffn_shard * ffn_shard)
    small = jnp.zeros((2, width + HD), WIDE)
    small = lax.dynamic_update_slice(small, gain_terms, (0, seq_index * shard_rows))
    small = small.at[0, width].set(squares)
    small = lax.psum(small, ("seq", "head"))
    gain_all = small[:, :width]
    gain_shard = lax.dynamic_slice_in_dim(gain_all, seq_index * shard_rows, shard_rows, 1)
    grad_norm = jnp.sqrt(small[0, width] + jnp.sum(gain_all * gain_all))
    clip_factor = jnp.minimum(1.0, CLIP / (grad_norm + 1e-06))

    qkv_shard_grad = (
        attn_shard[:, : 3 * head_width]
        .reshape(shard_rows, local_heads, 3, HD)
        .transpose(2, 0, 1, 3)
        .reshape(3, shard_rows, head_width)
    )
    attn_grad = (
        jnp.concatenate([qkv_shard_grad, attn_shard[None, :, 3 * head_width :]], axis=0) * clip_factor
    )
    ffn_grad = jnp.stack(jnp.split(ffn_shard, 3, axis=1)) * clip_factor
    gain_grad = gain_shard * clip_factor
    attn_state = adam_update(attn_grad, attn_first, attn_second, attn_master, RATE)
    ffn_state = adam_update(ffn_grad, ffn_first, ffn_second, ffn_master, RATE)
    gain_state = adam_update(gain_grad, gain_first, gain_second, gain_master, GAIN_RATE)
    return (
        layer_output,
        input_grad,
        attn_mass,
        grad_norm,
        attn_grad,
        attn_state[0],
        attn_state[1],
        attn_state[2],
        attn_state[3],
        ffn_grad,
        ffn_state[0],
        ffn_state[1],
        ffn_state[2],
        ffn_state[3],
        gain_grad,
        gain_state[0],
        gain_state[1],
        gain_state[2],
        gain_state[3],
    )


def solution(mesh):
    in_specs = (
        P("seq", None),
        P("seq", None),
        P(),
        P(None, "seq", "head"),
        P(None, "seq", "head"),
        P(None, "seq"),
        P(None, "seq", "head"),
        P(None, "seq", "head"),
        P(None, "seq", "head"),
        P(None, "seq", "head"),
        P(None, "seq"),
        P(None, "seq"),
    )
    out_specs = (
        P("seq", None),
        P("seq", None),
        P("head", "seq"),
        P(),
        P(None, "seq", "head"),
        P(None, "seq", "head"),
        P(None, "seq", "head"),
        P(None, "seq", "head"),
        P(None, "seq", "head"),
        P(None, "seq", "head"),
        P(None, "seq", "head"),
        P(None, "seq", "head"),
        P(None, "seq", "head"),
        P(None, "seq", "head"),
        P(None, "seq"),
        P(None, "seq"),
        P(None, "seq"),
        P(None, "seq"),
        P(None, "seq"),
    )
    return jax.shard_map(
        per_device, mesh=mesh, in_specs=in_specs, out_specs=out_specs, check_vma=False
    )
```

```python
import functools
import math

import jax
import jax.numpy as jnp
from jax import lax
from jax.experimental import pallas as pl
from jax.experimental.pallas import tpu as pltpu
from jax.sharding import PartitionSpec as P

HD = 128
STEP = 10


EPS = 1e-05
CLIP = 1.0
BETA1 = 0.5
BETA2 = 0.5
RATE = 0.03
GAIN_RATE = 0.3
DECAY = 0.1
ADAM_EPS = 1e-08

LOW = jnp.bfloat16
WIDE = jnp.float32
QUERY_FACTOR = -math.log2(math.e) / math.sqrt(HD)
FAR = 30000.0

NN = (((1,), (0,)), ((), ()))
NT = (((1,), (1,)), ((), ()))
TN = (((0,), (0,)), ((), ()))


def dot(left, right, dims=NN):
    return lax.dot_general(left, right, dims, preferred_element_type=WIDE)


def fill_key_columns(key_buf, sizes, cut):
    count, parts, block = sizes

    def step(at, _):
        place = at * block + lax.broadcasted_iota(jnp.int32, (block, HD), 0)
        lane = lax.broadcasted_iota(jnp.int32, (block, HD), 1)
        extra = jnp.where(lane < 3, 1.0, jnp.where((lane == 3) & (place < cut), FAR, 0.0))
        key_buf[pl.ds(pl.multiple_of(at * block, block), block), HD:] = extra.astype(LOW)
        return 0

    lax.fori_loop(0, count * parts, step, 0)


def query_columns(sizes, source, part, cut, floats):
    _, parts, block = sizes
    lane = lax.broadcasted_iota(jnp.int32, (block, HD), 1)
    place = (source * parts + part) * block + lax.broadcasted_iota(jnp.int32, (block, HD), 0)
    second = place >= cut

    def column(at):
        return jnp.where(second, floats[3 + at], floats[at])

    extra = jnp.where(
        lane == 0,
        column(0),
        jnp.where(
            lane == 1,
            column(1),
            jnp.where(lane == 2, column(2), jnp.where((lane == 3) & second, 1.0, 0.0)),
        ),
    )
    return extra.astype(LOW)


def in_causal_order(sizes, part, shape, key_dim):
    key_place = lax.broadcasted_iota(jnp.int32, shape, key_dim)
    query_place = part * sizes[2] + lax.broadcasted_iota(jnp.int32, shape, 1 - key_dim)
    return key_place <= query_place


def key_copies(sizes, part, key_values, key_buf, value_buf, sem):
    count, parts, block = sizes
    for other in range(parts):
        for at in range(count):
            row = pl.multiple_of((at * parts + (part ^ other)) * block, block)
            yield pltpu.make_async_copy(
                key_values[other].at[at, :, 0:HD], key_buf.at[pl.ds(row, block), 0:HD], sem.at[0]
            )
            yield pltpu.make_async_copy(
                key_values[other].at[at, :, HD:], value_buf.at[pl.ds(row, block), 0:HD], sem.at[0]
            )


def forward_kernel(sizes, ints, floats, q_ref, *rest):
    count, parts, block = sizes
    tile = block * parts
    key_values = rest[:parts]
    out_ref, mass_ref, key_buf, value_buf, query_buf, total, sem = rest[parts:]
    step = pl.program_id(0)
    cut, part = ints[0], ints[1]

    @pl.when(step == 0)
    def _():
        for copy in key_copies(sizes, part, key_values, key_buf, value_buf, sem):
            copy.start()
        fill_key_columns(key_buf, sizes, cut)
        value_buf[:, HD:] = jnp.ones((count * tile, HD), LOW)
        for copy in key_copies(sizes, part, key_values, key_buf, value_buf, sem):
            copy.wait()

    query_buf[:, :HD] = q_ref[...]
    query_buf[:, HD:] = query_columns(sizes, step, part, cut, floats)
    total[...] = jnp.zeros_like(total)
    first = jnp.where(step * tile >= cut, cut // tile, 0)

    def walk(at, masked):
        keys = pl.ds(pl.multiple_of(at * tile, tile), tile)
        exponent = dot(query_buf[...], key_buf[keys, :], NT)
        weight = pl.reciprocal(1.0 + jnp.exp2(exponent), approx=True)
        if masked:
            weight = jnp.where(in_causal_order(sizes, part, (block, tile), 1), weight, 0.0)
        total[...] += dot(weight.astype(LOW), value_buf[keys, :])

    def body(at, carry):
        walk(at, False)
        return carry

    lax.fori_loop(first, step, body, 0)
    walk(step, True)
    out_ref[...] = total[:, :HD].astype(LOW)
    mass_ref[...] = jnp.transpose(total[:, HD:])[0:1, :]


def attention_forward(sizes, ints, floats, queries, key_values):
    count, parts, block = sizes
    total_rows = count * parts * block
    pairs = total_rows * total_rows // (2 * parts)
    return pl.pallas_call(
        functools.partial(forward_kernel, sizes),
        out_shape=[
            jax.ShapeDtypeStruct((count, block, HD), LOW),
            jax.ShapeDtypeStruct((count, 1, block), WIDE),
        ],
        grid_spec=pltpu.PrefetchScalarGridSpec(
            num_scalar_prefetch=2,
            grid=(count,),
            in_specs=[pl.BlockSpec((None, block, HD), lambda i, *_: (i, 0, 0))]
            + [pl.BlockSpec(memory_space=pl.ANY)] * parts,
            out_specs=[
                pl.BlockSpec((None, block, HD), lambda i, *_: (i, 0, 0)),
                pl.BlockSpec((None, 1, block), lambda i, *_: (i, 0, 0)),
            ],
            scratch_shapes=[
                pltpu.VMEM((total_rows, 2 * HD), LOW),
                pltpu.VMEM((total_rows, 2 * HD), LOW),
                pltpu.VMEM((block, 2 * HD), LOW),
                pltpu.VMEM((block, 2 * HD), WIDE),
                pltpu.SemaphoreType.DMA((1,)),
            ],
        ),
        compiler_params=pltpu.CompilerParams(vmem_limit_bytes=48 * 2**20),
        cost_estimate=pl.CostEstimate(
            flops=pairs * 8 * HD, bytes_accessed=total_rows * HD * 8, transcendentals=2 * pairs
        ),
        name="attention_forward",
    )(ints, floats, queries, *key_values)


def backward_kernel(sizes, ints, floats, q_ref, grad_ref, *rest):
    count, parts, block = sizes
    tile = block * parts
    key_values = rest[:parts]
    q_grad_ref, *kv_grad_refs = rest[parts : 2 * parts + 1]
    key_buf, value_buf, turned, query_buf, q_total, k_total, v_total, sem = rest[2 * parts + 1 :]
    step = pl.program_id(0)
    cut, part = ints[0], ints[1]

    @pl.when(step == 0)
    def _():
        for copy in key_copies(sizes, part, key_values, key_buf, value_buf, sem):
            copy.start()
        fill_key_columns(key_buf, sizes, cut)
        k_total[...] = jnp.zeros_like(k_total)
        v_total[...] = jnp.zeros_like(v_total)
        for copy in key_copies(sizes, part, key_values, key_buf, value_buf, sem):
            copy.wait()

        def turn(at, carry):
            keys = pl.ds(pl.multiple_of(at * tile, tile), tile)
            turned[:, keys] = jnp.transpose(key_buf[keys, :HD])
            return carry

        lax.fori_loop(0, count, turn, 0)

    query_buf[:, :HD] = q_ref[...]
    query_buf[:, HD:] = query_columns(sizes, step, part, cut, floats)
    q_total[...] = jnp.zeros_like(q_total)
    first = jnp.where(step * tile >= cut, cut // tile, 0)

    def walk(at, masked):
        keys = pl.ds(pl.multiple_of(at * tile, tile), tile)
        exponent = dot(key_buf[keys, :], query_buf[...], NT)
        weight = pl.reciprocal(1.0 + jnp.exp2(exponent), approx=True)
        if masked:
            weight = jnp.where(in_causal_order(sizes, part, (tile, block), 0), weight, 0.0)
        weight_grad = dot(value_buf[keys, :], grad_ref[...], NT)
        score_grad = (weight_grad * (weight * (1.0 - weight))).astype(LOW)
        v_total[keys, :] += dot(weight.astype(LOW), grad_ref[...])
        k_total[keys, :] += dot(score_grad, query_buf[:, :HD])
        q_total[...] += dot(turned[:, keys], score_grad)

    def body(at, carry):
        walk(at, False)
        return carry

    lax.fori_loop(first, step, body, 0)
    walk(step, True)
    q_grad_ref[...] = (jnp.transpose(q_total[...]) * (1.0 / math.sqrt(HD))).astype(LOW)

    @pl.when(step == count - 1)
    def _():
        for other in range(parts):
            for at in range(count):
                row = pl.multiple_of((at * parts + (part ^ other)) * block, block)
                rows = pl.ds(row, block)
                kv_grad_refs[other][at, :, :HD] = (k_total[rows, :] * (-math.log(2.0))).astype(LOW)
                kv_grad_refs[other][at, :, HD:] = v_total[rows, :].astype(LOW)


def attention_backward(sizes, ints, floats, queries, grads, key_values):
    count, parts, block = sizes
    total_rows = count * parts * block
    pairs = total_rows * total_rows // (2 * parts)
    return pl.pallas_call(
        functools.partial(backward_kernel, sizes),
        out_shape=[
            jax.ShapeDtypeStruct((count, block, HD), LOW),
        ]
        + [jax.ShapeDtypeStruct((count, block, 2 * HD), LOW)] * parts,
        grid_spec=pltpu.PrefetchScalarGridSpec(
            num_scalar_prefetch=2,
            grid=(count,),
            in_specs=[pl.BlockSpec((None, block, HD), lambda i, *_: (i, 0, 0))] * 2
            + [pl.BlockSpec(memory_space=pl.ANY)] * parts,
            out_specs=[
                pl.BlockSpec((None, block, HD), lambda i, *_: (i, 0, 0)),
            ]
            + [pl.BlockSpec((count, block, 2 * HD), lambda i, *_: (0, 0, 0))] * parts,
            scratch_shapes=[
                pltpu.VMEM((total_rows, 2 * HD), LOW),
                pltpu.VMEM((total_rows, HD), LOW),
                pltpu.VMEM((HD, total_rows), LOW),
                pltpu.VMEM((block, 2 * HD), LOW),
                pltpu.VMEM((HD, block), WIDE),
                pltpu.VMEM((total_rows, HD), WIDE),
                pltpu.VMEM((total_rows, HD), WIDE),
                pltpu.SemaphoreType.DMA((1,)),
            ],
        ),
        compiler_params=pltpu.CompilerParams(vmem_limit_bytes=60 * 2**20),
        cost_estimate=pl.CostEstimate(
            flops=pairs * 100 * HD, bytes_accessed=total_rows * HD * 16, transcendentals=2 * pairs
        ),
        name="attention_backward",
    )(ints, floats, queries, grads, *key_values)


def attention_scalars(seq_lengths, total_rows, part):
    cut = seq_lengths[0]
    length = jnp.log2(jnp.stack([cut, total_rows - cut]).astype(WIDE))
    high = lax.reduce_precision(length, 8, 7)
    middle = lax.reduce_precision(length - high, 8, 7)
    low = length - high - middle
    return (
        jnp.stack([cut, part]).astype(jnp.int32),
        jnp.stack([high, middle, low], axis=1).reshape(6),
    )


def ffn_kernel(pieces, table, *refs):
    given = refs[:pieces]
    c_ref, gate_w, up_w, down_w = refs[pieces : pieces + 4]
    normed_ref, hidden_ref, gate_ref, up_ref, two_ref, total, sem = refs[pieces + 4 :]
    step = pl.program_id(0)
    rows = normed_ref.shape[0]
    slots = table.shape[0]
    slot_rows = rows // slots

    @pl.when(step == 0)
    def _():
        def each(act):
            for slot in range(slots):
                for piece in range(pieces):

                    @pl.when(table[slot] == piece)
                    def _(slot=slot, piece=piece):
                        act(
                            pltpu.make_async_copy(
                                given[piece],
                                normed_ref.at[pl.ds(slot * slot_rows, slot_rows), :],
                                sem.at[slot],
                            )
                        )

        each(lambda copy: copy.start())
        total[...] = jnp.zeros_like(total)
        each(lambda copy: copy.wait())

    chunk = min(256, rows)
    for at in range(0, rows, chunk):
        here = pl.ds(at, chunk)
        gate = dot(normed_ref[here, :], gate_w[...])
        up = dot(normed_ref[here, :], up_w[...])
        grad = dot(c_ref[here, :], down_w[...])
        sig = 1.0 / (1.0 + jnp.exp(-gate))
        silu = gate * sig
        hidden_ref[here, :] = (silu * up).astype(LOW)
        gate_grad = (grad * up * (sig + silu * (1.0 - sig))).astype(LOW)
        up_grad = (grad * silu).astype(LOW)
        gate_ref[here, :] = gate_grad
        up_ref[here, :] = up_grad
        total[here, :] += dot(gate_grad, gate_w[...], NT) + dot(up_grad, up_w[...], NT)

    @pl.when(step == pl.num_programs(0) - 1)
    def _():
        two_ref[...] = total[...].astype(LOW)


def feed_forward(pieces, order, cotangent, half, weight, hidden_width):
    rows, width = cotangent.shape[0] // 2, cotangent.shape[1]
    step = min(512, hidden_width)
    steps = hidden_width // step
    out = jax.ShapeDtypeStruct((rows, hidden_width), LOW)
    full = jax.ShapeDtypeStruct((rows, width), LOW)
    once = pl.Buffered(1)
    whole = pl.BlockSpec((rows, width), lambda j, *_: (0, 0), pipeline_mode=once)
    return pl.pallas_call(
        functools.partial(ffn_kernel, len(pieces)),
        out_shape=[full, out, out, out, full],
        grid_spec=pltpu.PrefetchScalarGridSpec(
            num_scalar_prefetch=1,
            grid=(steps,),
            in_specs=[pl.BlockSpec(memory_space=pl.ANY)] * len(pieces)
            + [
                pl.BlockSpec((rows, width), lambda j, *_: (half, 0), pipeline_mode=once),
                pl.BlockSpec((width, step), lambda j, *_: (0, j)),
                pl.BlockSpec((width, step), lambda j, *_: (0, steps + j)),
                pl.BlockSpec((width, step), lambda j, *_: (0, 2 * steps + j)),
            ],
            out_specs=[whole]
            + [pl.BlockSpec((rows, step), lambda j, *_: (0, j))] * 3
            + [whole],
            scratch_shapes=[pltpu.VMEM((rows, width), WIDE), pltpu.SemaphoreType.DMA((order.shape[0],))],
        ),
        compiler_params=pltpu.CompilerParams(vmem_limit_bytes=60 * 2**20),
        cost_estimate=pl.CostEstimate(
            flops=10 * rows * width * hidden_width,
            bytes_accessed=6 * width * hidden_width,
            transcendentals=rows * hidden_width,
        ),
        name="feed_forward",
    )(order, *pieces, cotangent, weight, weight, weight)


def ffn_wgrad_kernel(steps, n_a, n_b, c_ref, gate_a, gate_b, up_a, up_b, hid_a, hid_b, out_ref, n_turned, c_turned):
    step = pl.program_id(0)
    half = n_a.shape[0]

    @pl.when(step == 0)
    def _():
        n_turned[:, :half] = jnp.transpose(n_a[...])
        n_turned[:, half:] = jnp.transpose(n_b[...])
        c_turned[...] = jnp.transpose(c_ref[...])

    def product(turned, first, second):
        out_ref[...] = (dot(turned[:, :half], first[...]) + dot(turned[:, half:], second[...])).astype(LOW)

    @pl.when(step < steps)
    def _():
        product(n_turned, gate_a, gate_b)

    @pl.when((step >= steps) & (step < 2 * steps))
    def _():
        product(n_turned, up_a, up_b)

    @pl.when(step >= 2 * steps)
    def _():
        product(c_turned, hid_a, hid_b)


def feed_forward_wgrad(normed, cotangent, gate_grad, up_grad, hidden):
    rows, width = cotangent.shape
    hidden_width = hidden[0].shape[1]
    step = min(512, hidden_width)
    steps = hidden_width // step
    once = pl.Buffered(1)

    def whole(count):
        return pl.BlockSpec((count, width), lambda j: (0, 0), pipeline_mode=once)

    def third(at):
        return pl.BlockSpec((rows // 2, step), lambda j: (0, jnp.clip(j - at * steps, 0, steps - 1)))

    return pl.pallas_call(
        functools.partial(ffn_wgrad_kernel, steps),
        out_shape=jax.ShapeDtypeStruct((width, 3 * hidden_width), LOW),
        grid=(3 * steps,),
        in_specs=[whole(rows // 2), whole(rows // 2), whole(rows)]
        + [third(0)] * 2
        + [third(1)] * 2
        + [third(2)] * 2,
        out_specs=pl.BlockSpec((width, step), lambda j: (0, j)),
        scratch_shapes=[pltpu.VMEM((width, rows), LOW), pltpu.VMEM((width, rows), LOW)],
        compiler_params=pltpu.CompilerParams(vmem_limit_bytes=60 * 2**20),
        cost_estimate=pl.CostEstimate(
            flops=rows * width,
            bytes_accessed=rows * width,
            transcendentals=0,
        ),
        name="feed_forward_wgrad",
    )(*normed, cotangent, *gate_grad, *up_grad, *hidden)


def adam_kernel(clip, grad, first, second, master, grad_out, first_out, second_out, new_out, low_out):
    gradient = grad[...].astype(WIDE) * clip[0]
    grad_out[...] = gradient
    first_new, second_new, master_new, low = adam_update(
        gradient, first[...], second[...], master[...], RATE
    )
    first_out[...] = first_new
    second_out[...] = second_new
    new_out[...] = master_new
    low_out[...] = low


def adam_arrays(clip_factor, grad, first, second, master):
    arrays, rows, columns = master.shape
    step = min(rows, max(16, 2**17 // columns))
    state = pl.BlockSpec((None, step, columns), lambda a, i, *_: (a, i, 0))
    wide = jax.ShapeDtypeStruct(master.shape, WIDE)
    return pl.pallas_call(
        adam_kernel,
        out_shape=[wide] * 4 + [jax.ShapeDtypeStruct(master.shape, LOW)],
        grid_spec=pltpu.PrefetchScalarGridSpec(
            num_scalar_prefetch=1,
            grid=(arrays, rows // step),
            in_specs=[pl.BlockSpec((step, columns), lambda a, i, *_: (i, a))] + [state] * 3,
            out_specs=[state] * 5,
        ),
        compiler_params=pltpu.CompilerParams(vmem_limit_bytes=32 * 2**20),
        cost_estimate=pl.CostEstimate(
            flops=20 * master.size, bytes_accessed=32 * master.size, transcendentals=2 * master.size
        ),
        name="adam",
    )(clip_factor.reshape(1), grad, first, second, master)


def slice_sum(terms):
    count = lax.axis_size("head")
    got = lax.all_to_all(terms, "head", split_axis=0, concat_axis=0, tiled=True)
    rows = terms.shape[0] // count
    return functools.reduce(
        lambda a, b: a + b, [got[j * rows : (j + 1) * rows].astype(WIDE) for j in range(count)]
    )


def added(*terms):
    return functools.reduce(lambda a, b: a + b, [t.astype(WIDE) for t in terms])


def line_sum_begin(terms):
    inward = [(0, 1), (3, 2)]
    far = lax.ppermute(terms[3], "head", inward)
    outer = lax.ppermute(terms[0], "head", [(1, 0), (2, 3)])
    middle = lax.ppermute(terms[2], "head", inward)
    near = lax.ppermute(terms[1], "head", inward)
    return far, outer, middle, near


def line_sum_end(terms, got):
    at = lax.axis_index("head")
    far, outer, middle, near = got
    far_in = lax.ppermute(added(far, terms[3]).astype(LOW), "head", [(1, 3), (2, 0)])
    middle_in = lax.ppermute(added(middle, terms[2]).astype(LOW), "head", [(1, 2), (2, 1)])
    return jnp.where(
        (at == 0) | (at == 3),
        added(terms[0], outer, far_in),
        added(terms[1], near, middle_in),
    )


def gather_step_one(piece):
    return (
        lax.ppermute(piece, "head", [(0, 1), (1, 2), (2, 3)]),
        lax.ppermute(piece, "head", [(3, 2), (2, 1), (1, 0)]),
    )


def gather_step_two(got):
    return (
        lax.ppermute(got[0], "head", [(1, 2), (2, 3)]),
        lax.ppermute(got[1], "head", [(2, 1), (1, 0)]),
    )


def gather_step_three(got):
    at = lax.axis_index("head")
    return (lax.ppermute(jnp.where(at == 2, got[0], got[1]), "head", [(2, 3), (1, 0)]),)


def gathered_pieces(piece, one, two, three):
    away = lax.axis_index("head") - jnp.arange(4, dtype=jnp.int32)
    order = jnp.where(
        away == 0, 0, jnp.where(jnp.abs(away) == 3, 5, jnp.where(away > 0, away, 2 - away))
    )
    return [piece, one[0], two[0], one[1], two[1], three[0]], order


def line_gather_pieces(piece):
    count = lax.axis_size("head")
    if count != 4:
        full = lax.all_gather(piece, "head", axis=0, tiled=True)
        return jnp.split(full, count, axis=0), jnp.arange(count, dtype=jnp.int32)
    one = gather_step_one(piece)
    two = gather_step_two(one)
    return gathered_pieces(piece, one, two, gather_step_three(two))


def line_gather_wide(full, piece, got):
    count = lax.axis_size("head")
    at = lax.axis_index("head")
    rows = piece.shape[1]
    if count != 4:
        every = lax.all_gather(piece, "head", axis=0, tiled=False).astype(WIDE)
        return every.transpose(1, 0, 2, 3).reshape(full.shape)
    one, two, three = got
    for where, part in (
        (at, piece),
        (at - 1, one[0]),
        (at + 1, one[1]),
        (at - 2, two[0]),
        (at + 2, two[1]),
        (jnp.where(at == 0, 3, jnp.where(at == 3, 0, at)), three[0]),
    ):
        there = (where >= 0) & (where < count) & (where != at)
        full = lax.dynamic_update_slice(
            full,
            jnp.where(there, part, piece).astype(WIDE),
            (0, jnp.where(there, where, at) * rows, 0),
        )
    return full


def group_exchange(blocks, parts):
    count = lax.axis_size("seq")
    return [blocks[0]] + [
        lax.ppermute(blocks[k], "seq", [(j, j ^ k) for j in range(count)]) for k in range(1, parts)
    ]


def direct_terms(terms):
    at = lax.axis_index("head")
    count = lax.axis_size("head")
    return [lax.dynamic_index_in_dim(terms, at, 1, False)] + [
        lax.ppermute(
            lax.dynamic_index_in_dim(terms, at ^ k, 1, False),
            "head",
            [(j, j ^ k) for j in range(count)],
        )
        for k in range(1, count)
    ]


def direct_gather(piece):
    at = lax.axis_index("head")
    count = lax.axis_size("head")
    full = jnp.zeros((count,) + piece.shape, piece.dtype)
    for k in range(count):
        term = piece if k == 0 else lax.ppermute(piece, "head", [(j, j ^ k) for j in range(count)])
        full = lax.dynamic_update_index_in_dim(full, term, at ^ k, 0)
    return full


def sum_everywhere(values):
    for axis in ("seq", "head"):
        count = lax.axis_size(axis)
        bit = 1
        while bit < count:
            values = values + lax.ppermute(values, axis, [(j, j ^ bit) for j in range(count)])
            bit *= 2
    return values


def after(value, *others):
    return lax.optimization_barrier((value,) + others)[0]


def adam_update(gradient, first_moment, second, master, step_rate):
    first_new = BETA1 * first_moment + (1.0 - BETA1) * gradient
    second_new = BETA2 * second + (1.0 - BETA2) * gradient * gradient
    first_hat = first_new / (1.0 - BETA1**STEP)
    second_hat = second_new / (1.0 - BETA2**STEP)
    master_new = master - step_rate * (
        first_hat / (jnp.sqrt(second_hat) + ADAM_EPS) + DECAY * master
    )
    return (first_new, second_new, master_new, master_new.astype(LOW))


def per_device(
    tokens,
    cotangent,
    seq_lengths,
    attn_master,
    ffn_master,
    gain_master,
    attn_first,
    attn_second,
    ffn_first,
    ffn_second,
    gain_first,
    gain_second,
):
    seq_count = lax.axis_size("seq")
    head_count = lax.axis_size("head")
    seq_index = lax.axis_index("seq")
    head_index = lax.axis_index("head")
    local_rows, width = tokens.shape
    total_rows = local_rows * seq_count
    head_width = attn_master.shape[2]
    hidden_width = ffn_master.shape[2]
    shard_rows = attn_master.shape[1]
    local_heads = head_width // HD
    parts = seq_count // local_heads
    block = local_rows // parts
    part = seq_index % parts
    slice_rows = local_rows // head_count
    sub = slice_rows // parts
    sizes = (seq_count, parts, block)
    half_parts = parts // 2
    half_rows = local_rows // 2
    quarter_rows = slice_rows // 2

    def own_slice(array):
        columns = array.shape[1]
        return lax.dynamic_slice_in_dim(
            array.reshape(parts, block, columns), head_index * sub, sub, 1
        ).reshape(slice_rows, columns)

    def halves(array):
        return array[: array.shape[0] // 2], array[array.shape[0] // 2 :]

    def by_slices(array):
        rows, columns = array.shape
        return (
            array.reshape(rows // half_rows, half_parts, head_count, sub, columns)
            .transpose(0, 2, 1, 3, 4)
            .reshape(rows, columns)
        )

    qkv_shard = (
        attn_master[:3]
        .astype(LOW)
        .reshape(3, shard_rows, local_heads, HD)
        .transpose(1, 2, 0, 3)
        .reshape(shard_rows, 3 * head_width)
    )
    ffn_shard_low = jnp.concatenate([ffn_master[0], ffn_master[1], ffn_master[2]], axis=1).astype(LOW)
    gain_values = lax.all_gather(gain_master.astype(LOW), "seq", axis=1, tiled=True).astype(WIDE)
    qkv_weight = lax.all_gather(qkv_shard, "seq", axis=0, tiled=True)
    out_rows = (
        direct_gather(attn_master[3].astype(LOW)).transpose(1, 0, 2).reshape(shard_rows, width)
    )

    ints, floats = attention_scalars(seq_lengths, total_rows, part)

    gain_values, out_rows = lax.optimization_barrier((gain_values, out_rows))
    residual = tokens.astype(WIDE)
    scale_one = lax.rsqrt(jnp.mean(residual * residual, axis=-1, keepdims=True) + EPS)
    normed_one = (residual * scale_one * gain_values[0]).astype(LOW)
    column = jnp.arange(3 * head_width, dtype=jnp.int32) % (3 * HD)
    column_factor = jnp.where(column < HD, QUERY_FACTOR, 1.0).astype(WIDE)
    projected = (dot(normed_one, qkv_weight) * column_factor).astype(LOW)

    sent = (
        projected.reshape(parts, block, local_heads, 3 * HD)
        .transpose(2, 0, 1, 3)
        .reshape(seq_count, block, 3 * HD)
    )
    out_weight = lax.all_gather(after(out_rows, sent), "seq", axis=0, tiled=True)
    qkv = lax.all_to_all(sent, "seq", split_axis=0, concat_axis=0, tiled=True)
    head_queries = qkv[:, :, :HD]
    own_key_values = qkv[:, :, HD:]
    key_values = group_exchange([own_key_values] * parts, parts)
    ffn_weight = lax.all_gather(after(ffn_shard_low, key_values[-1]), "seq", axis=0, tiled=True)
    mixed, mass = attention_forward(sizes, ints, floats, head_queries, key_values)

    everywhere = ("seq", "head")
    slices_out = lax.all_to_all(
        mixed.reshape(seq_count * head_count, sub, HD), everywhere, split_axis=0, concat_axis=0, tiled=True
    )
    heads_out = (
        slices_out.reshape(local_heads, parts, head_count, sub, HD)
        .transpose(1, 3, 2, 0, 4)
        .reshape(slice_rows, width)
    )
    mass_high = lax.reduce_precision(mass, 8, 7)
    mass_middle = lax.reduce_precision(mass - mass_high, 8, 7)
    mass_parts = jnp.stack([mass_high, mass_middle, mass - mass_high - mass_middle], axis=1).astype(LOW)
    mass_rows = block // HD
    mass_sent = jnp.pad(
        mass_parts.reshape(seq_count, mass_rows, 3 * HD), ((0, 0), (0, 16 - mass_rows), (0, 0))
    )

    attn_sum = dot(heads_out, out_weight, NT)
    resid_one = own_slice(tokens).astype(WIDE) + attn_sum
    scale_two = lax.rsqrt(jnp.mean(resid_one * resid_one, axis=-1, keepdims=True) + EPS)
    unit_two = resid_one * scale_two
    normed_slice = (unit_two * gain_values[1]).astype(LOW)
    cot_slices = by_slices(cotangent)
    first_slice, second_slice = halves(normed_slice)

    first_pieces, order = line_gather_pieces(first_slice)
    second_pieces, order = line_gather_pieces(second_slice)
    first_pieces[-1], *second_pieces = lax.optimization_barrier((first_pieces[-1], *second_pieces))
    normed_a, hidden_a, gate_a, up_a, two_a = feed_forward(
        first_pieces, order, cot_slices, 0, ffn_weight, hidden_width
    )
    second_pieces[-1] = after(second_pieces[-1], two_a)
    normed_b, hidden_b, gate_b, up_b, two_b = feed_forward(
        second_pieces, order, cot_slices, 1, ffn_weight, hidden_width
    )
    two_sum_a = slice_sum(two_a)
    two_sum_b = slice_sum(two_b)
    two_sum_a, hidden_a, hidden_b = lax.optimization_barrier((two_sum_a, hidden_a, hidden_b))
    ffn_raw = feed_forward_wgrad(
        (normed_a, normed_b), cot_slices, (gate_a, gate_b), (up_a, up_b), (hidden_a, hidden_b)
    )
    ffn_shard = lax.psum_scatter(ffn_raw, "seq", scatter_dimension=0, tiled=True)
    down_weight = ffn_weight[:, 2 * hidden_width :]
    def norm_grad(grad, unit, scale, gain, passed):
        inner = grad * gain
        return passed + scale * (inner - unit * jnp.mean(inner * unit, axis=-1, keepdims=True))

    two_sum_b = after(two_sum_b, ffn_raw)
    cot_own = own_slice(cotangent).astype(WIDE)
    resid_grads = [
        norm_grad(*args, gain_values[1], passed)
        for args, passed in zip(
            zip((two_sum_a, two_sum_b), halves(unit_two), halves(scale_two)), halves(cot_own)
        )
    ]
    branch_low = jnp.concatenate([r.astype(LOW) for r in resid_grads], axis=0)
    heads_grad = dot(branch_low, out_weight).astype(LOW)

    grads_sent = (
        heads_grad.reshape(parts, sub, head_count, local_heads, HD)
        .transpose(3, 0, 2, 1, 4)
        .reshape(seq_count * head_count, sub, HD)
    )
    head_grads = lax.all_to_all(
        grads_sent, everywhere, split_axis=0, concat_axis=0, tiled=True
    ).reshape(seq_count, block, HD)
    out_raw = dot(branch_low, heads_out, TN).astype(LOW)
    out_mine = lax.psum_scatter(out_raw, "seq", scatter_dimension=0, tiled=True)
    hidden_a, hidden_b, grads_sent = lax.optimization_barrier((hidden_a, hidden_b, grads_sent))
    ffn_part = jnp.stack(
        [dot(hidden_a, down_weight, NT).astype(LOW), dot(hidden_b, down_weight, NT).astype(LOW)]
    )
    ffn_terms = direct_terms(
        after(ffn_part, head_grads).reshape(2, head_count, quarter_rows, width)
    )
    early_terms, late_terms = ffn_terms[:3], ffn_terms[3:]
    q_grad, *kv_grads = attention_backward(sizes, ints, floats, head_queries, head_grads, key_values)
    kv_grads, early_terms = lax.optimization_barrier((kv_grads, early_terms))
    kv_terms = group_exchange(kv_grads, parts)
    kv_sum = functools.reduce(lambda a, b: a + b, [t.astype(WIDE) for t in kv_terms]).astype(LOW)
    returned = lax.all_to_all(
        jnp.concatenate([jnp.concatenate([q_grad, kv_sum], axis=2), mass_sent], axis=1),
        "seq",
        split_axis=0,
        concat_axis=0,
        tiled=True,
    )
    ffn_sum = added(*early_terms, *late_terms).reshape(slice_rows, width)
    layer_slice = (resid_one + ffn_sum).astype(LOW).reshape(parts, sub, width)
    line = head_count == 4
    layer_one = gather_step_one(layer_slice) if line else ()
    returned, layer_one = lax.optimization_barrier((returned, layer_one))
    grads_back = returned[:, :block]
    mass_got = returned[:, block : block + mass_rows].astype(WIDE).reshape(local_heads, parts, 3, block)
    attn_mass = jnp.sum(mass_got, axis=2).reshape(local_heads, local_rows)
    qkv_grad = (
        grads_back.reshape(local_heads, parts, block, 3 * HD)
        .transpose(1, 2, 0, 3)
        .reshape(local_rows, 3 * head_width)
    )

    one_grad_part = (
        dot(qkv_grad, qkv_weight, NT).astype(LOW).reshape(parts, head_count, sub, width)
    )
    if line:
        forward = jnp.arange(4, dtype=jnp.int32)
        order = jnp.where(head_index < 2, forward, 3 - forward)
        terms = [lax.dynamic_index_in_dim(one_grad_part, order[k], 1, False) for k in range(4)]
        got = line_sum_begin(terms)
        first, qkv_grad = lax.optimization_barrier((got[0], qkv_grad))
        normed_one_grad = line_sum_end(terms, (first,) + got[1:])
    else:
        normed_one_grad = lax.psum_scatter(
            one_grad_part, "head", scatter_dimension=1, tiled=True
        ).astype(WIDE)
    qkv_raw = dot(normed_one, qkv_grad, TN).astype(LOW)
    qkv_raw, ffn_shard, out_mine = lax.optimization_barrier((qkv_raw, ffn_shard, out_mine))
    qkv_mine = lax.psum_scatter(qkv_raw, "seq", scatter_dimension=0, tiled=True)
    normed_one_grad, out_mine = lax.optimization_barrier((normed_one_grad, out_mine))
    out_terms = jnp.stack(
        [out_mine[:, j * head_width : (j + 1) * head_width] for j in range(head_count)]
    )
    out_own = added(*direct_terms(out_terms[None])).astype(LOW)[0]
    normed_one_grad = normed_one_grad.reshape(slice_rows, width)
    own_scale = own_slice(scale_one)
    unit_one = own_slice(tokens).astype(WIDE) * own_scale
    input_slice = norm_grad(
        normed_one_grad, unit_one, own_scale, gain_values[0], jnp.concatenate(resid_grads, axis=0)
    )
    input_slice = input_slice.astype(LOW).reshape(parts, sub, width)
    input_one = gather_step_one(input_slice) if line else ()
    layer_two = gather_step_two(layer_one) if line else ()
    input_one, layer_two, out_own = lax.optimization_barrier((input_one, layer_two, out_own))
    input_two = gather_step_two(input_one) if line else ()
    layer_three = gather_step_three(layer_two) if line else ()
    own_gain = gain_master.astype(LOW).astype(WIDE)
    qkv_wide = qkv_mine.astype(WIDE)
    ffn_wide = ffn_shard.astype(WIDE)
    gain_two_term = (
        jnp.sum(
            ffn_shard_low[:, : 2 * hidden_width].astype(WIDE) * ffn_wide[:, : 2 * hidden_width], axis=1
        )
        / own_gain[1]
    )
    gain_one_term = jnp.sum(qkv_shard.astype(WIDE) * qkv_wide, axis=1) / own_gain[0]
    out_wide = out_own.astype(WIDE)
    squares = jnp.sum(ffn_wide * ffn_wide) + jnp.sum(out_wide * out_wide) + jnp.sum(qkv_wide * qkv_wide)
    row = jnp.arange(2 * seq_count + 8, dtype=jnp.int32)[:, None]
    small = jnp.where(
        row == seq_index,
        gain_one_term[None, :],
        jnp.where(
            row == seq_count + seq_index,
            gain_two_term[None, :],
            jnp.where(row == 2 * seq_count, squares / shard_rows, 0.0),
        ),
    )
    small = sum_everywhere(small)
    gain_all = small[: 2 * seq_count]
    gain_shard = jnp.stack(
        [
            lax.dynamic_index_in_dim(gain_all, seq_index, 0, False),
            lax.dynamic_index_in_dim(gain_all, seq_count + seq_index, 0, False),
        ]
    )
    grad_norm = jnp.sqrt(jnp.sum(small[2 * seq_count]) + jnp.sum(gain_all * gain_all))
    clip_factor = jnp.minimum(1.0, CLIP / (grad_norm + 1e-06))

    attn_grads = jnp.concatenate(
        [
            qkv_mine.reshape(shard_rows, local_heads, 3, HD)
            .transpose(0, 2, 1, 3)
            .reshape(shard_rows, 3 * head_width),
            out_own,
        ],
        axis=1,
    )
    input_two, layer_three, clip_factor, attn_grads = lax.optimization_barrier(
        (input_two, layer_three, clip_factor, attn_grads)
    )
    input_three = gather_step_three(input_two) if line else ()
    blank = jnp.zeros((parts, block, width), WIDE)
    layer_output = line_gather_wide(blank, layer_slice, (layer_one, layer_two, layer_three))
    layer_output = layer_output.reshape(local_rows, width)
    input_grad = line_gather_wide(blank, input_slice, (input_one, input_two, input_three))
    input_grad = input_grad.reshape(local_rows, width)
    gain_grad = gain_shard * clip_factor
    ffn_state = adam_arrays(clip_factor, ffn_shard, ffn_first, ffn_second, ffn_master)
    attn_state = adam_arrays(clip_factor, attn_grads, attn_first, attn_second, attn_master)
    gain_state = adam_update(gain_grad, gain_first, gain_second, gain_master, GAIN_RATE)
    return (
        layer_output,
        input_grad,
        attn_mass,
        grad_norm,
        attn_state[0],
        attn_state[1],
        attn_state[2],
        attn_state[3],
        attn_state[4],
        ffn_state[0],
        ffn_state[1],
        ffn_state[2],
        ffn_state[3],
        ffn_state[4],
        gain_grad,
        gain_state[0],
        gain_state[1],
        gain_state[2],
        gain_state[3],
    )


def solution(mesh):
    in_specs = (
        P("seq", None),
        P("seq", None),
        P(),
        P(None, "seq", "head"),
        P(None, "seq", "head"),
        P(None, "seq"),
        P(None, "seq", "head"),
        P(None, "seq", "head"),
        P(None, "seq", "head"),
        P(None, "seq", "head"),
        P(None, "seq"),
        P(None, "seq"),
    )
    out_specs = (
        P("seq", None),
        P("seq", None),
        P("head", "seq"),
        P(),
        P(None, "seq", "head"),
        P(None, "seq", "head"),
        P(None, "seq", "head"),
        P(None, "seq", "head"),
        P(None, "seq", "head"),
        P(None, "seq", "head"),
        P(None, "seq", "head"),
        P(None, "seq", "head"),
        P(None, "seq", "head"),
        P(None, "seq", "head"),
        P(None, "seq"),
        P(None, "seq"),
        P(None, "seq"),
        P(None, "seq"),
        P(None, "seq"),
    )
    return jax.shard_map(
        per_device, mesh=mesh, in_specs=in_specs, out_specs=out_specs, check_vma=False
    )
```

```python
import functools
import math

import jax
import jax.numpy as jnp
from jax import lax
from jax.experimental import pallas as pl
from jax.experimental.pallas import tpu as pltpu
from jax.sharding import PartitionSpec as P

HD = 128
STEP = 10


EPS = 1e-05
CLIP = 1.0
BETA1 = 0.5
BETA2 = 0.5
RATE = 0.03
GAIN_RATE = 0.3
DECAY = 0.1
ADAM_EPS = 1e-08

LOW = jnp.bfloat16
WIDE = jnp.float32
QUERY_FACTOR = -math.log2(math.e) / math.sqrt(HD)
FAR = 30000.0

NN = (((1,), (0,)), ((), ()))
NT = (((1,), (1,)), ((), ()))
TN = (((0,), (0,)), ((), ()))


def dot(left, right, dims=NN):
    return lax.dot_general(left, right, dims, preferred_element_type=WIDE)


def fill_key_columns(key_buf, sizes, cut):
    count, parts, block = sizes

    def step(at, _):
        place = at * block + lax.broadcasted_iota(jnp.int32, (block, HD), 0)
        lane = lax.broadcasted_iota(jnp.int32, (block, HD), 1)
        extra = jnp.where(lane < 3, 1.0, jnp.where((lane == 3) & (place < cut), FAR, 0.0))
        key_buf[pl.ds(pl.multiple_of(at * block, block), block), HD:] = extra.astype(LOW)
        return 0

    lax.fori_loop(0, count * parts, step, 0)


def query_columns(sizes, source, part, cut, floats):
    _, parts, block = sizes
    lane = lax.broadcasted_iota(jnp.int32, (block, HD), 1)
    place = (source * parts + part) * block + lax.broadcasted_iota(jnp.int32, (block, HD), 0)
    second = place >= cut

    def column(at):
        return jnp.where(second, floats[3 + at], floats[at])

    extra = jnp.where(
        lane == 0,
        column(0),
        jnp.where(
            lane == 1,
            column(1),
            jnp.where(lane == 2, column(2), jnp.where((lane == 3) & second, 1.0, 0.0)),
        ),
    )
    return extra.astype(LOW)


def in_causal_order(sizes, part, shape, key_dim, first_key=0):
    key_place = first_key + lax.broadcasted_iota(jnp.int32, shape, key_dim)
    query_place = part * sizes[2] + lax.broadcasted_iota(jnp.int32, shape, 1 - key_dim)
    return key_place <= query_place


def key_copies(sizes, part, key_values, key_buf, value_buf, sem):
    count, parts, block = sizes
    for other in range(parts):
        for at in range(count):
            row = pl.multiple_of((at * parts + (part ^ other)) * block, block)
            yield pltpu.make_async_copy(
                key_values[other].at[at, :, 0:HD], key_buf.at[pl.ds(row, block), 0:HD], sem.at[0]
            )
            yield pltpu.make_async_copy(
                key_values[other].at[at, :, HD:], value_buf.at[pl.ds(row, block), 0:HD], sem.at[0]
            )


def forward_kernel(sizes, ints, floats, q_ref, *rest):
    count, parts, block = sizes
    tile = block * parts
    key_values = rest[:parts]
    out_ref, mass_ref, key_buf, value_buf, query_buf, total, sem = rest[parts:]
    step = pl.program_id(0)
    cut, part = ints[0], ints[1]

    @pl.when(step == 0)
    def _():
        for copy in key_copies(sizes, part, key_values, key_buf, value_buf, sem):
            copy.start()
        fill_key_columns(key_buf, sizes, cut)
        value_buf[:, HD:] = jnp.ones((count * tile, HD), LOW)
        for copy in key_copies(sizes, part, key_values, key_buf, value_buf, sem):
            copy.wait()

    query_buf[:, :HD] = q_ref[...]
    query_buf[:, HD:] = query_columns(sizes, step, part, cut, floats)
    total[...] = jnp.zeros_like(total)
    first = jnp.where(step * tile >= cut, cut // tile, 0)

    def walk(at, masked):
        keys = pl.ds(pl.multiple_of(at * tile, tile), tile)
        exponent = dot(query_buf[...], key_buf[keys, :], NT)
        weight = pl.reciprocal(1.0 + jnp.exp2(exponent), approx=True)
        if masked:
            weight = jnp.where(in_causal_order(sizes, part, (block, tile), 1), weight, 0.0)
        total[...] += dot(weight.astype(LOW), value_buf[keys, :])

    def body(at, carry):
        walk(at, False)
        return carry

    lax.fori_loop(first, step, body, 0)
    walk(step, True)
    out_ref[...] = total[:, :HD].astype(LOW)
    mass_ref[...] = jnp.transpose(total[:, HD:])[0:1, :]


def attention_forward(sizes, ints, floats, queries, key_values):
    count, parts, block = sizes
    total_rows = count * parts * block
    pairs = total_rows * total_rows // (2 * parts)
    return pl.pallas_call(
        functools.partial(forward_kernel, sizes),
        out_shape=[
            jax.ShapeDtypeStruct((count, block, HD), LOW),
            jax.ShapeDtypeStruct((count, 1, block), WIDE),
        ],
        grid_spec=pltpu.PrefetchScalarGridSpec(
            num_scalar_prefetch=2,
            grid=(count,),
            in_specs=[pl.BlockSpec((None, block, HD), lambda i, *_: (i, 0, 0))]
            + [pl.BlockSpec(memory_space=pl.ANY)] * parts,
            out_specs=[
                pl.BlockSpec((None, block, HD), lambda i, *_: (i, 0, 0)),
                pl.BlockSpec((None, 1, block), lambda i, *_: (i, 0, 0)),
            ],
            scratch_shapes=[
                pltpu.VMEM((total_rows, 2 * HD), LOW),
                pltpu.VMEM((total_rows, 2 * HD), LOW),
                pltpu.VMEM((block, 2 * HD), LOW),
                pltpu.VMEM((block, 2 * HD), WIDE),
                pltpu.SemaphoreType.DMA((1,)),
            ],
        ),
        compiler_params=pltpu.CompilerParams(vmem_limit_bytes=48 * 2**20),
        cost_estimate=pl.CostEstimate(
            flops=pairs * 8 * HD, bytes_accessed=total_rows * HD * 8, transcendentals=2 * pairs
        ),
        name="attention_forward",
    )(ints, floats, queries, *key_values)


def backward_kernel(sizes, ints, floats, q_ref, grad_ref, *rest):
    count, parts, block = sizes
    tile = block * parts
    chunk = min(256, tile)
    key_values = rest[:parts]
    q_grad_ref, *kv_grad_refs = rest[parts : 2 * parts + 1]
    key_buf, value_buf, query_buf, q_turned, grad_turned, q_total, k_total, v_total, sem = rest[
        2 * parts + 1 :
    ]
    step = pl.program_id(0)
    cut, part = ints[0], ints[1]

    @pl.when(step == 0)
    def _():
        for copy in key_copies(sizes, part, key_values, key_buf, value_buf, sem):
            copy.start()
        fill_key_columns(key_buf, sizes, cut)
        k_total[...] = jnp.zeros_like(k_total)
        v_total[...] = jnp.zeros_like(v_total)
        for copy in key_copies(sizes, part, key_values, key_buf, value_buf, sem):
            copy.wait()

    query_buf[:, :HD] = q_ref[...]
    query_buf[:, HD:] = query_columns(sizes, step, part, cut, floats)
    q_turned[...] = jnp.transpose(q_ref[...])
    grad_turned[...] = jnp.transpose(grad_ref[...])
    q_total[...] = jnp.zeros_like(q_total)
    first = jnp.where(step * tile >= cut, cut // tile, 0)

    def walk(at, masked):
        base = pl.multiple_of(at * tile, tile)

        def products(place):
            keys = pl.ds(base + place, chunk)
            return (
                dot(query_buf[...], key_buf[keys, :], NT),
                dot(grad_ref[...], value_buf[keys, :], NT),
            )

        score_grads = []
        following = products(0)
        for place in range(0, tile, chunk):
            exponent, weight_grad = following
            if place + chunk < tile:
                following = products(place + chunk)
            weight = pl.reciprocal(1.0 + jnp.exp2(exponent), approx=True)
            if masked:
                weight = jnp.where(
                    in_causal_order(sizes, part, (block, chunk), 1, place), weight, 0.0
                )
            score_grad = (weight_grad * (weight - weight * weight)).astype(LOW)
            keys = pl.ds(base + place, chunk)
            v_total[:, keys] += dot(grad_turned[...], weight.astype(LOW))
            k_total[:, keys] += dot(q_turned[...], score_grad)
            score_grads.append(score_grad)
        q_total[...] += dot(
            jnp.concatenate(score_grads, axis=1), key_buf[pl.ds(base, tile), :HD]
        )

    def body(at, carry):
        walk(at, False)
        return carry

    lax.fori_loop(first, step, body, 0)
    walk(step, True)
    q_grad_ref[...] = (q_total[...] * (1.0 / math.sqrt(HD))).astype(LOW)

    @pl.when(step == count - 1)
    def _():
        for other in range(parts):
            for at in range(count):
                row = pl.multiple_of((at * parts + (part ^ other)) * block, block)
                rows = pl.ds(row, block)
                kv_grad_refs[other][at, :, :HD] = jnp.transpose(
                    k_total[:, rows] * (-math.log(2.0))
                ).astype(LOW)
                kv_grad_refs[other][at, :, HD:] = jnp.transpose(v_total[:, rows]).astype(LOW)


def attention_backward(sizes, ints, floats, queries, grads, key_values):
    count, parts, block = sizes
    total_rows = count * parts * block
    pairs = total_rows * total_rows // (2 * parts)
    return pl.pallas_call(
        functools.partial(backward_kernel, sizes),
        out_shape=[
            jax.ShapeDtypeStruct((count, block, HD), LOW),
        ]
        + [jax.ShapeDtypeStruct((count, block, 2 * HD), LOW)] * parts,
        grid_spec=pltpu.PrefetchScalarGridSpec(
            num_scalar_prefetch=2,
            grid=(count,),
            in_specs=[pl.BlockSpec((None, block, HD), lambda i, *_: (i, 0, 0))] * 2
            + [pl.BlockSpec(memory_space=pl.ANY)] * parts,
            out_specs=[
                pl.BlockSpec((None, block, HD), lambda i, *_: (i, 0, 0)),
            ]
            + [pl.BlockSpec((count, block, 2 * HD), lambda i, *_: (0, 0, 0))] * parts,
            scratch_shapes=[
                pltpu.VMEM((total_rows, 2 * HD), LOW),
                pltpu.VMEM((total_rows, HD), LOW),
                pltpu.VMEM((block, 2 * HD), LOW),
                pltpu.VMEM((HD, block), LOW),
                pltpu.VMEM((HD, block), LOW),
                pltpu.VMEM((block, HD), WIDE),
                pltpu.VMEM((HD, total_rows), WIDE),
                pltpu.VMEM((HD, total_rows), WIDE),
                pltpu.SemaphoreType.DMA((1,)),
            ],
        ),
        compiler_params=pltpu.CompilerParams(vmem_limit_bytes=60 * 2**20),
        cost_estimate=pl.CostEstimate(
            flops=pairs * 100 * HD, bytes_accessed=total_rows * HD * 16, transcendentals=2 * pairs
        ),
        name="attention_backward",
    )(ints, floats, queries, grads, *key_values)


def attention_scalars(seq_lengths, total_rows, part):
    cut = seq_lengths[0]
    length = jnp.log2(jnp.stack([cut, total_rows - cut]).astype(WIDE))
    high = lax.reduce_precision(length, 8, 7)
    middle = lax.reduce_precision(length - high, 8, 7)
    low = length - high - middle
    return (
        jnp.stack([cut, part]).astype(jnp.int32),
        jnp.stack([high, middle, low], axis=1).reshape(6),
    )


def ffn_kernel(pieces, table, *refs):
    given = refs[:pieces]
    c_ref, gate_w, up_w, down_w = refs[pieces : pieces + 4]
    normed_ref, hidden_ref, gate_ref, up_ref, two_ref, total, sem = refs[pieces + 4 :]
    step = pl.program_id(0)
    rows = normed_ref.shape[0]
    slots = table.shape[0]
    slot_rows = rows // slots

    @pl.when(step == 0)
    def _():
        def each(act):
            for slot in range(slots):
                for piece in range(pieces):

                    @pl.when(table[slot] == piece)
                    def _(slot=slot, piece=piece):
                        act(
                            pltpu.make_async_copy(
                                given[piece],
                                normed_ref.at[pl.ds(slot * slot_rows, slot_rows), :],
                                sem.at[slot],
                            )
                        )

        each(lambda copy: copy.start())
        total[...] = jnp.zeros_like(total)
        each(lambda copy: copy.wait())

    chunk = min(256, rows)
    for at in range(0, rows, chunk):
        here = pl.ds(at, chunk)
        gate = dot(normed_ref[here, :], gate_w[...])
        up = dot(normed_ref[here, :], up_w[...])
        grad = dot(c_ref[here, :], down_w[...])
        sig = 1.0 / (1.0 + jnp.exp(-gate))
        silu = gate * sig
        hidden_ref[here, :] = (silu * up).astype(LOW)
        gate_grad = (grad * up * (sig + silu * (1.0 - sig))).astype(LOW)
        up_grad = (grad * silu).astype(LOW)
        gate_ref[here, :] = gate_grad
        up_ref[here, :] = up_grad
        total[here, :] += dot(gate_grad, gate_w[...], NT) + dot(up_grad, up_w[...], NT)

    @pl.when(step == pl.num_programs(0) - 1)
    def _():
        two_ref[...] = total[...].astype(LOW)


def feed_forward(pieces, order, cotangent, half, weight, hidden_width):
    rows, width = cotangent.shape[0] // 2, cotangent.shape[1]
    step = min(512, hidden_width)
    steps = hidden_width // step
    out = jax.ShapeDtypeStruct((rows, hidden_width), LOW)
    full = jax.ShapeDtypeStruct((rows, width), LOW)
    once = pl.Buffered(1)
    whole = pl.BlockSpec((rows, width), lambda j, *_: (0, 0), pipeline_mode=once)
    return pl.pallas_call(
        functools.partial(ffn_kernel, len(pieces)),
        out_shape=[full, out, out, out, full],
        grid_spec=pltpu.PrefetchScalarGridSpec(
            num_scalar_prefetch=1,
            grid=(steps,),
            in_specs=[pl.BlockSpec(memory_space=pl.ANY)] * len(pieces)
            + [
                pl.BlockSpec((rows, width), lambda j, *_: (half, 0), pipeline_mode=once),
                pl.BlockSpec((width, step), lambda j, *_: (0, j)),
                pl.BlockSpec((width, step), lambda j, *_: (0, steps + j)),
                pl.BlockSpec((width, step), lambda j, *_: (0, 2 * steps + j)),
            ],
            out_specs=[whole]
            + [pl.BlockSpec((rows, step), lambda j, *_: (0, j))] * 3
            + [whole],
            scratch_shapes=[pltpu.VMEM((rows, width), WIDE), pltpu.SemaphoreType.DMA((order.shape[0],))],
        ),
        compiler_params=pltpu.CompilerParams(vmem_limit_bytes=60 * 2**20),
        cost_estimate=pl.CostEstimate(
            flops=10 * rows * width * hidden_width,
            bytes_accessed=6 * width * hidden_width,
            transcendentals=rows * hidden_width,
        ),
        name="feed_forward",
    )(order, *pieces, cotangent, weight, weight, weight)


def ffn_wgrad_kernel(steps, n_a, n_b, c_ref, gate_a, gate_b, up_a, up_b, hid_a, hid_b, out_ref, n_turned, c_turned):
    step = pl.program_id(0)
    half = n_a.shape[0]

    @pl.when(step == 0)
    def _():
        n_turned[:, :half] = jnp.transpose(n_a[...])
        n_turned[:, half:] = jnp.transpose(n_b[...])
        c_turned[...] = jnp.transpose(c_ref[...])

    def product(turned, first, second):
        out_ref[...] = (dot(turned[:, :half], first[...]) + dot(turned[:, half:], second[...])).astype(LOW)

    @pl.when(step < steps)
    def _():
        product(n_turned, gate_a, gate_b)

    @pl.when((step >= steps) & (step < 2 * steps))
    def _():
        product(n_turned, up_a, up_b)

    @pl.when(step >= 2 * steps)
    def _():
        product(c_turned, hid_a, hid_b)


def feed_forward_wgrad(normed, cotangent, gate_grad, up_grad, hidden):
    rows, width = cotangent.shape
    hidden_width = hidden[0].shape[1]
    step = min(512, hidden_width)
    steps = hidden_width // step
    once = pl.Buffered(1)

    def whole(count):
        return pl.BlockSpec((count, width), lambda j: (0, 0), pipeline_mode=once)

    def third(at):
        return pl.BlockSpec((rows // 2, step), lambda j: (0, jnp.clip(j - at * steps, 0, steps - 1)))

    return pl.pallas_call(
        functools.partial(ffn_wgrad_kernel, steps),
        out_shape=jax.ShapeDtypeStruct((width, 3 * hidden_width), LOW),
        grid=(3 * steps,),
        in_specs=[whole(rows // 2), whole(rows // 2), whole(rows)]
        + [third(0)] * 2
        + [third(1)] * 2
        + [third(2)] * 2,
        out_specs=pl.BlockSpec((width, step), lambda j: (0, j)),
        scratch_shapes=[pltpu.VMEM((width, rows), LOW), pltpu.VMEM((width, rows), LOW)],
        compiler_params=pltpu.CompilerParams(vmem_limit_bytes=60 * 2**20),
        cost_estimate=pl.CostEstimate(
            flops=rows * width,
            bytes_accessed=rows * width,
            transcendentals=0,
        ),
        name="feed_forward_wgrad",
    )(*normed, cotangent, *gate_grad, *up_grad, *hidden)


def adam_kernel(clip, grad, first, second, master, grad_out, first_out, second_out, new_out, low_out):
    gradient = grad[...].astype(WIDE) * clip[0]
    grad_out[...] = gradient
    first_new, second_new, master_new, low = adam_update(
        gradient, first[...], second[...], master[...], RATE
    )
    first_out[...] = first_new
    second_out[...] = second_new
    new_out[...] = master_new
    low_out[...] = low


def adam_arrays(clip_factor, grad, first, second, master):
    arrays, rows, columns = master.shape
    step = min(rows, max(16, 2**17 // columns))
    state = pl.BlockSpec((None, step, columns), lambda a, i, *_: (a, i, 0))
    wide = jax.ShapeDtypeStruct(master.shape, WIDE)
    return pl.pallas_call(
        adam_kernel,
        out_shape=[wide] * 4 + [jax.ShapeDtypeStruct(master.shape, LOW)],
        grid_spec=pltpu.PrefetchScalarGridSpec(
            num_scalar_prefetch=1,
            grid=(arrays, rows // step),
            in_specs=[pl.BlockSpec((step, columns), lambda a, i, *_: (i, a))] + [state] * 3,
            out_specs=[state] * 5,
        ),
        compiler_params=pltpu.CompilerParams(vmem_limit_bytes=32 * 2**20),
        cost_estimate=pl.CostEstimate(
            flops=20 * master.size, bytes_accessed=32 * master.size, transcendentals=2 * master.size
        ),
        name="adam",
    )(clip_factor.reshape(1), grad, first, second, master)


def slice_sum(terms):
    count = lax.axis_size("head")
    got = lax.all_to_all(terms, "head", split_axis=0, concat_axis=0, tiled=True)
    rows = terms.shape[0] // count
    return functools.reduce(
        lambda a, b: a + b, [got[j * rows : (j + 1) * rows].astype(WIDE) for j in range(count)]
    )


def added(*terms):
    return functools.reduce(lambda a, b: a + b, [t.astype(WIDE) for t in terms])


INWARD = [(0, 1), (3, 2)]
ACROSS = [(1, 2), (2, 1)]
OUTWARD = [(1, 0), (2, 3)]


def sum_step_one(terms):
    return (lax.ppermute(terms[3], "head", INWARD),)


def sum_step_two(terms, got):
    far = added(got[0], terms[3]).astype(LOW)
    return (lax.ppermute(terms[2], "head", INWARD), lax.ppermute(far, "head", ACROSS))


def sum_step_three(terms, got):
    middle = added(got[0], terms[2]).astype(LOW)
    far = added(got[1], terms[0]).astype(LOW)
    return (
        lax.ppermute(terms[1], "head", INWARD),
        lax.ppermute(middle, "head", ACROSS),
        lax.ppermute(far, "head", OUTWARD),
    )


def sum_last(terms, got):
    at = lax.axis_index("head")
    return jnp.where(
        (at == 0) | (at == 3), added(terms[0], got[2]), added(terms[1], got[0], got[1])
    )


def gather_step_one(piece):
    return (
        lax.ppermute(piece, "head", [(0, 1), (1, 2), (2, 3)]),
        lax.ppermute(piece, "head", [(3, 2), (2, 1), (1, 0)]),
    )


def gather_step_two(got):
    return (
        lax.ppermute(got[0], "head", [(1, 2), (2, 3)]),
        lax.ppermute(got[1], "head", [(2, 1), (1, 0)]),
    )


def gather_step_three(got):
    at = lax.axis_index("head")
    return (lax.ppermute(jnp.where(at == 2, got[0], got[1]), "head", [(2, 3), (1, 0)]),)


def gathered_pieces(piece, one, two, three):
    away = lax.axis_index("head") - jnp.arange(4, dtype=jnp.int32)
    order = jnp.where(
        away == 0, 0, jnp.where(jnp.abs(away) == 3, 5, jnp.where(away > 0, away, 2 - away))
    )
    return [piece, one[0], two[0], one[1], two[1], three[0]], order


def line_gather_pieces(piece):
    count = lax.axis_size("head")
    if count != 4:
        full = lax.all_gather(piece, "head", axis=0, tiled=True)
        return jnp.split(full, count, axis=0), jnp.arange(count, dtype=jnp.int32)
    one = gather_step_one(piece)
    two = gather_step_two(one)
    return gathered_pieces(piece, one, two, gather_step_three(two))


def line_gather_wide(full, piece, got):
    count = lax.axis_size("head")
    at = lax.axis_index("head")
    rows = piece.shape[1]
    if count != 4:
        every = lax.all_gather(piece, "head", axis=0, tiled=False).astype(WIDE)
        return every.transpose(1, 0, 2, 3).reshape(full.shape)
    one, two, three = got
    for where, part in (
        (at, piece),
        (at - 1, one[0]),
        (at + 1, one[1]),
        (at - 2, two[0]),
        (at + 2, two[1]),
        (jnp.where(at == 0, 3, jnp.where(at == 3, 0, at)), three[0]),
    ):
        there = (where >= 0) & (where < count) & (where != at)
        full = lax.dynamic_update_slice(
            full,
            jnp.where(there, part, piece).astype(WIDE),
            (0, jnp.where(there, where, at) * rows, 0),
        )
    return full


def group_exchange(blocks, parts):
    count = lax.axis_size("seq")
    return [blocks[0]] + [
        lax.ppermute(blocks[k], "seq", [(j, j ^ k) for j in range(count)]) for k in range(1, parts)
    ]


def direct_terms(terms):
    at = lax.axis_index("head")
    count = lax.axis_size("head")
    return [lax.dynamic_index_in_dim(terms, at, 1, False)] + [
        lax.ppermute(
            lax.dynamic_index_in_dim(terms, at ^ k, 1, False),
            "head",
            [(j, j ^ k) for j in range(count)],
        )
        for k in range(1, count)
    ]


def direct_gather(piece):
    at = lax.axis_index("head")
    count = lax.axis_size("head")
    full = jnp.zeros((count,) + piece.shape, piece.dtype)
    for k in range(count):
        term = piece if k == 0 else lax.ppermute(piece, "head", [(j, j ^ k) for j in range(count)])
        full = lax.dynamic_update_index_in_dim(full, term, at ^ k, 0)
    return full


def sum_everywhere(values):
    for axis in ("seq", "head"):
        count = lax.axis_size(axis)
        bit = 1
        while bit < count:
            values = values + lax.ppermute(values, axis, [(j, j ^ bit) for j in range(count)])
            bit *= 2
    return values


def after(value, *others):
    return lax.optimization_barrier((value,) + others)[0]


def adam_update(gradient, first_moment, second, master, step_rate):
    first_new = BETA1 * first_moment + (1.0 - BETA1) * gradient
    second_new = BETA2 * second + (1.0 - BETA2) * gradient * gradient
    first_hat = first_new / (1.0 - BETA1**STEP)
    second_hat = second_new / (1.0 - BETA2**STEP)
    master_new = master - step_rate * (
        first_hat / (jnp.sqrt(second_hat) + ADAM_EPS) + DECAY * master
    )
    return (first_new, second_new, master_new, master_new.astype(LOW))


def per_device(
    tokens,
    cotangent,
    seq_lengths,
    attn_master,
    ffn_master,
    gain_master,
    attn_first,
    attn_second,
    ffn_first,
    ffn_second,
    gain_first,
    gain_second,
):
    seq_count = lax.axis_size("seq")
    head_count = lax.axis_size("head")
    seq_index = lax.axis_index("seq")
    head_index = lax.axis_index("head")
    local_rows, width = tokens.shape
    total_rows = local_rows * seq_count
    head_width = attn_master.shape[2]
    hidden_width = ffn_master.shape[2]
    shard_rows = attn_master.shape[1]
    local_heads = head_width // HD
    parts = seq_count // local_heads
    block = local_rows // parts
    part = seq_index % parts
    slice_rows = local_rows // head_count
    sub = slice_rows // parts
    sizes = (seq_count, parts, block)
    half_parts = parts // 2
    half_rows = local_rows // 2
    quarter_rows = slice_rows // 2

    def own_slice(array):
        columns = array.shape[1]
        return lax.dynamic_slice_in_dim(
            array.reshape(parts, block, columns), head_index * sub, sub, 1
        ).reshape(slice_rows, columns)

    def halves(array):
        return array[: array.shape[0] // 2], array[array.shape[0] // 2 :]

    def by_slices(array):
        rows, columns = array.shape
        return (
            array.reshape(rows // half_rows, half_parts, head_count, sub, columns)
            .transpose(0, 2, 1, 3, 4)
            .reshape(rows, columns)
        )

    qkv_shard = (
        attn_master[:3]
        .astype(LOW)
        .reshape(3, shard_rows, local_heads, HD)
        .transpose(1, 2, 0, 3)
        .reshape(shard_rows, 3 * head_width)
    )
    ffn_shard_low = jnp.concatenate([ffn_master[0], ffn_master[1], ffn_master[2]], axis=1).astype(LOW)
    gain_values = lax.all_gather(gain_master.astype(LOW), "seq", axis=1, tiled=True).astype(WIDE)
    qkv_weight = lax.all_gather(qkv_shard, "seq", axis=0, tiled=True)
    out_rows = (
        direct_gather(attn_master[3].astype(LOW)).transpose(1, 0, 2).reshape(shard_rows, width)
    )

    ints, floats = attention_scalars(seq_lengths, total_rows, part)

    gain_values, out_rows = lax.optimization_barrier((gain_values, out_rows))
    residual = tokens.astype(WIDE)
    scale_one = lax.rsqrt(jnp.mean(residual * residual, axis=-1, keepdims=True) + EPS)
    normed_one = (residual * scale_one * gain_values[0]).astype(LOW)
    column = jnp.arange(3 * head_width, dtype=jnp.int32) % (3 * HD)
    column_factor = jnp.where(column < HD, QUERY_FACTOR, 1.0).astype(WIDE)
    projected = (dot(normed_one, qkv_weight) * column_factor).astype(LOW)

    sent = (
        projected.reshape(parts, block, local_heads, 3 * HD)
        .transpose(2, 0, 1, 3)
        .reshape(seq_count, block, 3 * HD)
    )
    out_weight = lax.all_gather(after(out_rows, sent), "seq", axis=0, tiled=True)
    qkv = lax.all_to_all(sent, "seq", split_axis=0, concat_axis=0, tiled=True)
    head_queries = qkv[:, :, :HD]
    own_key_values = qkv[:, :, HD:]
    key_values = group_exchange([own_key_values] * parts, parts)
    ffn_weight = lax.all_gather(after(ffn_shard_low, key_values[-1]), "seq", axis=0, tiled=True)
    mixed, mass = attention_forward(sizes, ints, floats, head_queries, key_values)

    everywhere = ("seq", "head")
    slices_out = lax.all_to_all(
        mixed.reshape(seq_count * head_count, sub, HD), everywhere, split_axis=0, concat_axis=0, tiled=True
    )
    heads_out = (
        slices_out.reshape(local_heads, parts, head_count, sub, HD)
        .transpose(1, 3, 2, 0, 4)
        .reshape(slice_rows, width)
    )
    mass_high = lax.reduce_precision(mass, 8, 7)
    mass_middle = lax.reduce_precision(mass - mass_high, 8, 7)
    mass_parts = jnp.stack([mass_high, mass_middle, mass - mass_high - mass_middle], axis=1).astype(LOW)
    mass_rows = block // HD
    mass_sent = jnp.pad(
        mass_parts.reshape(seq_count, mass_rows, 3 * HD), ((0, 0), (0, 16 - mass_rows), (0, 0))
    )

    attn_sum = dot(heads_out, out_weight, NT)
    resid_one = own_slice(tokens).astype(WIDE) + attn_sum
    scale_two = lax.rsqrt(jnp.mean(resid_one * resid_one, axis=-1, keepdims=True) + EPS)
    unit_two = resid_one * scale_two
    normed_slice = (unit_two * gain_values[1]).astype(LOW)
    cot_slices = by_slices(cotangent)
    first_slice, second_slice = halves(normed_slice)

    first_pieces, order = line_gather_pieces(first_slice)
    second_pieces, order = line_gather_pieces(second_slice)
    first_pieces[-1], *second_pieces = lax.optimization_barrier((first_pieces[-1], *second_pieces))
    normed_a, hidden_a, gate_a, up_a, two_a = feed_forward(
        first_pieces, order, cot_slices, 0, ffn_weight, hidden_width
    )
    second_pieces[-1] = after(second_pieces[-1], two_a)
    normed_b, hidden_b, gate_b, up_b, two_b = feed_forward(
        second_pieces, order, cot_slices, 1, ffn_weight, hidden_width
    )
    two_sum_a = slice_sum(two_a)
    two_sum_b = slice_sum(two_b)
    two_sum_a, hidden_a, hidden_b = lax.optimization_barrier((two_sum_a, hidden_a, hidden_b))
    ffn_raw = feed_forward_wgrad(
        (normed_a, normed_b), cot_slices, (gate_a, gate_b), (up_a, up_b), (hidden_a, hidden_b)
    )
    ffn_shard = lax.psum_scatter(ffn_raw, "seq", scatter_dimension=0, tiled=True)
    down_weight = ffn_weight[:, 2 * hidden_width :]
    def norm_grad(grad, unit, scale, gain, passed):
        inner = grad * gain
        return passed + scale * (inner - unit * jnp.mean(inner * unit, axis=-1, keepdims=True))

    two_sum_b = after(two_sum_b, ffn_raw)
    cot_own = own_slice(cotangent).astype(WIDE)
    resid_grads = [
        norm_grad(*args, gain_values[1], passed)
        for args, passed in zip(
            zip((two_sum_a, two_sum_b), halves(unit_two), halves(scale_two)), halves(cot_own)
        )
    ]
    branch_low = jnp.concatenate([r.astype(LOW) for r in resid_grads], axis=0)
    heads_grad = dot(branch_low, out_weight).astype(LOW)

    grads_sent = (
        heads_grad.reshape(parts, sub, head_count, local_heads, HD)
        .transpose(3, 0, 2, 1, 4)
        .reshape(seq_count * head_count, sub, HD)
    )
    head_grads = lax.all_to_all(
        grads_sent, everywhere, split_axis=0, concat_axis=0, tiled=True
    ).reshape(seq_count, block, HD)
    out_raw = dot(branch_low, heads_out, TN).astype(LOW)
    out_mine = lax.psum_scatter(out_raw, "seq", scatter_dimension=0, tiled=True)
    hidden_a, hidden_b, grads_sent = lax.optimization_barrier((hidden_a, hidden_b, grads_sent))
    ffn_part = jnp.stack(
        [dot(hidden_a, down_weight, NT).astype(LOW), dot(hidden_b, down_weight, NT).astype(LOW)]
    )
    ffn_terms = direct_terms(
        after(ffn_part, head_grads).reshape(2, head_count, quarter_rows, width)
    )
    early_terms, late_terms = ffn_terms[:3], ffn_terms[3:]
    q_grad, *kv_grads = attention_backward(sizes, ints, floats, head_queries, head_grads, key_values)
    kv_grads, early_terms = lax.optimization_barrier((kv_grads, early_terms))
    kv_terms = group_exchange(kv_grads, parts)
    kv_sum = functools.reduce(lambda a, b: a + b, [t.astype(WIDE) for t in kv_terms]).astype(LOW)
    returned = lax.all_to_all(
        jnp.concatenate([jnp.concatenate([q_grad, kv_sum], axis=2), mass_sent], axis=1),
        "seq",
        split_axis=0,
        concat_axis=0,
        tiled=True,
    )
    ffn_sum = added(*early_terms, *late_terms).reshape(slice_rows, width)
    layer_slice = (resid_one + ffn_sum).astype(LOW).reshape(parts, sub, width)
    line = head_count == 4
    layer_one = gather_step_one(layer_slice) if line else ()
    out_terms = (
        out_mine.reshape(shard_rows, head_count, head_width)
        .transpose(1, 0, 2)
        .reshape(head_count, out_mine.size // head_count // width, width)
    )
    returned, layer_one, out_terms = lax.optimization_barrier((returned, layer_one, out_terms))
    grads_back = returned[:, :block]
    mass_got = returned[:, block : block + mass_rows].astype(WIDE).reshape(local_heads, parts, 3, block)
    attn_mass = jnp.sum(mass_got, axis=2).reshape(local_heads, local_rows)
    qkv_grad = (
        grads_back.reshape(local_heads, parts, block, 3 * HD)
        .transpose(1, 2, 0, 3)
        .reshape(local_rows, 3 * head_width)
    )

    one_grad_part = dot(qkv_grad, qkv_weight, NT).astype(LOW).reshape(parts, head_count, sub, width)
    if line:
        forward = jnp.arange(4, dtype=jnp.int32)
        order = jnp.where(head_index < 2, forward, 3 - forward)
        terms = [
            jnp.concatenate(
                [
                    lax.dynamic_index_in_dim(one_grad_part, order[k], 1, False).reshape(
                        slice_rows, width
                    ),
                    lax.dynamic_index_in_dim(out_terms, order[k], 0, False),
                ],
                axis=0,
            )
            for k in range(4)
        ]
        got = sum_step_one(terms)
        layer_two = gather_step_two(layer_one)
        got, layer_two, terms, qkv_grad = lax.optimization_barrier((got, layer_two, terms, qkv_grad))
        got = sum_step_two(terms, got)
        layer_three = gather_step_three(layer_two)
        qkv_raw = dot(normed_one, qkv_grad, TN).astype(LOW)
        got, layer_three, terms, qkv_raw, ffn_shard = lax.optimization_barrier(
            (got, layer_three, terms, qkv_raw, ffn_shard)
        )
        got = sum_step_three(terms, got)
        got, layer_three = lax.optimization_barrier((got, layer_three))
        summed = sum_last(terms, got)
    else:
        layer_two = layer_three = ()
        qkv_raw = dot(normed_one, qkv_grad, TN).astype(LOW)
        summed = jnp.concatenate(
            [
                lax.psum_scatter(one_grad_part, "head", scatter_dimension=1, tiled=True).reshape(
                    slice_rows, width
                ),
                lax.psum_scatter(out_terms, "head", scatter_dimension=0, tiled=False),
            ],
            axis=0,
        ).astype(WIDE)
    qkv_mine = lax.psum_scatter(qkv_raw, "seq", scatter_dimension=0, tiled=True)
    normed_one_grad = summed[:slice_rows]
    out_own = summed[slice_rows:].astype(LOW).reshape(shard_rows, head_width)
    normed_one_grad = normed_one_grad.reshape(slice_rows, width)
    own_scale = own_slice(scale_one)
    unit_one = own_slice(tokens).astype(WIDE) * own_scale
    input_slice = norm_grad(
        normed_one_grad, unit_one, own_scale, gain_values[0], jnp.concatenate(resid_grads, axis=0)
    )
    input_slice = input_slice.astype(LOW).reshape(parts, sub, width)
    input_one = gather_step_one(input_slice) if line else ()
    input_two = gather_step_two(input_one) if line else ()
    own_gain = gain_master.astype(LOW).astype(WIDE)
    qkv_wide = qkv_mine.astype(WIDE)
    ffn_wide = ffn_shard.astype(WIDE)
    gain_two_term = (
        jnp.sum(
            ffn_shard_low[:, : 2 * hidden_width].astype(WIDE) * ffn_wide[:, : 2 * hidden_width], axis=1
        )
        / own_gain[1]
    )
    gain_one_term = jnp.sum(qkv_shard.astype(WIDE) * qkv_wide, axis=1) / own_gain[0]
    out_wide = out_own.astype(WIDE)
    squares = jnp.sum(ffn_wide * ffn_wide) + jnp.sum(out_wide * out_wide) + jnp.sum(qkv_wide * qkv_wide)
    row = jnp.arange(2 * seq_count + 8, dtype=jnp.int32)[:, None]
    small = jnp.where(
        row == seq_index,
        gain_one_term[None, :],
        jnp.where(
            row == seq_count + seq_index,
            gain_two_term[None, :],
            jnp.where(row == 2 * seq_count, squares / shard_rows, 0.0),
        ),
    )
    small = sum_everywhere(small)
    gain_all = small[: 2 * seq_count]
    gain_shard = jnp.stack(
        [
            lax.dynamic_index_in_dim(gain_all, seq_index, 0, False),
            lax.dynamic_index_in_dim(gain_all, seq_count + seq_index, 0, False),
        ]
    )
    grad_norm = jnp.sqrt(jnp.sum(small[2 * seq_count]) + jnp.sum(gain_all * gain_all))
    clip_factor = jnp.minimum(1.0, CLIP / (grad_norm + 1e-06))

    attn_grads = jnp.concatenate(
        [
            qkv_mine.reshape(shard_rows, local_heads, 3, HD)
            .transpose(0, 2, 1, 3)
            .reshape(shard_rows, 3 * head_width),
            out_own,
        ],
        axis=1,
    )
    input_two, clip_factor, attn_grads = lax.optimization_barrier((input_two, clip_factor, attn_grads))
    input_three = gather_step_three(input_two) if line else ()
    blank = jnp.zeros((parts, block, width), WIDE)
    layer_output = line_gather_wide(blank, layer_slice, (layer_one, layer_two, layer_three))
    layer_output = layer_output.reshape(local_rows, width)
    input_grad = line_gather_wide(blank, input_slice, (input_one, input_two, input_three))
    input_grad = input_grad.reshape(local_rows, width)
    gain_grad = gain_shard * clip_factor
    ffn_state = adam_arrays(clip_factor, ffn_shard, ffn_first, ffn_second, ffn_master)
    attn_state = adam_arrays(clip_factor, attn_grads, attn_first, attn_second, attn_master)
    gain_state = adam_update(gain_grad, gain_first, gain_second, gain_master, GAIN_RATE)
    return (
        layer_output,
        input_grad,
        attn_mass,
        grad_norm,
        attn_state[0],
        attn_state[1],
        attn_state[2],
        attn_state[3],
        attn_state[4],
        ffn_state[0],
        ffn_state[1],
        ffn_state[2],
        ffn_state[3],
        ffn_state[4],
        gain_grad,
        gain_state[0],
        gain_state[1],
        gain_state[2],
        gain_state[3],
    )


def solution(mesh):
    in_specs = (
        P("seq", None),
        P("seq", None),
        P(),
        P(None, "seq", "head"),
        P(None, "seq", "head"),
        P(None, "seq"),
        P(None, "seq", "head"),
        P(None, "seq", "head"),
        P(None, "seq", "head"),
        P(None, "seq", "head"),
        P(None, "seq"),
        P(None, "seq"),
    )
    out_specs = (
        P("seq", None),
        P("seq", None),
        P("head", "seq"),
        P(),
        P(None, "seq", "head"),
        P(None, "seq", "head"),
        P(None, "seq", "head"),
        P(None, "seq", "head"),
        P(None, "seq", "head"),
        P(None, "seq", "head"),
        P(None, "seq", "head"),
        P(None, "seq", "head"),
        P(None, "seq", "head"),
        P(None, "seq", "head"),
        P(None, "seq"),
        P(None, "seq"),
        P(None, "seq"),
        P(None, "seq"),
        P(None, "seq"),
    )
    return jax.shard_map(
        per_device, mesh=mesh, in_specs=in_specs, out_specs=out_specs, check_vma=False
    )
```

```python
import functools
import math

import jax
import jax.numpy as jnp
from jax import lax
from jax.experimental import pallas as pl
from jax.experimental.pallas import tpu as pltpu
from jax.sharding import PartitionSpec as P

HD = 128
STEP = 10


EPS = 1e-05
CLIP = 1.0
BETA1 = 0.5
BETA2 = 0.5
RATE = 0.03
GAIN_RATE = 0.3
DECAY = 0.1
ADAM_EPS = 1e-08

LOW = jnp.bfloat16
WIDE = jnp.float32
QUERY_FACTOR = -math.log2(math.e) / math.sqrt(HD)
FAR = 30000.0

NN = (((1,), (0,)), ((), ()))
NT = (((1,), (1,)), ((), ()))
TN = (((0,), (0,)), ((), ()))


def dot(left, right, dims=NN):
    return lax.dot_general(left, right, dims, preferred_element_type=WIDE)


def fill_key_columns(key_buf, sizes, cut):
    count, parts, block = sizes

    def step(at, _):
        place = at * block + lax.broadcasted_iota(jnp.int32, (block, HD), 0)
        lane = lax.broadcasted_iota(jnp.int32, (block, HD), 1)
        extra = jnp.where(lane < 3, 1.0, jnp.where((lane == 3) & (place < cut), FAR, 0.0))
        key_buf[pl.ds(pl.multiple_of(at * block, block), block), HD:] = extra.astype(LOW)
        return 0

    lax.fori_loop(0, count * parts, step, 0)


def query_columns(sizes, source, part, cut, floats):
    _, parts, block = sizes
    lane = lax.broadcasted_iota(jnp.int32, (block, HD), 1)
    place = (source * parts + part) * block + lax.broadcasted_iota(jnp.int32, (block, HD), 0)
    second = place >= cut

    def column(at):
        return jnp.where(second, floats[3 + at], floats[at])

    extra = jnp.where(
        lane == 0,
        column(0),
        jnp.where(
            lane == 1,
            column(1),
            jnp.where(lane == 2, column(2), jnp.where((lane == 3) & second, 1.0, 0.0)),
        ),
    )
    return extra.astype(LOW)


def in_causal_order(sizes, part, shape, key_dim, first_key=0):
    key_place = first_key + lax.broadcasted_iota(jnp.int32, shape, key_dim)
    query_place = part * sizes[2] + lax.broadcasted_iota(jnp.int32, shape, 1 - key_dim)
    return key_place <= query_place


def key_copies(sizes, part, key_values, key_buf, value_buf, sem):
    count, parts, block = sizes
    for other in range(parts):
        for at in range(count):
            row = pl.multiple_of((at * parts + (part ^ other)) * block, block)
            yield pltpu.make_async_copy(
                key_values[other].at[at, :, 0:HD], key_buf.at[pl.ds(row, block), 0:HD], sem.at[0]
            )
            yield pltpu.make_async_copy(
                key_values[other].at[at, :, HD:], value_buf.at[pl.ds(row, block), 0:HD], sem.at[0]
            )


def forward_kernel(sizes, ints, floats, q_ref, *rest):
    count, parts, block = sizes
    tile = block * parts
    key_values = rest[:parts]
    out_ref, mass_ref, key_buf, value_buf, query_buf, total, sem = rest[parts:]
    step = pl.program_id(0)
    cut, part = ints[0], ints[1]

    @pl.when(step == 0)
    def _():
        for copy in key_copies(sizes, part, key_values, key_buf, value_buf, sem):
            copy.start()
        fill_key_columns(key_buf, sizes, cut)
        value_buf[:, HD:] = jnp.ones((count * tile, HD), LOW)
        for copy in key_copies(sizes, part, key_values, key_buf, value_buf, sem):
            copy.wait()

    query_buf[:, :HD] = q_ref[...]
    query_buf[:, HD:] = query_columns(sizes, step, part, cut, floats)
    total[...] = jnp.zeros_like(total)
    first = jnp.where(step * tile >= cut, cut // tile, 0)

    def walk(at, masked):
        keys = pl.ds(pl.multiple_of(at * tile, tile), tile)
        exponent = dot(query_buf[...], key_buf[keys, :], NT)
        weight = pl.reciprocal(1.0 + jnp.exp2(exponent), approx=True)
        if masked:
            weight = jnp.where(in_causal_order(sizes, part, (block, tile), 1), weight, 0.0)
        total[...] += dot(weight.astype(LOW), value_buf[keys, :])

    def body(at, carry):
        walk(at, False)
        return carry

    lax.fori_loop(first, step, body, 0)
    walk(step, True)
    out_ref[...] = total[:, :HD].astype(LOW)
    mass_ref[...] = jnp.transpose(total[:, HD:])[0:1, :]


def attention_forward(sizes, ints, floats, queries, key_values):
    count, parts, block = sizes
    total_rows = count * parts * block
    pairs = total_rows * total_rows // (2 * parts)
    return pl.pallas_call(
        functools.partial(forward_kernel, sizes),
        out_shape=[
            jax.ShapeDtypeStruct((count, block, HD), LOW),
            jax.ShapeDtypeStruct((count, 1, block), WIDE),
        ],
        grid_spec=pltpu.PrefetchScalarGridSpec(
            num_scalar_prefetch=2,
            grid=(count,),
            in_specs=[pl.BlockSpec((None, block, HD), lambda i, *_: (i, 0, 0))]
            + [pl.BlockSpec(memory_space=pl.ANY)] * parts,
            out_specs=[
                pl.BlockSpec((None, block, HD), lambda i, *_: (i, 0, 0)),
                pl.BlockSpec((None, 1, block), lambda i, *_: (i, 0, 0)),
            ],
            scratch_shapes=[
                pltpu.VMEM((total_rows, 2 * HD), LOW),
                pltpu.VMEM((total_rows, 2 * HD), LOW),
                pltpu.VMEM((block, 2 * HD), LOW),
                pltpu.VMEM((block, 2 * HD), WIDE),
                pltpu.SemaphoreType.DMA((1,)),
            ],
        ),
        compiler_params=pltpu.CompilerParams(vmem_limit_bytes=48 * 2**20),
        cost_estimate=pl.CostEstimate(
            flops=pairs * 8 * HD, bytes_accessed=total_rows * HD * 8, transcendentals=2 * pairs
        ),
        name="attention_forward",
    )(ints, floats, queries, *key_values)


def backward_kernel(sizes, ints, floats, q_ref, grad_ref, *rest):
    count, parts, block = sizes
    tile = block * parts
    chunk = min(256, tile)
    key_values = rest[:parts]
    q_grad_ref, *kv_grad_refs = rest[parts : 2 * parts + 1]
    key_buf, value_buf, query_buf, q_turned, grad_turned, q_total, k_total, v_total, sem = rest[
        2 * parts + 1 :
    ]
    step = pl.program_id(0)
    cut, part = ints[0], ints[1]

    @pl.when(step == 0)
    def _():
        for copy in key_copies(sizes, part, key_values, key_buf, value_buf, sem):
            copy.start()
        fill_key_columns(key_buf, sizes, cut)
        k_total[...] = jnp.zeros_like(k_total)
        v_total[...] = jnp.zeros_like(v_total)
        for copy in key_copies(sizes, part, key_values, key_buf, value_buf, sem):
            copy.wait()

    query_buf[:, :HD] = q_ref[...]
    query_buf[:, HD:] = query_columns(sizes, step, part, cut, floats)
    q_turned[...] = jnp.transpose(q_ref[...])
    grad_turned[...] = jnp.transpose(grad_ref[...])
    q_total[...] = jnp.zeros_like(q_total)
    first = jnp.where(step * tile >= cut, cut // tile, 0)

    def walk(at, masked):
        base = pl.multiple_of(at * tile, tile)

        def products(place):
            keys = pl.ds(base + place, chunk)
            return (
                dot(query_buf[...], key_buf[keys, :], NT),
                dot(grad_ref[...], value_buf[keys, :], NT),
            )

        score_grads = []
        following = products(0)
        for place in range(0, tile, chunk):
            exponent, weight_grad = following
            if place + chunk < tile:
                following = products(place + chunk)
            weight = pl.reciprocal(1.0 + jnp.exp2(exponent), approx=True)
            if masked:
                weight = jnp.where(
                    in_causal_order(sizes, part, (block, chunk), 1, place), weight, 0.0
                )
            score_grad = (weight_grad * (weight - weight * weight)).astype(LOW)
            keys = pl.ds(base + place, chunk)
            v_total[:, keys] += dot(grad_turned[...], weight.astype(LOW))
            k_total[:, keys] += dot(q_turned[...], score_grad)
            score_grads.append(score_grad)
        q_total[...] += dot(
            jnp.concatenate(score_grads, axis=1), key_buf[pl.ds(base, tile), :HD]
        )

    def body(at, carry):
        walk(at, False)
        return carry

    lax.fori_loop(first, step, body, 0)
    walk(step, True)
    q_grad_ref[...] = (q_total[...] * (1.0 / math.sqrt(HD))).astype(LOW)

    @pl.when(step == count - 1)
    def _():
        for other in range(parts):
            for at in range(count):
                row = pl.multiple_of((at * parts + (part ^ other)) * block, block)
                rows = pl.ds(row, block)
                kv_grad_refs[other][at, :, :HD] = jnp.transpose(
                    k_total[:, rows] * (-math.log(2.0))
                ).astype(LOW)
                kv_grad_refs[other][at, :, HD:] = jnp.transpose(v_total[:, rows]).astype(LOW)


def attention_backward(sizes, ints, floats, queries, grads, key_values):
    count, parts, block = sizes
    total_rows = count * parts * block
    pairs = total_rows * total_rows // (2 * parts)
    return pl.pallas_call(
        functools.partial(backward_kernel, sizes),
        out_shape=[
            jax.ShapeDtypeStruct((count, block, HD), LOW),
        ]
        + [jax.ShapeDtypeStruct((count, block, 2 * HD), LOW)] * parts,
        grid_spec=pltpu.PrefetchScalarGridSpec(
            num_scalar_prefetch=2,
            grid=(count,),
            in_specs=[pl.BlockSpec((None, block, HD), lambda i, *_: (i, 0, 0))] * 2
            + [pl.BlockSpec(memory_space=pl.ANY)] * parts,
            out_specs=[
                pl.BlockSpec((None, block, HD), lambda i, *_: (i, 0, 0)),
            ]
            + [pl.BlockSpec((count, block, 2 * HD), lambda i, *_: (0, 0, 0))] * parts,
            scratch_shapes=[
                pltpu.VMEM((total_rows, 2 * HD), LOW),
                pltpu.VMEM((total_rows, HD), LOW),
                pltpu.VMEM((block, 2 * HD), LOW),
                pltpu.VMEM((HD, block), LOW),
                pltpu.VMEM((HD, block), LOW),
                pltpu.VMEM((block, HD), WIDE),
                pltpu.VMEM((HD, total_rows), WIDE),
                pltpu.VMEM((HD, total_rows), WIDE),
                pltpu.SemaphoreType.DMA((1,)),
            ],
        ),
        compiler_params=pltpu.CompilerParams(vmem_limit_bytes=60 * 2**20),
        cost_estimate=pl.CostEstimate(
            flops=pairs * 100 * HD, bytes_accessed=total_rows * HD * 16, transcendentals=2 * pairs
        ),
        name="attention_backward",
    )(ints, floats, queries, grads, *key_values)


def attention_scalars(seq_lengths, total_rows, part):
    cut = seq_lengths[0]
    length = jnp.log2(jnp.stack([cut, total_rows - cut]).astype(WIDE))
    high = lax.reduce_precision(length, 8, 7)
    middle = lax.reduce_precision(length - high, 8, 7)
    low = length - high - middle
    return (
        jnp.stack([cut, part]).astype(jnp.int32),
        jnp.stack([high, middle, low], axis=1).reshape(6),
    )


def projection_kernel(n_ref, w_ref, out_ref):
    heads, parts, block, columns = out_ref.shape
    lane = lax.broadcasted_iota(jnp.int32, (1, columns), 1)
    factor = jnp.where(lane < HD, QUERY_FACTOR, 1.0)
    for part in range(parts):
        rows = pl.ds(part * block, block)
        result = dot(n_ref[rows, :], w_ref[...])
        for head in range(heads):
            out_ref[head, part] = (
                result[:, head * columns : (head + 1) * columns] * factor
            ).astype(LOW)


def project(normed, weight, local_heads, parts):
    rows, width = normed.shape
    columns = 3 * HD
    heads = 2
    return pl.pallas_call(
        projection_kernel,
        out_shape=jax.ShapeDtypeStruct((local_heads, parts, rows // parts, columns), LOW),
        grid=(local_heads // heads,),
        in_specs=[
            pl.BlockSpec((rows, width), lambda j: (0, 0), pipeline_mode=pl.Buffered(1)),
            pl.BlockSpec((width, heads * columns), lambda j: (0, j)),
        ],
        out_specs=pl.BlockSpec((heads, parts, rows // parts, columns), lambda j: (j, 0, 0, 0)),
        compiler_params=pltpu.CompilerParams(vmem_limit_bytes=56 * 2**20),
        cost_estimate=pl.CostEstimate(
            flops=2 * rows * width * local_heads * columns,
            bytes_accessed=2 * (rows * width + (rows + width) * local_heads * columns),
            transcendentals=0,
        ),
        name="projection",
    )(normed, weight)


def ffn_kernel(pieces, table, *refs):
    given = refs[:pieces]
    c_ref, gate_w, up_w, down_w = refs[pieces : pieces + 4]
    normed_ref, hidden_ref, gate_ref, up_ref, two_ref, total, sem = refs[pieces + 4 :]
    step = pl.program_id(0)
    rows = normed_ref.shape[0]
    slots = table.shape[0]
    slot_rows = rows // slots

    @pl.when(step == 0)
    def _():
        def each(act):
            for slot in range(slots):
                for piece in range(pieces):

                    @pl.when(table[slot] == piece)
                    def _(slot=slot, piece=piece):
                        act(
                            pltpu.make_async_copy(
                                given[piece],
                                normed_ref.at[pl.ds(slot * slot_rows, slot_rows), :],
                                sem.at[slot],
                            )
                        )

        each(lambda copy: copy.start())
        total[...] = jnp.zeros_like(total)
        each(lambda copy: copy.wait())

    chunk = min(512, rows)
    for at in range(0, rows, chunk):
        here = pl.ds(at, chunk)
        gate = dot(normed_ref[here, :], gate_w[...])
        up = dot(normed_ref[here, :], up_w[...])
        grad = dot(c_ref[here, :], down_w[...])
        sig = 1.0 / (1.0 + jnp.exp(-gate))
        silu = gate * sig
        hidden_ref[here, :] = (silu * up).astype(LOW)
        gate_grad = (grad * up * (sig + silu * (1.0 - sig))).astype(LOW)
        up_grad = (grad * silu).astype(LOW)
        gate_ref[here, :] = gate_grad
        up_ref[here, :] = up_grad
        total[here, :] += dot(gate_grad, gate_w[...], NT) + dot(up_grad, up_w[...], NT)

    @pl.when(step == pl.num_programs(0) - 1)
    def _():
        two_ref[...] = total[...].astype(LOW)


def feed_forward(pieces, order, cotangent, half, weight, hidden_width):
    rows, width = cotangent.shape[0] // 2, cotangent.shape[1]
    step = min(512, hidden_width)
    steps = hidden_width // step
    out = jax.ShapeDtypeStruct((rows, hidden_width), LOW)
    full = jax.ShapeDtypeStruct((rows, width), LOW)
    once = pl.Buffered(1)
    whole = pl.BlockSpec((rows, width), lambda j, *_: (0, 0), pipeline_mode=once)
    return pl.pallas_call(
        functools.partial(ffn_kernel, len(pieces)),
        out_shape=[full, out, out, out, full],
        grid_spec=pltpu.PrefetchScalarGridSpec(
            num_scalar_prefetch=1,
            grid=(steps,),
            in_specs=[pl.BlockSpec(memory_space=pl.ANY)] * len(pieces)
            + [
                pl.BlockSpec((rows, width), lambda j, *_: (half, 0), pipeline_mode=once),
                pl.BlockSpec((width, step), lambda j, *_: (0, j)),
                pl.BlockSpec((width, step), lambda j, *_: (0, steps + j)),
                pl.BlockSpec((width, step), lambda j, *_: (0, 2 * steps + j)),
            ],
            out_specs=[whole]
            + [pl.BlockSpec((rows, step), lambda j, *_: (0, j))] * 3
            + [whole],
            scratch_shapes=[pltpu.VMEM((rows, width), WIDE), pltpu.SemaphoreType.DMA((order.shape[0],))],
        ),
        compiler_params=pltpu.CompilerParams(vmem_limit_bytes=60 * 2**20),
        cost_estimate=pl.CostEstimate(
            flops=10 * rows * width * hidden_width,
            bytes_accessed=6 * width * hidden_width,
            transcendentals=rows * hidden_width,
        ),
        name="feed_forward",
    )(order, *pieces, cotangent, weight, weight, weight)


def ffn_wgrad_kernel(steps, n_a, n_b, c_ref, gate_a, gate_b, up_a, up_b, hid_a, hid_b, out_ref, n_turned, c_turned):
    step = pl.program_id(0)
    half = n_a.shape[0]

    @pl.when(step == 0)
    def _():
        n_turned[:, :half] = jnp.transpose(n_a[...])
        n_turned[:, half:] = jnp.transpose(n_b[...])
        c_turned[...] = jnp.transpose(c_ref[...])

    def product(turned, first, second):
        out_ref[...] = (dot(turned[:, :half], first[...]) + dot(turned[:, half:], second[...])).astype(LOW)

    @pl.when(step < steps)
    def _():
        product(n_turned, gate_a, gate_b)

    @pl.when((step >= steps) & (step < 2 * steps))
    def _():
        product(n_turned, up_a, up_b)

    @pl.when(step >= 2 * steps)
    def _():
        product(c_turned, hid_a, hid_b)


def feed_forward_wgrad(normed, cotangent, gate_grad, up_grad, hidden):
    rows, width = cotangent.shape
    hidden_width = hidden[0].shape[1]
    step = min(512, hidden_width)
    steps = hidden_width // step
    once = pl.Buffered(1)

    def whole(count):
        return pl.BlockSpec((count, width), lambda j: (0, 0), pipeline_mode=once)

    def third(at):
        return pl.BlockSpec((rows // 2, step), lambda j: (0, jnp.clip(j - at * steps, 0, steps - 1)))

    return pl.pallas_call(
        functools.partial(ffn_wgrad_kernel, steps),
        out_shape=jax.ShapeDtypeStruct((width, 3 * hidden_width), LOW),
        grid=(3 * steps,),
        in_specs=[whole(rows // 2), whole(rows // 2), whole(rows)]
        + [third(0)] * 2
        + [third(1)] * 2
        + [third(2)] * 2,
        out_specs=pl.BlockSpec((width, step), lambda j: (0, j)),
        scratch_shapes=[pltpu.VMEM((width, rows), LOW), pltpu.VMEM((width, rows), LOW)],
        compiler_params=pltpu.CompilerParams(vmem_limit_bytes=60 * 2**20),
        cost_estimate=pl.CostEstimate(
            flops=rows * width,
            bytes_accessed=rows * width,
            transcendentals=0,
        ),
        name="feed_forward_wgrad",
    )(*normed, cotangent, *gate_grad, *up_grad, *hidden)


def adam_kernel(clip, grad, first, second, master, grad_out, first_out, second_out, new_out, low_out):
    gradient = grad[...].astype(WIDE) * clip[0]
    grad_out[...] = gradient
    first_new, second_new, master_new, low = adam_update(
        gradient, first[...], second[...], master[...], RATE
    )
    first_out[...] = first_new
    second_out[...] = second_new
    new_out[...] = master_new
    low_out[...] = low


def adam_arrays(clip_factor, grad, first, second, master):
    arrays, rows, columns = master.shape
    step = min(rows, max(16, 2**17 // columns))
    state = pl.BlockSpec((None, step, columns), lambda a, i, *_: (a, i, 0))
    wide = jax.ShapeDtypeStruct(master.shape, WIDE)
    return pl.pallas_call(
        adam_kernel,
        out_shape=[wide] * 4 + [jax.ShapeDtypeStruct(master.shape, LOW)],
        grid_spec=pltpu.PrefetchScalarGridSpec(
            num_scalar_prefetch=1,
            grid=(arrays, rows // step),
            in_specs=[pl.BlockSpec((step, columns), lambda a, i, *_: (i, a))] + [state] * 3,
            out_specs=[state] * 5,
        ),
        compiler_params=pltpu.CompilerParams(vmem_limit_bytes=32 * 2**20),
        cost_estimate=pl.CostEstimate(
            flops=20 * master.size, bytes_accessed=32 * master.size, transcendentals=2 * master.size
        ),
        name="adam",
    )(clip_factor.reshape(1), grad, first, second, master)


def slice_sum(terms):
    count = lax.axis_size("head")
    got = lax.all_to_all(terms, "head", split_axis=0, concat_axis=0, tiled=True)
    rows = terms.shape[0] // count
    return functools.reduce(
        lambda a, b: a + b, [got[j * rows : (j + 1) * rows].astype(WIDE) for j in range(count)]
    )


def added(*terms):
    return functools.reduce(lambda a, b: a + b, [t.astype(WIDE) for t in terms])


INWARD = [(0, 1), (3, 2)]
ACROSS = [(1, 2), (2, 1)]
OUTWARD = [(1, 0), (2, 3)]


def sum_step_one(terms):
    return (lax.ppermute(terms[3], "head", INWARD),)


def sum_step_two(terms, got):
    far = added(got[0], terms[3]).astype(LOW)
    return (lax.ppermute(terms[2], "head", INWARD), lax.ppermute(far, "head", ACROSS))


def sum_step_three(terms, got):
    middle = added(got[0], terms[2]).astype(LOW)
    far = added(got[1], terms[0]).astype(LOW)
    return (
        lax.ppermute(terms[1], "head", INWARD),
        lax.ppermute(middle, "head", ACROSS),
        lax.ppermute(far, "head", OUTWARD),
    )


def sum_last(terms, got):
    at = lax.axis_index("head")
    return jnp.where(
        (at == 0) | (at == 3), added(terms[0], got[2]), added(terms[1], got[0], got[1])
    )


def gather_step_one(piece):
    return (
        lax.ppermute(piece, "head", [(0, 1), (1, 2), (2, 3)]),
        lax.ppermute(piece, "head", [(3, 2), (2, 1), (1, 0)]),
    )


def gather_step_two(got):
    return (
        lax.ppermute(got[0], "head", [(1, 2), (2, 3)]),
        lax.ppermute(got[1], "head", [(2, 1), (1, 0)]),
    )


def gather_step_three(got):
    at = lax.axis_index("head")
    return (lax.ppermute(jnp.where(at == 2, got[0], got[1]), "head", [(2, 3), (1, 0)]),)


def gathered_pieces(piece, one, two, three):
    away = lax.axis_index("head") - jnp.arange(4, dtype=jnp.int32)
    order = jnp.where(
        away == 0, 0, jnp.where(jnp.abs(away) == 3, 5, jnp.where(away > 0, away, 2 - away))
    )
    return [piece, one[0], two[0], one[1], two[1], three[0]], order


def line_gather_pieces(piece):
    count = lax.axis_size("head")
    if count != 4:
        full = lax.all_gather(piece, "head", axis=0, tiled=True)
        return jnp.split(full, count, axis=0), jnp.arange(count, dtype=jnp.int32)
    one = gather_step_one(piece)
    two = gather_step_two(one)
    return gathered_pieces(piece, one, two, gather_step_three(two))


def line_gather_wide(full, piece, got):
    count = lax.axis_size("head")
    at = lax.axis_index("head")
    rows = piece.shape[1]
    if count != 4:
        every = lax.all_gather(piece, "head", axis=0, tiled=False).astype(WIDE)
        return every.transpose(1, 0, 2, 3).reshape(full.shape)
    one, two, three = got
    for where, part in (
        (at, piece),
        (at - 1, one[0]),
        (at + 1, one[1]),
        (at - 2, two[0]),
        (at + 2, two[1]),
        (jnp.where(at == 0, 3, jnp.where(at == 3, 0, at)), three[0]),
    ):
        there = (where >= 0) & (where < count) & (where != at)
        full = lax.dynamic_update_slice(
            full,
            jnp.where(there, part, piece).astype(WIDE),
            (0, jnp.where(there, where, at) * rows, 0),
        )
    return full


def group_exchange(blocks, parts):
    count = lax.axis_size("seq")
    return [blocks[0]] + [
        lax.ppermute(blocks[k], "seq", [(j, j ^ k) for j in range(count)]) for k in range(1, parts)
    ]


def direct_terms(terms):
    count = lax.axis_size("head")
    return terms[:1] + [
        lax.ppermute(terms[k], "head", [(j, j ^ k) for j in range(count)]) for k in range(1, count)
    ]


def direct_gather(piece):
    at = lax.axis_index("head")
    count = lax.axis_size("head")
    full = jnp.zeros((count,) + piece.shape, piece.dtype)
    for k in range(count):
        term = piece if k == 0 else lax.ppermute(piece, "head", [(j, j ^ k) for j in range(count)])
        full = lax.dynamic_update_index_in_dim(full, term, at ^ k, 0)
    return full


def sum_everywhere(values):
    for axis in ("seq", "head"):
        count = lax.axis_size(axis)
        bit = 1
        while bit < count:
            values = values + lax.ppermute(values, axis, [(j, j ^ bit) for j in range(count)])
            bit *= 2
    return values


def after(value, *others):
    return lax.optimization_barrier((value,) + others)[0]


def adam_update(gradient, first_moment, second, master, step_rate):
    first_new = BETA1 * first_moment + (1.0 - BETA1) * gradient
    second_new = BETA2 * second + (1.0 - BETA2) * gradient * gradient
    first_hat = first_new / (1.0 - BETA1**STEP)
    second_hat = second_new / (1.0 - BETA2**STEP)
    master_new = master - step_rate * (
        first_hat / (jnp.sqrt(second_hat) + ADAM_EPS) + DECAY * master
    )
    return (first_new, second_new, master_new, master_new.astype(LOW))


def per_device(
    tokens,
    cotangent,
    seq_lengths,
    attn_master,
    ffn_master,
    gain_master,
    attn_first,
    attn_second,
    ffn_first,
    ffn_second,
    gain_first,
    gain_second,
):
    seq_count = lax.axis_size("seq")
    head_count = lax.axis_size("head")
    seq_index = lax.axis_index("seq")
    head_index = lax.axis_index("head")
    local_rows, width = tokens.shape
    total_rows = local_rows * seq_count
    head_width = attn_master.shape[2]
    hidden_width = ffn_master.shape[2]
    shard_rows = attn_master.shape[1]
    local_heads = head_width // HD
    parts = seq_count // local_heads
    block = local_rows // parts
    part = seq_index % parts
    slice_rows = local_rows // head_count
    sub = slice_rows // parts
    sizes = (seq_count, parts, block)
    half_parts = parts // 2
    half_rows = local_rows // 2
    quarter_rows = slice_rows // 2

    def own_slice(array):
        columns = array.shape[1]
        return lax.dynamic_slice_in_dim(
            array.reshape(parts, block, columns), head_index * sub, sub, 1
        ).reshape(slice_rows, columns)

    def halves(array):
        return array[: array.shape[0] // 2], array[array.shape[0] // 2 :]

    def by_slices(array):
        rows, columns = array.shape
        return (
            array.reshape(rows // half_rows, half_parts, head_count, sub, columns)
            .transpose(0, 2, 1, 3, 4)
            .reshape(rows, columns)
        )

    qkv_shard = (
        attn_master[:3]
        .astype(LOW)
        .reshape(3, shard_rows, local_heads, HD)
        .transpose(1, 2, 0, 3)
        .reshape(shard_rows, 3 * head_width)
    )
    ffn_shard_low = jnp.concatenate([ffn_master[0], ffn_master[1], ffn_master[2]], axis=1).astype(LOW)
    gain_values = lax.all_gather(gain_master.astype(LOW), "seq", axis=1, tiled=True).astype(WIDE)
    qkv_weight = lax.all_gather(qkv_shard, "seq", axis=0, tiled=True)
    out_rows = (
        direct_gather(attn_master[3].astype(LOW)).transpose(1, 0, 2).reshape(shard_rows, width)
    )

    ints, floats = attention_scalars(seq_lengths, total_rows, part)

    gain_values, out_rows, ffn_shard_low = lax.optimization_barrier(
        (gain_values, out_rows, ffn_shard_low)
    )
    residual = tokens.astype(WIDE)
    scale_one = lax.rsqrt(jnp.mean(residual * residual, axis=-1, keepdims=True) + EPS)
    normed_one = (residual * scale_one * gain_values[0]).astype(LOW)
    sent = project(normed_one, qkv_weight, local_heads, parts).reshape(seq_count, block, 3 * HD)
    out_weight = lax.all_gather(after(out_rows, sent), "seq", axis=0, tiled=True)
    qkv = lax.all_to_all(sent, "seq", split_axis=0, concat_axis=0, tiled=True)
    head_queries = qkv[:, :, :HD]
    own_key_values = qkv[:, :, HD:]
    key_values = group_exchange([own_key_values] * parts, parts)
    ffn_weight = lax.all_gather(after(ffn_shard_low, key_values[-1]), "seq", axis=0, tiled=True)
    mixed, mass = attention_forward(sizes, ints, floats, head_queries, key_values)

    everywhere = ("seq", "head")
    slices_out = lax.all_to_all(
        mixed.reshape(seq_count * head_count, sub, HD), everywhere, split_axis=0, concat_axis=0, tiled=True
    )
    heads_out = (
        slices_out.reshape(local_heads, parts, head_count, sub, HD)
        .transpose(1, 3, 2, 0, 4)
        .reshape(slice_rows, width)
    )
    mass_high = lax.reduce_precision(mass, 8, 7)
    mass_middle = lax.reduce_precision(mass - mass_high, 8, 7)
    mass_parts = jnp.stack([mass_high, mass_middle, mass - mass_high - mass_middle], axis=1).astype(LOW)
    mass_rows = block // HD
    mass_sent = jnp.pad(
        mass_parts.reshape(seq_count, mass_rows, 3 * HD), ((0, 0), (0, 16 - mass_rows), (0, 0))
    )

    attn_sum = dot(heads_out, out_weight, NT)
    resid_one = own_slice(tokens).astype(WIDE) + attn_sum
    scale_two = lax.rsqrt(jnp.mean(resid_one * resid_one, axis=-1, keepdims=True) + EPS)
    unit_two = resid_one * scale_two
    normed_slice = (unit_two * gain_values[1]).astype(LOW)
    cot_slices = by_slices(cotangent)
    first_slice, second_slice = halves(normed_slice)

    first_pieces, order = line_gather_pieces(first_slice)
    second_pieces, order = line_gather_pieces(second_slice)
    first_pieces[-1], *second_pieces = lax.optimization_barrier((first_pieces[-1], *second_pieces))
    normed_a, hidden_a, gate_a, up_a, two_a = feed_forward(
        first_pieces, order, cot_slices, 0, ffn_weight, hidden_width
    )
    second_pieces[-1] = after(second_pieces[-1], two_a)
    normed_b, hidden_b, gate_b, up_b, two_b = feed_forward(
        second_pieces, order, cot_slices, 1, ffn_weight, hidden_width
    )
    two_sum_a = slice_sum(two_a)
    two_sum_b = slice_sum(two_b)
    two_sum_a, hidden_a, hidden_b = lax.optimization_barrier((two_sum_a, hidden_a, hidden_b))
    ffn_raw = feed_forward_wgrad(
        (normed_a, normed_b), cot_slices, (gate_a, gate_b), (up_a, up_b), (hidden_a, hidden_b)
    )
    ffn_shard = lax.psum_scatter(ffn_raw, "seq", scatter_dimension=0, tiled=True)
    down_weight = ffn_weight[:, 2 * hidden_width :]
    def norm_grad(grad, unit, scale, gain, passed):
        inner = grad * gain
        return passed + scale * (inner - unit * jnp.mean(inner * unit, axis=-1, keepdims=True))

    two_sum_b = after(two_sum_b, ffn_raw)
    cot_own = own_slice(cotangent).astype(WIDE)
    resid_grads = [
        norm_grad(*args, gain_values[1], passed)
        for args, passed in zip(
            zip((two_sum_a, two_sum_b), halves(unit_two), halves(scale_two)), halves(cot_own)
        )
    ]
    branch_low = jnp.concatenate([r.astype(LOW) for r in resid_grads], axis=0)
    heads_grad = dot(branch_low, out_weight).astype(LOW)

    grads_sent = (
        heads_grad.reshape(parts, sub, head_count, local_heads, HD)
        .transpose(3, 0, 2, 1, 4)
        .reshape(seq_count * head_count, sub, HD)
    )
    head_grads = lax.all_to_all(
        grads_sent, everywhere, split_axis=0, concat_axis=0, tiled=True
    ).reshape(seq_count, block, HD)
    out_raw = dot(branch_low, heads_out, TN).astype(LOW)
    out_mine = lax.psum_scatter(out_raw, "seq", scatter_dimension=0, tiled=True)
    hidden_a, hidden_b, grads_sent = lax.optimization_barrier((hidden_a, hidden_b, grads_sent))
    ffn_part = jnp.stack(
        [dot(hidden_a, down_weight, NT).astype(LOW), dot(hidden_b, down_weight, NT).astype(LOW)]
    )
    ffn_part = ffn_part.reshape(2, head_count, quarter_rows, width)
    ffn_terms = [
        lax.dynamic_index_in_dim(ffn_part, head_index ^ k, 1, False) for k in range(head_count)
    ]
    ffn_terms, head_grads = lax.optimization_barrier((ffn_terms, head_grads))
    ffn_terms = direct_terms(ffn_terms)
    early_terms, late_terms = ffn_terms[:3], ffn_terms[3:]
    q_grad, *kv_grads = attention_backward(sizes, ints, floats, head_queries, head_grads, key_values)
    kv_grads, early_terms = lax.optimization_barrier((kv_grads, early_terms))
    kv_terms = group_exchange(kv_grads, parts)
    kv_sum = functools.reduce(lambda a, b: a + b, [t.astype(WIDE) for t in kv_terms]).astype(LOW)
    returned = lax.all_to_all(
        jnp.concatenate([jnp.concatenate([q_grad, kv_sum], axis=2), mass_sent], axis=1),
        "seq",
        split_axis=0,
        concat_axis=0,
        tiled=True,
    )
    ffn_sum = added(*early_terms, *late_terms).reshape(slice_rows, width)
    layer_slice = (resid_one + ffn_sum).astype(LOW).reshape(parts, sub, width)
    line = head_count == 4
    layer_one = gather_step_one(layer_slice) if line else ()
    out_terms = (
        out_mine.reshape(shard_rows, head_count, head_width)
        .transpose(1, 0, 2)
        .reshape(head_count, out_mine.size // head_count // width, width)
    )
    returned, layer_one, out_terms = lax.optimization_barrier((returned, layer_one, out_terms))
    grads_back = returned[:, :block]
    mass_got = returned[:, block : block + mass_rows].astype(WIDE).reshape(local_heads, parts, 3, block)
    attn_mass = jnp.sum(mass_got, axis=2).reshape(local_heads, local_rows)
    qkv_grad = (
        grads_back.reshape(local_heads, parts, block, 3 * HD)
        .transpose(1, 2, 0, 3)
        .reshape(local_rows, 3 * head_width)
    )

    one_grad_part = dot(qkv_grad, qkv_weight, NT).astype(LOW).reshape(parts, head_count, sub, width)
    if line:
        forward = jnp.arange(4, dtype=jnp.int32)
        order = jnp.where(head_index < 2, forward, 3 - forward)
        terms = [
            jnp.concatenate(
                [
                    lax.dynamic_index_in_dim(one_grad_part, order[k], 1, False).reshape(
                        slice_rows, width
                    ),
                    lax.dynamic_index_in_dim(out_terms, order[k], 0, False),
                ],
                axis=0,
            )
            for k in range(4)
        ]
        got = sum_step_one(terms)
        layer_two = gather_step_two(layer_one)
        got, layer_two, terms, qkv_grad = lax.optimization_barrier((got, layer_two, terms, qkv_grad))
        got = sum_step_two(terms, got)
        layer_three = gather_step_three(layer_two)
        qkv_raw = dot(normed_one, qkv_grad, TN).astype(LOW)
        got, layer_three, terms, qkv_raw, ffn_shard = lax.optimization_barrier(
            (got, layer_three, terms, qkv_raw, ffn_shard)
        )
        got = sum_step_three(terms, got)
        got, layer_three = lax.optimization_barrier((got, layer_three))
        summed = sum_last(terms, got)
    else:
        layer_two = layer_three = ()
        qkv_raw = dot(normed_one, qkv_grad, TN).astype(LOW)
        summed = jnp.concatenate(
            [
                lax.psum_scatter(one_grad_part, "head", scatter_dimension=1, tiled=True).reshape(
                    slice_rows, width
                ),
                lax.psum_scatter(out_terms, "head", scatter_dimension=0, tiled=False),
            ],
            axis=0,
        ).astype(WIDE)
    qkv_mine = lax.psum_scatter(qkv_raw, "seq", scatter_dimension=0, tiled=True)
    normed_one_grad = summed[:slice_rows]
    out_own = summed[slice_rows:].astype(LOW).reshape(shard_rows, head_width)
    normed_one_grad = normed_one_grad.reshape(slice_rows, width)
    own_scale = own_slice(scale_one)
    unit_one = own_slice(tokens).astype(WIDE) * own_scale
    input_slice = norm_grad(
        normed_one_grad, unit_one, own_scale, gain_values[0], jnp.concatenate(resid_grads, axis=0)
    )
    input_slice = input_slice.astype(LOW).reshape(parts, sub, width)
    input_one = gather_step_one(input_slice) if line else ()
    input_two = gather_step_two(input_one) if line else ()
    own_gain = gain_master.astype(LOW).astype(WIDE)
    qkv_wide = qkv_mine.astype(WIDE)
    ffn_wide = ffn_shard.astype(WIDE)
    gain_two_term = (
        jnp.sum(
            ffn_shard_low[:, : 2 * hidden_width].astype(WIDE) * ffn_wide[:, : 2 * hidden_width], axis=1
        )
        / own_gain[1]
    )
    gain_one_term = jnp.sum(qkv_shard.astype(WIDE) * qkv_wide, axis=1) / own_gain[0]
    out_wide = out_own.astype(WIDE)
    squares = jnp.sum(ffn_wide * ffn_wide) + jnp.sum(out_wide * out_wide) + jnp.sum(qkv_wide * qkv_wide)
    row = jnp.arange(2 * seq_count + 8, dtype=jnp.int32)[:, None]
    small = jnp.where(
        row == seq_index,
        gain_one_term[None, :],
        jnp.where(
            row == seq_count + seq_index,
            gain_two_term[None, :],
            jnp.where(row == 2 * seq_count, squares / shard_rows, 0.0),
        ),
    )
    small = sum_everywhere(small)
    gain_all = small[: 2 * seq_count]
    gain_shard = jnp.stack(
        [
            lax.dynamic_index_in_dim(gain_all, seq_index, 0, False),
            lax.dynamic_index_in_dim(gain_all, seq_count + seq_index, 0, False),
        ]
    )
    grad_norm = jnp.sqrt(jnp.sum(small[2 * seq_count]) + jnp.sum(gain_all * gain_all))
    clip_factor = jnp.minimum(1.0, CLIP / (grad_norm + 1e-06))

    attn_grads = jnp.concatenate(
        [
            qkv_mine.reshape(shard_rows, local_heads, 3, HD)
            .transpose(0, 2, 1, 3)
            .reshape(shard_rows, 3 * head_width),
            out_own,
        ],
        axis=1,
    )
    input_two, clip_factor, attn_grads = lax.optimization_barrier((input_two, clip_factor, attn_grads))
    input_three = gather_step_three(input_two) if line else ()
    blank = jnp.zeros((parts, block, width), WIDE)
    layer_output = line_gather_wide(blank, layer_slice, (layer_one, layer_two, layer_three))
    layer_output = layer_output.reshape(local_rows, width)
    input_grad = line_gather_wide(blank, input_slice, (input_one, input_two, input_three))
    input_grad = input_grad.reshape(local_rows, width)
    gain_grad = gain_shard * clip_factor
    ffn_state = adam_arrays(clip_factor, ffn_shard, ffn_first, ffn_second, ffn_master)
    attn_state = adam_arrays(clip_factor, attn_grads, attn_first, attn_second, attn_master)
    gain_state = adam_update(gain_grad, gain_first, gain_second, gain_master, GAIN_RATE)
    return (
        layer_output,
        input_grad,
        attn_mass,
        grad_norm,
        attn_state[0],
        attn_state[1],
        attn_state[2],
        attn_state[3],
        attn_state[4],
        ffn_state[0],
        ffn_state[1],
        ffn_state[2],
        ffn_state[3],
        ffn_state[4],
        gain_grad,
        gain_state[0],
        gain_state[1],
        gain_state[2],
        gain_state[3],
    )


def solution(mesh):
    in_specs = (
        P("seq", None),
        P("seq", None),
        P(),
        P(None, "seq", "head"),
        P(None, "seq", "head"),
        P(None, "seq"),
        P(None, "seq", "head"),
        P(None, "seq", "head"),
        P(None, "seq", "head"),
        P(None, "seq", "head"),
        P(None, "seq"),
        P(None, "seq"),
    )
    out_specs = (
        P("seq", None),
        P("seq", None),
        P("head", "seq"),
        P(),
        P(None, "seq", "head"),
        P(None, "seq", "head"),
        P(None, "seq", "head"),
        P(None, "seq", "head"),
        P(None, "seq", "head"),
        P(None, "seq", "head"),
        P(None, "seq", "head"),
        P(None, "seq", "head"),
        P(None, "seq", "head"),
        P(None, "seq", "head"),
        P(None, "seq"),
        P(None, "seq"),
        P(None, "seq"),
        P(None, "seq"),
        P(None, "seq"),
    )
    return jax.shard_map(
        per_device, mesh=mesh, in_specs=in_specs, out_specs=out_specs, check_vma=False
    )
```

```python
import functools
import math

import jax
import jax.numpy as jnp
from jax import lax
from jax.experimental import pallas as pl
from jax.experimental.pallas import tpu as pltpu
from jax.sharding import PartitionSpec as P

HD = 128
STEP = 10


EPS = 1e-05
CLIP = 1.0
BETA1 = 0.5
BETA2 = 0.5
RATE = 0.03
GAIN_RATE = 0.3
DECAY = 0.1
ADAM_EPS = 1e-08

LOW = jnp.bfloat16
WIDE = jnp.float32
QUERY_FACTOR = -math.log2(math.e) / math.sqrt(HD)
FAR = 30000.0

NN = (((1,), (0,)), ((), ()))
NT = (((1,), (1,)), ((), ()))
TN = (((0,), (0,)), ((), ()))


def dot(left, right, dims=NN):
    return lax.dot_general(left, right, dims, preferred_element_type=WIDE)


def fill_key_columns(key_buf, sizes, cut):
    count, parts, block = sizes

    def step(at, _):
        place = at * block + lax.broadcasted_iota(jnp.int32, (block, HD), 0)
        lane = lax.broadcasted_iota(jnp.int32, (block, HD), 1)
        extra = jnp.where(lane < 3, 1.0, jnp.where((lane == 3) & (place < cut), FAR, 0.0))
        key_buf[pl.ds(pl.multiple_of(at * block, block), block), HD:] = extra.astype(LOW)
        return 0

    lax.fori_loop(0, count * parts, step, 0)


def query_columns(sizes, source, part, cut, floats):
    _, parts, block = sizes
    lane = lax.broadcasted_iota(jnp.int32, (block, HD), 1)
    place = (source * parts + part) * block + lax.broadcasted_iota(jnp.int32, (block, HD), 0)
    second = place >= cut

    def column(at):
        return jnp.where(second, floats[3 + at], floats[at])

    extra = jnp.where(
        lane == 0,
        column(0),
        jnp.where(
            lane == 1,
            column(1),
            jnp.where(lane == 2, column(2), jnp.where((lane == 3) & second, 1.0, 0.0)),
        ),
    )
    return extra.astype(LOW)


def in_causal_order(sizes, part, shape, key_dim, first_key=0):
    key_place = first_key + lax.broadcasted_iota(jnp.int32, shape, key_dim)
    query_place = part * sizes[2] + lax.broadcasted_iota(jnp.int32, shape, 1 - key_dim)
    return key_place <= query_place


def key_copies(sizes, part, key_values, key_buf, value_buf, sem):
    count, parts, block = sizes
    for other in range(parts):
        for at in range(count):
            row = pl.multiple_of((at * parts + (part ^ other)) * block, block)
            yield pltpu.make_async_copy(
                key_values[other].at[at, :, 0:HD], key_buf.at[pl.ds(row, block), 0:HD], sem.at[0]
            )
            yield pltpu.make_async_copy(
                key_values[other].at[at, :, HD:], value_buf.at[pl.ds(row, block), 0:HD], sem.at[0]
            )


def forward_kernel(sizes, ints, floats, q_ref, *rest):
    count, parts, block = sizes
    tile = block * parts
    key_values = rest[:parts]
    out_ref, mass_ref, key_buf, value_buf, query_buf, total, sem = rest[parts:]
    step = pl.program_id(0)
    cut, part = ints[0], ints[1]

    @pl.when(step == 0)
    def _():
        for copy in key_copies(sizes, part, key_values, key_buf, value_buf, sem):
            copy.start()
        fill_key_columns(key_buf, sizes, cut)
        value_buf[:, HD:] = jnp.ones((count * tile, HD), LOW)
        for copy in key_copies(sizes, part, key_values, key_buf, value_buf, sem):
            copy.wait()

    query_buf[:, :HD] = q_ref[...]
    query_buf[:, HD:] = query_columns(sizes, step, part, cut, floats)
    total[...] = jnp.zeros_like(total)
    first = jnp.where(step * tile >= cut, cut // tile, 0)

    def walk(at, masked):
        keys = pl.ds(pl.multiple_of(at * tile, tile), tile)
        exponent = dot(query_buf[...], key_buf[keys, :], NT)
        weight = pl.reciprocal(1.0 + jnp.exp2(exponent), approx=True)
        if masked:
            weight = jnp.where(in_causal_order(sizes, part, (block, tile), 1), weight, 0.0)
        total[...] += dot(weight.astype(LOW), value_buf[keys, :])

    def body(at, carry):
        walk(at, False)
        return carry

    lax.fori_loop(first, step, body, 0)
    walk(step, True)
    out_ref[...] = total[:, :HD].astype(LOW)
    mass_ref[...] = jnp.transpose(total[:, HD:])[0:1, :]


def attention_forward(sizes, ints, floats, queries, key_values):
    count, parts, block = sizes
    total_rows = count * parts * block
    pairs = total_rows * total_rows // (2 * parts)
    return pl.pallas_call(
        functools.partial(forward_kernel, sizes),
        out_shape=[
            jax.ShapeDtypeStruct((count, block, HD), LOW),
            jax.ShapeDtypeStruct((count, 1, block), WIDE),
        ],
        grid_spec=pltpu.PrefetchScalarGridSpec(
            num_scalar_prefetch=2,
            grid=(count,),
            in_specs=[pl.BlockSpec((None, block, HD), lambda i, *_: (i, 0, 0))]
            + [pl.BlockSpec(memory_space=pl.ANY)] * parts,
            out_specs=[
                pl.BlockSpec((None, block, HD), lambda i, *_: (i, 0, 0)),
                pl.BlockSpec((None, 1, block), lambda i, *_: (i, 0, 0)),
            ],
            scratch_shapes=[
                pltpu.VMEM((total_rows, 2 * HD), LOW),
                pltpu.VMEM((total_rows, 2 * HD), LOW),
                pltpu.VMEM((block, 2 * HD), LOW),
                pltpu.VMEM((block, 2 * HD), WIDE),
                pltpu.SemaphoreType.DMA((1,)),
            ],
        ),
        compiler_params=pltpu.CompilerParams(vmem_limit_bytes=48 * 2**20),
        cost_estimate=pl.CostEstimate(
            flops=pairs * 8 * HD, bytes_accessed=total_rows * HD * 8, transcendentals=2 * pairs
        ),
        name="attention_forward",
    )(ints, floats, queries, *key_values)


def backward_kernel(sizes, ints, floats, q_ref, grad_ref, *rest):
    count, parts, block = sizes
    tile = block * parts
    chunk = min(256, tile)
    key_values = rest[:parts]
    q_grad_ref, *kv_grad_refs = rest[parts : 2 * parts + 1]
    key_buf, value_buf, query_buf, q_turned, grad_turned, q_total, k_total, v_total, sem = rest[
        2 * parts + 1 :
    ]
    step = pl.program_id(0)
    cut, part = ints[0], ints[1]

    @pl.when(step == 0)
    def _():
        for copy in key_copies(sizes, part, key_values, key_buf, value_buf, sem):
            copy.start()
        fill_key_columns(key_buf, sizes, cut)
        k_total[...] = jnp.zeros_like(k_total)
        v_total[...] = jnp.zeros_like(v_total)
        for copy in key_copies(sizes, part, key_values, key_buf, value_buf, sem):
            copy.wait()

    query_buf[:, :HD] = q_ref[...]
    query_buf[:, HD:] = query_columns(sizes, step, part, cut, floats)
    q_turned[...] = jnp.transpose(q_ref[...])
    grad_turned[...] = jnp.transpose(grad_ref[...])
    q_total[...] = jnp.zeros_like(q_total)
    first = jnp.where(step * tile >= cut, cut // tile, 0)

    def walk(at, masked):
        base = pl.multiple_of(at * tile, tile)

        def products(place):
            keys = pl.ds(base + place, chunk)
            return (
                dot(query_buf[...], key_buf[keys, :], NT),
                dot(grad_ref[...], value_buf[keys, :], NT),
            )

        score_grads = []
        following = products(0)
        for place in range(0, tile, chunk):
            exponent, weight_grad = following
            if place + chunk < tile:
                following = products(place + chunk)
            weight = pl.reciprocal(1.0 + jnp.exp2(exponent), approx=True)
            if masked:
                weight = jnp.where(
                    in_causal_order(sizes, part, (block, chunk), 1, place), weight, 0.0
                )
            score_grad = (weight_grad * (weight - weight * weight)).astype(LOW)
            keys = pl.ds(base + place, chunk)
            v_total[:, keys] += dot(grad_turned[...], weight.astype(LOW))
            k_total[:, keys] += dot(q_turned[...], score_grad)
            score_grads.append(score_grad)
        q_total[...] += dot(
            jnp.concatenate(score_grads, axis=1), key_buf[pl.ds(base, tile), :HD]
        )

    def body(at, carry):
        walk(at, False)
        return carry

    lax.fori_loop(first, step, body, 0)
    walk(step, True)
    q_grad_ref[...] = (q_total[...] * (1.0 / math.sqrt(HD))).astype(LOW)

    @pl.when(step == count - 1)
    def _():
        for other in range(parts):
            for at in range(count):
                row = pl.multiple_of((at * parts + (part ^ other)) * block, block)
                rows = pl.ds(row, block)
                kv_grad_refs[other][at, :, :HD] = jnp.transpose(
                    k_total[:, rows] * (-math.log(2.0))
                ).astype(LOW)
                kv_grad_refs[other][at, :, HD:] = jnp.transpose(v_total[:, rows]).astype(LOW)


def attention_backward(sizes, ints, floats, queries, grads, key_values):
    count, parts, block = sizes
    total_rows = count * parts * block
    pairs = total_rows * total_rows // (2 * parts)
    return pl.pallas_call(
        functools.partial(backward_kernel, sizes),
        out_shape=[
            jax.ShapeDtypeStruct((count, block, HD), LOW),
        ]
        + [jax.ShapeDtypeStruct((count, block, 2 * HD), LOW)] * parts,
        grid_spec=pltpu.PrefetchScalarGridSpec(
            num_scalar_prefetch=2,
            grid=(count,),
            in_specs=[pl.BlockSpec((None, block, HD), lambda i, *_: (i, 0, 0))] * 2
            + [pl.BlockSpec(memory_space=pl.ANY)] * parts,
            out_specs=[
                pl.BlockSpec((None, block, HD), lambda i, *_: (i, 0, 0)),
            ]
            + [pl.BlockSpec((count, block, 2 * HD), lambda i, *_: (0, 0, 0))] * parts,
            scratch_shapes=[
                pltpu.VMEM((total_rows, 2 * HD), LOW),
                pltpu.VMEM((total_rows, HD), LOW),
                pltpu.VMEM((block, 2 * HD), LOW),
                pltpu.VMEM((HD, block), LOW),
                pltpu.VMEM((HD, block), LOW),
                pltpu.VMEM((block, HD), WIDE),
                pltpu.VMEM((HD, total_rows), WIDE),
                pltpu.VMEM((HD, total_rows), WIDE),
                pltpu.SemaphoreType.DMA((1,)),
            ],
        ),
        compiler_params=pltpu.CompilerParams(vmem_limit_bytes=60 * 2**20),
        cost_estimate=pl.CostEstimate(
            flops=pairs * 100 * HD, bytes_accessed=total_rows * HD * 16, transcendentals=2 * pairs
        ),
        name="attention_backward",
    )(ints, floats, queries, grads, *key_values)


def attention_scalars(seq_lengths, total_rows, part):
    cut = seq_lengths[0]
    length = jnp.log2(jnp.stack([cut, total_rows - cut]).astype(WIDE))
    high = lax.reduce_precision(length, 8, 7)
    middle = lax.reduce_precision(length - high, 8, 7)
    low = length - high - middle
    return (
        jnp.stack([cut, part]).astype(jnp.int32),
        jnp.stack([high, middle, low], axis=1).reshape(6),
    )


def projection_kernel(n_ref, w_ref, out_ref):
    heads, parts, block, columns = out_ref.shape
    lane = lax.broadcasted_iota(jnp.int32, (1, columns), 1)
    factor = jnp.where(lane < HD, QUERY_FACTOR, 1.0)
    for part in range(parts):
        rows = pl.ds(part * block, block)
        result = dot(n_ref[rows, :], w_ref[...])
        for head in range(heads):
            out_ref[head, part] = (
                result[:, head * columns : (head + 1) * columns] * factor
            ).astype(LOW)


def project(normed, weight, local_heads, parts):
    rows, width = normed.shape
    columns = 3 * HD
    heads = 2
    return pl.pallas_call(
        projection_kernel,
        out_shape=jax.ShapeDtypeStruct((local_heads, parts, rows // parts, columns), LOW),
        grid=(local_heads // heads,),
        in_specs=[
            pl.BlockSpec((rows, width), lambda j: (0, 0), pipeline_mode=pl.Buffered(1)),
            pl.BlockSpec((width, heads * columns), lambda j: (0, j)),
        ],
        out_specs=pl.BlockSpec((heads, parts, rows // parts, columns), lambda j: (j, 0, 0, 0)),
        compiler_params=pltpu.CompilerParams(vmem_limit_bytes=56 * 2**20),
        cost_estimate=pl.CostEstimate(
            flops=2 * rows * width * local_heads * columns,
            bytes_accessed=2 * (rows * width + (rows + width) * local_heads * columns),
            transcendentals=0,
        ),
        name="projection",
    )(normed, weight)


def ffn_kernel(pieces, table, *refs):
    given = refs[:pieces]
    c_ref, gate_w, up_w, down_w = refs[pieces : pieces + 4]
    normed_ref, hidden_ref, gate_ref, up_ref, two_ref, total, sem = refs[pieces + 4 :]
    step = pl.program_id(0)
    rows = normed_ref.shape[0]
    slots = table.shape[0]
    slot_rows = rows // slots

    @pl.when(step == 0)
    def _():
        def each(act):
            for slot in range(slots):
                for piece in range(pieces):

                    @pl.when(table[slot] == piece)
                    def _(slot=slot, piece=piece):
                        act(
                            pltpu.make_async_copy(
                                given[piece],
                                normed_ref.at[pl.ds(slot * slot_rows, slot_rows), :],
                                sem.at[slot],
                            )
                        )

        each(lambda copy: copy.start())
        total[...] = jnp.zeros_like(total)
        each(lambda copy: copy.wait())

    chunk = min(512, rows)
    for at in range(0, rows, chunk):
        here = pl.ds(at, chunk)
        gate = dot(normed_ref[here, :], gate_w[...])
        up = dot(normed_ref[here, :], up_w[...])
        grad = dot(c_ref[here, :], down_w[...])
        sig = 1.0 / (1.0 + jnp.exp(-gate))
        silu = gate * sig
        hidden_ref[here, :] = (silu * up).astype(LOW)
        gate_grad = (grad * up * (sig + silu * (1.0 - sig))).astype(LOW)
        up_grad = (grad * silu).astype(LOW)
        gate_ref[here, :] = gate_grad
        up_ref[here, :] = up_grad
        total[here, :] += dot(gate_grad, gate_w[...], NT) + dot(up_grad, up_w[...], NT)

    @pl.when(step == pl.num_programs(0) - 1)
    def _():
        two_ref[...] = total[...].astype(LOW)


def feed_forward(pieces, order, cotangent, half, weight, hidden_width):
    rows, width = cotangent.shape[0] // 2, cotangent.shape[1]
    step = min(512, hidden_width)
    steps = hidden_width // step
    out = jax.ShapeDtypeStruct((rows, hidden_width), LOW)
    full = jax.ShapeDtypeStruct((rows, width), LOW)
    once = pl.Buffered(1)
    whole = pl.BlockSpec((rows, width), lambda j, *_: (0, 0), pipeline_mode=once)
    return pl.pallas_call(
        functools.partial(ffn_kernel, len(pieces)),
        out_shape=[full, out, out, out, full],
        grid_spec=pltpu.PrefetchScalarGridSpec(
            num_scalar_prefetch=1,
            grid=(steps,),
            in_specs=[pl.BlockSpec(memory_space=pl.ANY)] * len(pieces)
            + [
                pl.BlockSpec((rows, width), lambda j, *_: (half, 0), pipeline_mode=once),
                pl.BlockSpec((width, step), lambda j, *_: (0, j)),
                pl.BlockSpec((width, step), lambda j, *_: (0, steps + j)),
                pl.BlockSpec((width, step), lambda j, *_: (0, 2 * steps + j)),
            ],
            out_specs=[whole]
            + [pl.BlockSpec((rows, step), lambda j, *_: (0, j))] * 3
            + [whole],
            scratch_shapes=[pltpu.VMEM((rows, width), WIDE), pltpu.SemaphoreType.DMA((order.shape[0],))],
        ),
        compiler_params=pltpu.CompilerParams(vmem_limit_bytes=60 * 2**20),
        cost_estimate=pl.CostEstimate(
            flops=10 * rows * width * hidden_width,
            bytes_accessed=6 * width * hidden_width,
            transcendentals=rows * hidden_width,
        ),
        name="feed_forward",
    )(order, *pieces, cotangent, weight, weight, weight)


def ffn_wgrad_kernel(steps, n_a, n_b, c_ref, gate_a, gate_b, up_a, up_b, hid_a, hid_b, out_ref, n_turned, c_turned):
    step = pl.program_id(0)
    half = n_a.shape[0]

    @pl.when(step == 0)
    def _():
        n_turned[:, :half] = jnp.transpose(n_a[...])
        n_turned[:, half:] = jnp.transpose(n_b[...])
        c_turned[...] = jnp.transpose(c_ref[...])

    def product(turned, first, second):
        out_ref[...] = (dot(turned[:, :half], first[...]) + dot(turned[:, half:], second[...])).astype(LOW)

    @pl.when(step < steps)
    def _():
        product(n_turned, gate_a, gate_b)

    @pl.when((step >= steps) & (step < 2 * steps))
    def _():
        product(n_turned, up_a, up_b)

    @pl.when(step >= 2 * steps)
    def _():
        product(c_turned, hid_a, hid_b)


def feed_forward_wgrad(normed, cotangent, gate_grad, up_grad, hidden):
    rows, width = cotangent.shape
    hidden_width = hidden[0].shape[1]
    step = min(512, hidden_width)
    steps = hidden_width // step
    once = pl.Buffered(1)

    def whole(count):
        return pl.BlockSpec((count, width), lambda j: (0, 0), pipeline_mode=once)

    def third(at):
        return pl.BlockSpec((rows // 2, step), lambda j: (0, jnp.clip(j - at * steps, 0, steps - 1)))

    return pl.pallas_call(
        functools.partial(ffn_wgrad_kernel, steps),
        out_shape=jax.ShapeDtypeStruct((width, 3 * hidden_width), LOW),
        grid=(3 * steps,),
        in_specs=[whole(rows // 2), whole(rows // 2), whole(rows)]
        + [third(0)] * 2
        + [third(1)] * 2
        + [third(2)] * 2,
        out_specs=pl.BlockSpec((width, step), lambda j: (0, j)),
        scratch_shapes=[pltpu.VMEM((width, rows), LOW), pltpu.VMEM((width, rows), LOW)],
        compiler_params=pltpu.CompilerParams(vmem_limit_bytes=60 * 2**20),
        cost_estimate=pl.CostEstimate(
            flops=rows * width,
            bytes_accessed=rows * width,
            transcendentals=0,
        ),
        name="feed_forward_wgrad",
    )(*normed, cotangent, *gate_grad, *up_grad, *hidden)


def adam_kernel(clip, grad, first, second, master, grad_out, first_out, second_out, new_out, low_out):
    gradient = grad[...].astype(WIDE) * clip[0]
    grad_out[...] = gradient
    first_new, second_new, master_new, low = adam_update(
        gradient, first[...], second[...], master[...], RATE
    )
    first_out[...] = first_new
    second_out[...] = second_new
    new_out[...] = master_new
    low_out[...] = low


def adam_arrays(clip_factor, grad, first, second, master):
    arrays, rows, columns = master.shape
    step = min(rows, max(16, 2**18 // columns))
    state = pl.BlockSpec((None, step, columns), lambda a, i, *_: (a, i, 0))
    wide = jax.ShapeDtypeStruct(master.shape, WIDE)
    return pl.pallas_call(
        adam_kernel,
        out_shape=[wide] * 4 + [jax.ShapeDtypeStruct(master.shape, LOW)],
        grid_spec=pltpu.PrefetchScalarGridSpec(
            num_scalar_prefetch=1,
            grid=(arrays, rows // step),
            in_specs=[pl.BlockSpec((step, columns), lambda a, i, *_: (i, a))] + [state] * 3,
            out_specs=[state] * 5,
        ),
        compiler_params=pltpu.CompilerParams(vmem_limit_bytes=32 * 2**20),
        cost_estimate=pl.CostEstimate(
            flops=20 * master.size, bytes_accessed=32 * master.size, transcendentals=2 * master.size
        ),
        name="adam",
    )(clip_factor.reshape(1), grad, first, second, master)


def slice_sum(terms):
    count = lax.axis_size("head")
    got = lax.all_to_all(terms, "head", split_axis=0, concat_axis=0, tiled=True)
    rows = terms.shape[0] // count
    return functools.reduce(
        lambda a, b: a + b, [got[j * rows : (j + 1) * rows].astype(WIDE) for j in range(count)]
    )


def added(*terms):
    return functools.reduce(lambda a, b: a + b, [t.astype(WIDE) for t in terms])


INWARD = [(0, 1), (3, 2)]
ACROSS = [(1, 2), (2, 1)]
OUTWARD = [(1, 0), (2, 3)]


def sum_step_one(terms):
    return (lax.ppermute(terms[3], "head", INWARD),)


def sum_step_two(terms, got):
    far = added(got[0], terms[3]).astype(LOW)
    return (lax.ppermute(terms[2], "head", INWARD), lax.ppermute(far, "head", ACROSS))


def sum_step_three(terms, got):
    middle = added(got[0], terms[2]).astype(LOW)
    far = added(got[1], terms[0]).astype(LOW)
    return (
        lax.ppermute(terms[1], "head", INWARD),
        lax.ppermute(middle, "head", ACROSS),
        lax.ppermute(far, "head", OUTWARD),
    )


def sum_last(terms, got):
    at = lax.axis_index("head")
    return jnp.where(
        (at == 0) | (at == 3), added(terms[0], got[2]), added(terms[1], got[0], got[1])
    )


def gather_step_one(piece):
    return (
        lax.ppermute(piece, "head", [(0, 1), (1, 2), (2, 3)]),
        lax.ppermute(piece, "head", [(3, 2), (2, 1), (1, 0)]),
    )


def gather_step_two(got):
    return (
        lax.ppermute(got[0], "head", [(1, 2), (2, 3)]),
        lax.ppermute(got[1], "head", [(2, 1), (1, 0)]),
    )


def gather_step_three(got):
    at = lax.axis_index("head")
    return (lax.ppermute(jnp.where(at == 2, got[0], got[1]), "head", [(2, 3), (1, 0)]),)


def gathered_pieces(piece, one, two, three):
    away = lax.axis_index("head") - jnp.arange(4, dtype=jnp.int32)
    order = jnp.where(
        away == 0, 0, jnp.where(jnp.abs(away) == 3, 5, jnp.where(away > 0, away, 2 - away))
    )
    return [piece, one[0], two[0], one[1], two[1], three[0]], order


def line_gather_pieces(piece):
    count = lax.axis_size("head")
    if count != 4:
        full = lax.all_gather(piece, "head", axis=0, tiled=True)
        return jnp.split(full, count, axis=0), jnp.arange(count, dtype=jnp.int32)
    one = gather_step_one(piece)
    two = gather_step_two(one)
    return gathered_pieces(piece, one, two, gather_step_three(two))


def line_gather_wide(full, piece, got):
    count = lax.axis_size("head")
    at = lax.axis_index("head")
    rows = piece.shape[1]
    if count != 4:
        every = lax.all_gather(piece, "head", axis=0, tiled=False).astype(WIDE)
        return every.transpose(1, 0, 2, 3).reshape(full.shape)
    one, two, three = got
    for where, part in (
        (at, piece),
        (at - 1, one[0]),
        (at + 1, one[1]),
        (at - 2, two[0]),
        (at + 2, two[1]),
        (jnp.where(at == 0, 3, jnp.where(at == 3, 0, at)), three[0]),
    ):
        there = (where >= 0) & (where < count) & (where != at)
        full = lax.dynamic_update_slice(
            full,
            jnp.where(there, part, piece).astype(WIDE),
            (0, jnp.where(there, where, at) * rows, 0),
        )
    return full


def group_exchange(blocks, parts):
    count = lax.axis_size("seq")
    return [blocks[0]] + [
        lax.ppermute(blocks[k], "seq", [(j, j ^ k) for j in range(count)]) for k in range(1, parts)
    ]


def direct_terms(terms):
    count = lax.axis_size("head")
    return terms[:1] + [
        lax.ppermute(terms[k], "head", [(j, j ^ k) for j in range(count)]) for k in range(1, count)
    ]


def direct_gather(piece):
    at = lax.axis_index("head")
    count = lax.axis_size("head")
    full = jnp.zeros((count,) + piece.shape, piece.dtype)
    for k in range(count):
        term = piece if k == 0 else lax.ppermute(piece, "head", [(j, j ^ k) for j in range(count)])
        full = lax.dynamic_update_index_in_dim(full, term, at ^ k, 0)
    return full


def sum_everywhere(values):
    for axis in ("seq", "head"):
        count = lax.axis_size(axis)
        bit = 1
        while bit < count:
            values = values + lax.ppermute(values, axis, [(j, j ^ bit) for j in range(count)])
            bit *= 2
    return values


def after(value, *others):
    return lax.optimization_barrier((value,) + others)[0]


def adam_update(gradient, first_moment, second, master, step_rate):
    first_new = BETA1 * first_moment + (1.0 - BETA1) * gradient
    second_new = BETA2 * second + (1.0 - BETA2) * gradient * gradient
    first_hat = first_new / (1.0 - BETA1**STEP)
    second_hat = second_new / (1.0 - BETA2**STEP)
    master_new = master - step_rate * (
        first_hat / (jnp.sqrt(second_hat) + ADAM_EPS) + DECAY * master
    )
    return (first_new, second_new, master_new, master_new.astype(LOW))


def per_device(
    tokens,
    cotangent,
    seq_lengths,
    attn_master,
    ffn_master,
    gain_master,
    attn_first,
    attn_second,
    ffn_first,
    ffn_second,
    gain_first,
    gain_second,
):
    seq_count = lax.axis_size("seq")
    head_count = lax.axis_size("head")
    seq_index = lax.axis_index("seq")
    head_index = lax.axis_index("head")
    local_rows, width = tokens.shape
    total_rows = local_rows * seq_count
    head_width = attn_master.shape[2]
    hidden_width = ffn_master.shape[2]
    shard_rows = attn_master.shape[1]
    local_heads = head_width // HD
    parts = seq_count // local_heads
    block = local_rows // parts
    part = seq_index % parts
    slice_rows = local_rows // head_count
    sub = slice_rows // parts
    sizes = (seq_count, parts, block)
    half_parts = parts // 2
    half_rows = local_rows // 2
    quarter_rows = slice_rows // 2

    def own_slice(array):
        columns = array.shape[1]
        return lax.dynamic_slice_in_dim(
            array.reshape(parts, block, columns), head_index * sub, sub, 1
        ).reshape(slice_rows, columns)

    def halves(array):
        return array[: array.shape[0] // 2], array[array.shape[0] // 2 :]

    def by_slices(array):
        rows, columns = array.shape
        return (
            array.reshape(rows // half_rows, half_parts, head_count, sub, columns)
            .transpose(0, 2, 1, 3, 4)
            .reshape(rows, columns)
        )

    qkv_shard = (
        attn_master[:3]
        .astype(LOW)
        .reshape(3, shard_rows, local_heads, HD)
        .transpose(1, 2, 0, 3)
        .reshape(shard_rows, 3 * head_width)
    )
    ffn_shard_low = jnp.concatenate([ffn_master[0], ffn_master[1], ffn_master[2]], axis=1).astype(LOW)
    gain_values = lax.all_gather(gain_master.astype(LOW), "seq", axis=1, tiled=True).astype(WIDE)
    qkv_weight = lax.all_gather(qkv_shard, "seq", axis=0, tiled=True)
    out_rows = (
        direct_gather(attn_master[3].astype(LOW)).transpose(1, 0, 2).reshape(shard_rows, width)
    )

    ints, floats = attention_scalars(seq_lengths, total_rows, part)

    gain_values, out_rows, ffn_shard_low = lax.optimization_barrier(
        (gain_values, out_rows, ffn_shard_low)
    )
    residual = tokens.astype(WIDE)
    scale_one = lax.rsqrt(jnp.mean(residual * residual, axis=-1, keepdims=True) + EPS)
    normed_one = (residual * scale_one * gain_values[0]).astype(LOW)
    sent = project(normed_one, qkv_weight, local_heads, parts).reshape(seq_count, block, 3 * HD)
    out_weight = lax.all_gather(after(out_rows, sent), "seq", axis=0, tiled=True)
    qkv = lax.all_to_all(sent, "seq", split_axis=0, concat_axis=0, tiled=True)
    head_queries = qkv[:, :, :HD]
    own_key_values = qkv[:, :, HD:]
    key_values = group_exchange([own_key_values] * parts, parts)
    ffn_weight = lax.all_gather(after(ffn_shard_low, key_values[-1]), "seq", axis=0, tiled=True)
    mixed, mass = attention_forward(sizes, ints, floats, head_queries, key_values)

    everywhere = ("seq", "head")
    slices_out = lax.all_to_all(
        mixed.reshape(seq_count * head_count, sub, HD), everywhere, split_axis=0, concat_axis=0, tiled=True
    )
    heads_out = (
        slices_out.reshape(local_heads, parts, head_count, sub, HD)
        .transpose(1, 3, 2, 0, 4)
        .reshape(slice_rows, width)
    )
    mass_high = lax.reduce_precision(mass, 8, 7)
    mass_middle = lax.reduce_precision(mass - mass_high, 8, 7)
    mass_parts = jnp.stack([mass_high, mass_middle, mass - mass_high - mass_middle], axis=1).astype(LOW)
    mass_rows = block // HD
    mass_sent = jnp.pad(
        mass_parts.reshape(seq_count, mass_rows, 3 * HD), ((0, 0), (0, 16 - mass_rows), (0, 0))
    )

    attn_sum = dot(heads_out, out_weight, NT)
    resid_one = own_slice(tokens).astype(WIDE) + attn_sum
    scale_two = lax.rsqrt(jnp.mean(resid_one * resid_one, axis=-1, keepdims=True) + EPS)
    unit_two = resid_one * scale_two
    normed_slice = (unit_two * gain_values[1]).astype(LOW)
    cot_slices = by_slices(cotangent)
    first_slice, second_slice = halves(normed_slice)

    first_pieces, order = line_gather_pieces(first_slice)
    second_pieces, order = line_gather_pieces(second_slice)
    first_pieces[-1], *second_pieces = lax.optimization_barrier((first_pieces[-1], *second_pieces))
    normed_a, hidden_a, gate_a, up_a, two_a = feed_forward(
        first_pieces, order, cot_slices, 0, ffn_weight, hidden_width
    )
    second_pieces[-1] = after(second_pieces[-1], two_a)
    normed_b, hidden_b, gate_b, up_b, two_b = feed_forward(
        second_pieces, order, cot_slices, 1, ffn_weight, hidden_width
    )
    two_sum_a = slice_sum(two_a)
    two_sum_b = slice_sum(two_b)
    two_sum_a, hidden_a, hidden_b = lax.optimization_barrier((two_sum_a, hidden_a, hidden_b))
    ffn_raw = feed_forward_wgrad(
        (normed_a, normed_b), cot_slices, (gate_a, gate_b), (up_a, up_b), (hidden_a, hidden_b)
    )
    ffn_shard = lax.psum_scatter(ffn_raw, "seq", scatter_dimension=0, tiled=True)
    down_weight = ffn_weight[:, 2 * hidden_width :]
    def norm_grad(grad, unit, scale, gain, passed):
        inner = grad * gain
        return passed + scale * (inner - unit * jnp.mean(inner * unit, axis=-1, keepdims=True))

    two_sum_b = after(two_sum_b, ffn_raw)
    cot_own = own_slice(cotangent).astype(WIDE)
    resid_grads = [
        norm_grad(*args, gain_values[1], passed)
        for args, passed in zip(
            zip((two_sum_a, two_sum_b), halves(unit_two), halves(scale_two)), halves(cot_own)
        )
    ]
    branch_low = jnp.concatenate([r.astype(LOW) for r in resid_grads], axis=0)
    heads_grad = dot(branch_low, out_weight).astype(LOW)

    grads_sent = (
        heads_grad.reshape(parts, sub, head_count, local_heads, HD)
        .transpose(3, 0, 2, 1, 4)
        .reshape(seq_count * head_count, sub, HD)
    )
    head_grads = lax.all_to_all(
        grads_sent, everywhere, split_axis=0, concat_axis=0, tiled=True
    ).reshape(seq_count, block, HD)
    out_raw = dot(branch_low, heads_out, TN).astype(LOW)
    out_mine = lax.psum_scatter(out_raw, "seq", scatter_dimension=0, tiled=True)
    hidden_a, hidden_b, grads_sent = lax.optimization_barrier((hidden_a, hidden_b, grads_sent))
    ffn_part = jnp.stack(
        [dot(hidden_a, down_weight, NT).astype(LOW), dot(hidden_b, down_weight, NT).astype(LOW)]
    )
    ffn_part = ffn_part.reshape(2, head_count, quarter_rows, width)
    ffn_terms = [
        lax.dynamic_index_in_dim(ffn_part, head_index ^ k, 1, False) for k in range(head_count)
    ]
    ffn_terms, head_grads = lax.optimization_barrier((ffn_terms, head_grads))
    ffn_terms = direct_terms(ffn_terms)
    early_terms, late_terms = ffn_terms[:3], ffn_terms[3:]
    q_grad, *kv_grads = attention_backward(sizes, ints, floats, head_queries, head_grads, key_values)
    kv_grads, early_terms = lax.optimization_barrier((kv_grads, early_terms))
    kv_terms = group_exchange(kv_grads, parts)
    kv_sum = functools.reduce(lambda a, b: a + b, [t.astype(WIDE) for t in kv_terms]).astype(LOW)
    returned = lax.all_to_all(
        jnp.concatenate([jnp.concatenate([q_grad, kv_sum], axis=2), mass_sent], axis=1),
        "seq",
        split_axis=0,
        concat_axis=0,
        tiled=True,
    )
    ffn_sum = added(*early_terms, *late_terms).reshape(slice_rows, width)
    layer_slice = (resid_one + ffn_sum).astype(LOW).reshape(parts, sub, width)
    line = head_count == 4
    layer_one = gather_step_one(layer_slice) if line else ()
    out_terms = (
        out_mine.reshape(shard_rows, head_count, head_width)
        .transpose(1, 0, 2)
        .reshape(head_count, out_mine.size // head_count // width, width)
    )
    returned, layer_one, out_terms = lax.optimization_barrier((returned, layer_one, out_terms))
    grads_back = returned[:, :block]
    mass_got = returned[:, block : block + mass_rows].astype(WIDE).reshape(local_heads, parts, 3, block)
    attn_mass = jnp.sum(mass_got, axis=2).reshape(local_heads, local_rows)
    qkv_grad = (
        grads_back.reshape(local_heads, parts, block, 3 * HD)
        .transpose(1, 2, 0, 3)
        .reshape(local_rows, 3 * head_width)
    )

    one_grad_part = dot(qkv_grad, qkv_weight, NT).astype(LOW).reshape(parts, head_count, sub, width)
    if line:
        forward = jnp.arange(4, dtype=jnp.int32)
        order = jnp.where(head_index < 2, forward, 3 - forward)
        terms = [
            jnp.concatenate(
                [
                    lax.dynamic_index_in_dim(one_grad_part, order[k], 1, False).reshape(
                        slice_rows, width
                    ),
                    lax.dynamic_index_in_dim(out_terms, order[k], 0, False),
                ],
                axis=0,
            )
            for k in range(4)
        ]
        got = sum_step_one(terms)
        layer_two = gather_step_two(layer_one)
        got, layer_two, terms, qkv_grad = lax.optimization_barrier((got, layer_two, terms, qkv_grad))
        got = sum_step_two(terms, got)
        layer_three = gather_step_three(layer_two)
        qkv_raw = dot(normed_one, qkv_grad, TN).astype(LOW)
        got, layer_three, terms, qkv_raw, ffn_shard = lax.optimization_barrier(
            (got, layer_three, terms, qkv_raw, ffn_shard)
        )
        got = sum_step_three(terms, got)
        got, layer_three = lax.optimization_barrier((got, layer_three))
        summed = sum_last(terms, got)
    else:
        layer_two = layer_three = ()
        qkv_raw = dot(normed_one, qkv_grad, TN).astype(LOW)
        summed = jnp.concatenate(
            [
                lax.psum_scatter(one_grad_part, "head", scatter_dimension=1, tiled=True).reshape(
                    slice_rows, width
                ),
                lax.psum_scatter(out_terms, "head", scatter_dimension=0, tiled=False),
            ],
            axis=0,
        ).astype(WIDE)
    qkv_mine = lax.psum_scatter(qkv_raw, "seq", scatter_dimension=0, tiled=True)
    normed_one_grad = summed[:slice_rows]
    out_own = summed[slice_rows:].astype(LOW).reshape(shard_rows, head_width)
    normed_one_grad = normed_one_grad.reshape(slice_rows, width)
    own_scale = own_slice(scale_one)
    unit_one = own_slice(tokens).astype(WIDE) * own_scale
    input_slice = norm_grad(
        normed_one_grad, unit_one, own_scale, gain_values[0], jnp.concatenate(resid_grads, axis=0)
    )
    input_slice = input_slice.astype(LOW).reshape(parts, sub, width)
    input_one = gather_step_one(input_slice) if line else ()
    input_two = gather_step_two(input_one) if line else ()
    own_gain = gain_master.astype(LOW).astype(WIDE)
    qkv_wide = qkv_mine.astype(WIDE)
    ffn_wide = ffn_shard.astype(WIDE)
    gain_two_term = (
        jnp.sum(
            ffn_shard_low[:, : 2 * hidden_width].astype(WIDE) * ffn_wide[:, : 2 * hidden_width], axis=1
        )
        / own_gain[1]
    )
    gain_one_term = jnp.sum(qkv_shard.astype(WIDE) * qkv_wide, axis=1) / own_gain[0]
    out_wide = out_own.astype(WIDE)
    squares = jnp.sum(ffn_wide * ffn_wide) + jnp.sum(out_wide * out_wide) + jnp.sum(qkv_wide * qkv_wide)
    row = jnp.arange(2 * seq_count + 8, dtype=jnp.int32)[:, None]
    small = jnp.where(
        row == seq_index,
        gain_one_term[None, :],
        jnp.where(
            row == seq_count + seq_index,
            gain_two_term[None, :],
            jnp.where(row == 2 * seq_count, squares / shard_rows, 0.0),
        ),
    )
    small = sum_everywhere(small)
    gain_all = small[: 2 * seq_count]
    gain_shard = jnp.stack(
        [
            lax.dynamic_index_in_dim(gain_all, seq_index, 0, False),
            lax.dynamic_index_in_dim(gain_all, seq_count + seq_index, 0, False),
        ]
    )
    grad_norm = jnp.sqrt(jnp.sum(small[2 * seq_count]) + jnp.sum(gain_all * gain_all))
    clip_factor = jnp.minimum(1.0, CLIP / (grad_norm + 1e-06))

    attn_grads = jnp.concatenate(
        [
            qkv_mine.reshape(shard_rows, local_heads, 3, HD)
            .transpose(0, 2, 1, 3)
            .reshape(shard_rows, 3 * head_width),
            out_own,
        ],
        axis=1,
    )
    input_two, clip_factor, attn_grads = lax.optimization_barrier((input_two, clip_factor, attn_grads))
    input_three = gather_step_three(input_two) if line else ()
    blank = jnp.zeros((parts, block, width), WIDE)
    layer_output = line_gather_wide(blank, layer_slice, (layer_one, layer_two, layer_three))
    layer_output = layer_output.reshape(local_rows, width)
    input_grad = line_gather_wide(blank, input_slice, (input_one, input_two, input_three))
    input_grad = input_grad.reshape(local_rows, width)
    gain_grad = gain_shard * clip_factor
    ffn_state = adam_arrays(clip_factor, ffn_shard, ffn_first, ffn_second, ffn_master)
    attn_state = adam_arrays(clip_factor, attn_grads, attn_first, attn_second, attn_master)
    gain_state = adam_update(gain_grad, gain_first, gain_second, gain_master, GAIN_RATE)
    return (
        layer_output,
        input_grad,
        attn_mass,
        grad_norm,
        attn_state[0],
        attn_state[1],
        attn_state[2],
        attn_state[3],
        attn_state[4],
        ffn_state[0],
        ffn_state[1],
        ffn_state[2],
        ffn_state[3],
        ffn_state[4],
        gain_grad,
        gain_state[0],
        gain_state[1],
        gain_state[2],
        gain_state[3],
    )


def solution(mesh):
    in_specs = (
        P("seq", None),
        P("seq", None),
        P(),
        P(None, "seq", "head"),
        P(None, "seq", "head"),
        P(None, "seq"),
        P(None, "seq", "head"),
        P(None, "seq", "head"),
        P(None, "seq", "head"),
        P(None, "seq", "head"),
        P(None, "seq"),
        P(None, "seq"),
    )
    out_specs = (
        P("seq", None),
        P("seq", None),
        P("head", "seq"),
        P(),
        P(None, "seq", "head"),
        P(None, "seq", "head"),
        P(None, "seq", "head"),
        P(None, "seq", "head"),
        P(None, "seq", "head"),
        P(None, "seq", "head"),
        P(None, "seq", "head"),
        P(None, "seq", "head"),
        P(None, "seq", "head"),
        P(None, "seq", "head"),
        P(None, "seq"),
        P(None, "seq"),
        P(None, "seq"),
        P(None, "seq"),
        P(None, "seq"),
    )
    return jax.shard_map(
        per_device, mesh=mesh, in_specs=in_specs, out_specs=out_specs, check_vma=False
    )
```
